128 devices in a mesh: section: 2 (over y_lo), dp: 64 (over x, y_hi, z, core).
Axes of the slice: x: 4, y: 4 (y_hi: 2, y_lo: 2; y = y_hi * 2 + y_lo), z: 4, core: 2. Of those that a mesh axis runs over, the one named last changes fastest.
Arguments:
- stream: bfloat16 [2, 4, 64, 128, 640], P('section', None, 'dp'), may hold values from -6 to 6
- cotangent: bfloat16 [2, 4, 64, 128, 640], P('section', None, 'dp'), may hold values from -6 to 6
- lengths: int32 [2, 4, 64], P(None, None, 'dp'), may hold values from 32 to 128, as said below
- pieces: int32 [4, 64], P(None, 'dp'), may hold values from 0 to 3
- configs: int32 [4, 4], replicated, may hold values from 1 to 3072, as said below
- gains: bfloat16 [2, 3, 640], P('section'), may hold values from 0.5 to 1.5
- attn_qkv: bfloat16 [2, 640, 1920], P('section'), may hold values from -0.3125 to 0.3125
- attn_out: bfloat16 [2, 640, 640], P('section'), may hold values from -0.625 to 0.625
- ffn_up: bfloat16 [2, 640, 3072], P('section'), may hold values from -0.25 to 0.25
- ffn_down: bfloat16 [2, 3072, 640], P('section'), may hold values from -0.109375 to 0.109375
- cross_proj: bfloat16 [2, 640, 1280], P('section')
Outputs:
- layer_out: bfloat16 [2, 4, 64, 128, 640], P('section', None, 'dp')
- stream_grad: bfloat16 [2, 4, 64, 128, 640], P('section', None, 'dp')
- gain_grad: float32 [2, 3, 640], P('section', None, 'dp')
- qkv_grad: float32 [2, 640, 1920], P('section', 'dp')
- out_grad: float32 [2, 640, 640], P('section', 'dp')
- up_grad: float32 [2, 640, 3072], P('section', 'dp')
- down_grad: float32 [2, 3072, 640], P('section', 'dp')
- cross_grad: float32 [2, 640, 1280], P('section', 'dp')
The draws below stay inside these ranges and needn't reach their ends.
Inputs may be any that keep to these rules, and one draw needn't show every extreme that they name: `configs`: column 0 is 640 or 512, column 8 or 4, column 2 one, two or three times 1024, column 3 1 or 2. Some piece has 640, 8, 3072 and 2. `lengths`: in every micro-batch, some sentence of each side has all 128 positions live.
All inputs are finite; a program needn't handle non-finite values.
Results may differ from the reference program's by a relative error of at most 0.024.
Values may be sent and summed in bfloat16 or wider, within the bound.
A program may use at most 448 MiB of HBM per device.

```python
import jax
import jax.numpy as jnp
from jax import lax

D = 640
HEADS = 8
FF = 3072
HEAD_DIM = 80
FF_BLOCK = 1024
SEQ_LEN = 128
MB = 4
PIECES = 4
B_ALL = 64


def draw_lengths(key, part):
    key = jax.random.fold_in(key, 7)
    first_key, second_key = jax.random.split(key)
    base = jax.random.randint(first_key, (2, MB, B_ALL), SEQ_LEN // 4, SEQ_LEN + 1)
    picked = jax.random.randint(second_key, (2, MB, 1), 0, B_ALL)
    full_row = jnp.arange(B_ALL, dtype=jnp.int32)[None, None, :] == picked
    return jnp.where(full_row, SEQ_LEN, base).astype(jnp.int32)


def draw_configs(key, part):
    key = jax.random.fold_in(key, 5)
    keys_list = jax.random.split(key, 5)
    wide_bit = jax.random.randint(keys_list[0], (PIECES,), 0, 2)
    heads_bit = jax.random.randint(keys_list[1], (PIECES,), 0, 2)
    blocks = jax.random.randint(keys_list[2], (PIECES,), 1, 4)
    layers = jax.random.randint(keys_list[3], (PIECES,), 1, 3)
    full_piece = jax.random.randint(keys_list[4], (), 0, PIECES)
    is_full = jnp.arange(PIECES, dtype=jnp.int32) == full_piece
    width_col = jnp.where(is_full | (wide_bit == 1), D, D * 4 // 5)
    heads_col = jnp.where(is_full | (heads_bit == 1), HEADS, HEADS // 2)
    ffn_col = jnp.where(is_full, 3, blocks) * FF_BLOCK
    cross_col = jnp.where(is_full, 2, layers)
    return jnp.stack([width_col, heads_col, ffn_col, cross_col], axis=1).astype(jnp.int32)


def draw_cross_proj(key, part):
    key = jax.random.fold_in(key, 11)
    base = jax.random.normal(key, (2, D, 2 * D), jnp.float32)
    column = jnp.arange(2 * D, dtype=jnp.int32)
    slot = jnp.arange(2, dtype=jnp.int32)
    output_part = (slot[:, None, None] == 1) & (column[None, None, :] >= D)
    factor = jnp.where(output_part, (D // 8) ** (-0.5), (D // 2) ** (-0.5))
    return (base * factor).astype(jnp.bfloat16)


def plant(drawn, own_key, low, top_value):
    place = [jax.random.randint(jax.random.fold_in(own_key, axis), (), 0, length) for axis, length in enumerate(drawn.shape)]
    main_axis = drawn.shape.index(max(drawn.shape))
    beside = place[:main_axis] + [(place[main_axis] + 1) % drawn.shape[main_axis]] + place[main_axis + 1:]
    return drawn.at[tuple(place)].set(low).at[tuple(beside)].set(top_value)


def block_levels(key, dims, cuts, low, high):
    loudness, own = 1.0, jax.random.fold_in(key, 6)
    for dim, parts in cuts:
        steps = jnp.exp(jax.random.uniform(jax.random.fold_in(own, dim), (parts,), jnp.float32, low / len(cuts), high / len(cuts)))
        loudness = loudness * jnp.repeat(steps, dims[dim] // parts).reshape([-1 if axis == dim else 1 for axis in range(len(dims))])
    return loudness


def gaussian(own_key, shape, width, limit, shards=(), kind=jnp.bfloat16):
    loudness = block_levels(own_key, shape, shards, -0.22, 0.18) if shards else 1.0
    drawn = jax.random.normal(own_key, shape, jnp.float32) * width * loudness
    return jnp.minimum(jnp.maximum(drawn, -limit), limit).astype(kind)


def setup_inputs(seed: int = 0) -> dict:
    splits = jax.random.split(jax.random.key(seed), 12)
    return {
        "stream": gaussian(splits[0], (2, MB, B_ALL, SEQ_LEN, D), 1.0, 6.0, ((0, 2), (2, 64))),
        "cotangent": gaussian(splits[1], (2, MB, B_ALL, SEQ_LEN, D), 1.0, 6.0, ((0, 2), (2, 64))),
        "lengths": draw_lengths(jax.random.fold_in(splits[11], 71), 0),
        "pieces": plant(jax.random.randint(splits[3], (MB, B_ALL), 0, PIECES), jax.random.fold_in(splits[3], 1), 0, PIECES - 1).astype(jnp.int32),
        "configs": draw_configs(jax.random.fold_in(splits[11], 71), 0),
        "gains": jnp.clip(1.0 + 0.1 * jax.random.normal(splits[5], (2, 3, D), jnp.float32), 0.5, 1.5).astype(jnp.bfloat16),
        "attn_qkv": gaussian(splits[6], (2, D, 3 * D), (D // 2) ** -0.5, 0.3125, ((0, 2),)),
        "attn_out": gaussian(splits[7], (2, D, D), (D // 8) ** -0.5, 0.625, ((0, 2),)),
        "ffn_up": gaussian(splits[8], (2, D, FF), D ** -0.5, 0.25, ((0, 2),)),
        "ffn_down": gaussian(splits[9], (2, FF, D), FF ** -0.5, 0.109375, ((0, 2),)),
        "cross_proj": draw_cross_proj(jax.random.fold_in(splits[11], 71), 0),
    }


EPSILON = 1e-05
NEGATIVE = -1e+30

@jax.custom_vjp
def low(v):
    return lax.optimization_barrier(v.astype(jnp.bfloat16)).astype(jnp.float32)

@jax.custom_vjp
def low_back(v):
    return v

def low_keep(v):
    return (low(v), None)

def low_pass(kept, grad):
    return (grad,)

def back_keep(v):
    return (v, None)

def back_low(kept, grad):
    return (low(grad),)
low.defvjp(low_keep, low_pass)
low_back.defvjp(back_keep, back_low)

def dense(barrier_operand, weight_matrix):
    return jnp.matmul(barrier_operand, weight_matrix, precision=lax.Precision.HIGHEST)

def layer_norm(values, norm_gain, feat_mask, live_width):
    average = lax.optimization_barrier(jnp.sum(values * feat_mask, -1, keepdims=True)) / live_width
    centred = (values - average) * feat_mask
    spread = lax.optimization_barrier(jnp.sum(centred * centred, -1, keepdims=True)) / live_width
    return centred * lax.rsqrt(spread + EPSILON) * norm_gain

def attend(queries, key_rows, value_rows, permitted_mask):
    seq_count, query_len = (queries.shape[0], queries.shape[1])
    key_len = key_rows.shape[1]
    query_heads = queries.reshape(seq_count, query_len, HEADS, HEAD_DIM)
    key_heads = key_rows.reshape(seq_count, key_len, HEADS, HEAD_DIM)
    value_head_count = value_rows.reshape(seq_count, key_len, HEADS, HEAD_DIM)
    scores = jnp.einsum('sqhd,skhd->shqk', query_heads, key_heads, precision=lax.Precision.HIGHEST) * HEAD_DIM ** (-0.5)
    scores = low_back(scores)
    scores = jnp.where(permitted_mask, scores, NEGATIVE)
    weights_soft = low(jax.nn.softmax(scores, axis=-1))
    blended = jnp.einsum('shqk,skhd->sqhd', weights_soft, value_head_count, precision=lax.Precision.HIGHEST)
    return blended.reshape(seq_count, query_len, HEADS * HEAD_DIM)

def self_block(inputs, norm_gain, w_qkv, w_out, permitted_mask, meta, rows):
    live_width, feat_mask, head_mask = (meta[0], meta[1], meta[2])
    barrier_operand = low(layer_norm(inputs, norm_gain, feat_mask, live_width))
    triple = low(low_back(dense(barrier_operand, w_qkv)))
    queries, key_rows, value_rows = jnp.split(triple, 3, axis=-1)
    heads_out = low(low_back(attend(queries, key_rows, value_rows, permitted_mask) * head_mask))
    return inputs + low_back(dense(heads_out, w_out) * feat_mask * rows)

def ffn_block(inputs, norm_gain, w_up, w_down, meta, rows):
    live_width, feat_mask, unit_mask = (meta[0], meta[1], meta[3])
    barrier_operand = low(layer_norm(inputs, norm_gain, feat_mask, live_width))
    hidden = low_back(dense(barrier_operand, w_up))
    activated = low(jax.nn.gelu(hidden, approximate=False) * unit_mask)
    return inputs + low_back(dense(activated, w_down) * feat_mask * rows)

def cross_block(inputs, norm_gain, w_cross, key_value, permitted_mask, meta, rows):
    live_width, feat_mask, head_mask = (meta[0], meta[1], meta[2])
    model_width = inputs.shape[-1]
    barrier_operand = low(layer_norm(inputs, norm_gain, feat_mask, live_width))
    queries = low(low_back(dense(barrier_operand, w_cross[:, :model_width])))
    key_rows = jnp.concatenate([key_value[0, :, :, :model_width], key_value[1, :, :, :model_width]], axis=1)
    value_rows = jnp.concatenate([key_value[0, :, :, model_width:], key_value[1, :, :, model_width:]], axis=1)
    heads_out = low(low_back(attend(queries, key_rows, value_rows, permitted_mask) * head_mask))
    return inputs + low_back(dense(heads_out, w_cross[:, model_width:]) * feat_mask * rows)

def encoder(inputs, meta, norm_gain, w_qkv, w_out, w_up, w_down, w_cross):
    live_width, feat_mask = (meta[0], meta[1])
    after_attn = self_block(inputs, norm_gain[0], w_qkv, w_out, meta[6], meta, meta[4])
    result = ffn_block(after_attn, norm_gain[1], w_up, w_down, meta, meta[4])
    encoded = jnp.stack([layer_norm(result, norm_gain[2], feat_mask, live_width), layer_norm(inputs, norm_gain[2], feat_mask, live_width)])
    key_value = low(low_back(dense(low(encoded), w_cross)))
    return (result, key_value)

def decoder(inputs, key_value, meta, norm_gain, w_qkv, w_out, w_up, w_down, w_cross):
    after_self = self_block(inputs, norm_gain[0], w_qkv, w_out, meta[7], meta, meta[5])
    after_cross = cross_block(after_self, norm_gain[1], w_cross, key_value, meta[8], meta, meta[5])
    return ffn_block(after_cross, norm_gain[2], w_up, w_down, meta, meta[5])

def reference(stream, cotangent, lengths, pieces, configs, gains, attn_qkv, attn_out, ffn_up, ffn_down, cross_proj):
    chosen = configs[pieces]
    feature = jnp.arange(D, dtype=jnp.int32)
    places = jnp.arange(SEQ_LEN, dtype=jnp.int32)
    key_slots = jnp.arange(2 * SEQ_LEN, dtype=jnp.int32)
    live_width = chosen[:, :, 0].astype(jnp.float32)[:, :, None, None]
    feat_mask = (feature < chosen[:, :, 0, None, None]).astype(jnp.float32)
    head_mask = (feature // HEAD_DIM < chosen[:, :, 1, None, None]).astype(jnp.float32)
    unit_mask = (jnp.arange(FF, dtype=jnp.int32) < chosen[:, :, 2, None, None]).astype(jnp.float32)
    source = lengths[0]
    target = lengths[1]
    src_rows = (places < source[:, :, None]).astype(jnp.float32)[..., None]
    tgt_rows = (places < target[:, :, None]).astype(jnp.float32)[..., None]
    enc_allowed = places < source[:, :, None, None, None]
    causal = places[None, :] <= places[:, None]
    dec_allowed = causal & (places < target[:, :, None, None, None])
    cross_allowed = (key_slots % SEQ_LEN < source[:, :, None, None, None]) & (key_slots // SEQ_LEN < chosen[:, :, 3, None, None, None])
    metas = (live_width, feat_mask, head_mask, unit_mask, src_rows, tgt_rows, enc_allowed, dec_allowed, cross_allowed)

    def forward(enc_in, dec_in, norm_gain, w_qkv, w_out, w_up, w_down, w_cross):

        def one_micro(items):
            enc_rows, dec_rows, meta = items
            enc_result, key_value = encoder(enc_rows, meta, norm_gain[0], w_qkv[0], w_out[0], w_up[0], w_down[0], w_cross[0])
            dec_result = decoder(dec_rows, key_value, meta, norm_gain[1], w_qkv[1], w_out[1], w_up[1], w_down[1], w_cross[1])
            return (enc_result, dec_result)
        return lax.map(jax.checkpoint(one_micro), (enc_in, dec_in, metas))
    primal, pullback = jax.vjp(forward, stream[0].astype(jnp.float32), stream[1].astype(jnp.float32), gains.astype(jnp.float32), attn_qkv.astype(jnp.float32), attn_out.astype(jnp.float32), ffn_up.astype(jnp.float32), ffn_down.astype(jnp.float32), cross_proj.astype(jnp.float32))
    grads = pullback((cotangent[0].astype(jnp.float32), cotangent[1].astype(jnp.float32)))
    d_enc, d_dec, d_gain, d_qkv, d_out, d_up, d_down, d_cross = grads
    tokens_all = pieces.shape[0] * pieces.shape[1] * SEQ_LEN
    heads_full = (chosen[:, :, 1] == HEADS).astype(jnp.int32)
    wide_two = (chosen[:, :, 2] > FF_BLOCK).astype(jnp.int32)
    wide_three = (chosen[:, :, 2] > 2 * FF_BLOCK).astype(jnp.int32)
    qkv_cols = jnp.arange(3 * D, dtype=jnp.int32) % D // HEAD_DIM >= HEADS // 2
    out_rows = jnp.arange(D, dtype=jnp.int32) // HEAD_DIM >= HEADS // 2
    ffn_block_index = jnp.arange(FF, dtype=jnp.int32) // FF_BLOCK
    qkv_list, out_list, up_list, down_list = ([], [], [], [])
    for side in range(2):
        own = lengths[side]
        counts = jnp.stack([jnp.sum(own), jnp.sum(own * heads_full), jnp.sum(own * wide_two), jnp.sum(own * wide_three)])
        rates = (tokens_all / (counts + tokens_all // 8)).astype(jnp.float32)
        ffn_rate = jnp.where(ffn_block_index == 0, rates[0], jnp.where(ffn_block_index == 1, rates[2], rates[3]))
        qkv_list.append(d_qkv[side] * jnp.where(qkv_cols, rates[1], rates[0])[None, :])
        out_list.append(d_out[side] * jnp.where(out_rows, rates[1], rates[0])[:, None])
        up_list.append(d_up[side] * ffn_rate[None, :])
        down_list.append(d_down[side] * ffn_rate[:, None])
    layer_out = jnp.stack([primal[0], primal[1]]).astype(jnp.bfloat16)
    stream_grad = jnp.stack([d_enc, d_dec]).astype(jnp.bfloat16)
    return (layer_out, stream_grad, d_gain, jnp.stack(qkv_list), jnp.stack(out_list), jnp.stack(up_list), jnp.stack(down_list), d_cross)
```

```python
import jax
import jax.numpy as jnp
from jax import lax
from jax.experimental import pallas as pl
from jax.experimental.pallas import tpu as pltpu
from jax.sharding import PartitionSpec as P

HEADS = 8
HEAD_DIM = 80
FF_BLOCK = 1024


EPSILON = 1e-05
NEGATIVE = -1e30


MESH = pl.DeviceIdType.MESH
NX_AXIS, NY_AXIS, NZ_AXIS, CORES = 4, 2, 4, 2


def place():
    me = lax.axis_index("dp")
    core = me % CORES
    z = me // CORES % NZ_AXIS
    y = me // (CORES * NZ_AXIS) % NY_AXIS
    x = me // (CORES * NZ_AXIS * NY_AXIS)
    return x, y, z, core


def device_at(x, y, z, core):
    return {"dp": ((x * NY_AXIS + y) * NZ_AXIS + z) * CORES + core}


def relative_order(first):
    x, y, z, core = place()
    spot = jnp.arange(640, dtype=jnp.int32)
    rc, ra, rb, ry, t = spot // 320, spot // 80 % 4, spot // 20 % 4, spot // 10 % 2, spot % 10
    rx, rz = (ra, rb) if first == "x" else (rb, ra)
    cx, cy, cz, cc = (x + rx) % 4, (y + ry) % 2, (z + rz) % 4, (core + rc) % 2
    return (((cx * 2 + cy) * 4 + cz) * 2 + cc) * 10 + t


class Sems:
    def __init__(self, send, recv):
        self.send, self.recv, self.at = send, recv, 0

    def copy(self, src, dst, device):
        k = self.at
        self.at += 1
        return pltpu.make_async_remote_copy(
            src_ref=src, dst_ref=dst, send_sem=self.send.at[k], recv_sem=self.recv.at[k],
            device_id=device, device_id_type=MESH)


def add_rows(dst, src, rows, step=16):
    def body(k, _):
        at = pl.ds(pl.multiple_of(k * step, step), step)
        dst[at] = dst[at] + src[at]
        return 0
    lax.fori_loop(0, rows // step, body, 0)


def ring_start(sems, s, buf_a, buf_b, cut, rows, plus, minus):
    a_p = sems.copy(s.at[2, pl.ds(0, cut)], buf_a.at[0, pl.ds(0, cut)], plus)
    a_m = sems.copy(s.at[2, pl.ds(cut, rows - cut)], buf_a.at[1, pl.ds(cut, rows - cut)], minus)
    a_p.start()
    a_m.start()
    b_p = sems.copy(s.at[1, pl.ds(cut, rows - cut)], buf_b.at[0, pl.ds(cut, rows - cut)], plus)
    b_m = sems.copy(s.at[3, pl.ds(0, cut)], buf_b.at[1, pl.ds(0, cut)], minus)
    b_p.start()
    b_m.start()
    return a_p, a_m, b_p, b_m


def ring_middle(sems, copies, s, buf_a, buf_b, cut, rows, plus, minus):
    a_p, a_m, b_p, b_m = copies
    a_p.wait_recv()
    add_rows(s.at[1, pl.ds(0, cut)], buf_a.at[0, pl.ds(0, cut)], cut)
    c_p = sems.copy(s.at[1, pl.ds(0, cut)], buf_b.at[0, pl.ds(0, cut)], plus)
    c_p.start()
    a_m.wait_recv()
    add_rows(s.at[3, pl.ds(cut, rows - cut)], buf_a.at[1, pl.ds(cut, rows - cut)], rows - cut)
    c_m = sems.copy(s.at[3, pl.ds(cut, rows - cut)], buf_b.at[1, pl.ds(cut, rows - cut)], minus)
    c_m.start()
    return c_p, c_m


def ring_end(copies):
    a_p, a_m, b_p, b_m, c_p, c_m = copies
    for c in (b_p, b_m, c_p, c_m):
        c.wait_recv()


def ring_sent(copies):
    for c in copies:
        c.wait_send()


def rs_kernel(fx, fz, dn, ox, oz, od,
              sx, rx, ax, bx, tx, ax2, bx2, yx,
              sz, rz, az, bz, tz, az2, bz2, yz,
              sd, rd, ad, bd, ad2, bd2, yd,
              load_sem, send_sem, recv_sem):
    x, y, z, core = place()
    sib = device_at(x, y, z, 1 - core)
    xp, xm = device_at((x + 1) % 4, y, z, core), device_at((x + 3) % 4, y, z, core)
    zp, zm = device_at(x, y, (z + 1) % 4, core), device_at(x, y, (z + 3) % 4, core)
    yo = device_at(x, 1 - y, z, core)
    barrier = pltpu.get_barrier_semaphore()
    for d in (sib, xp, xm, zp, zm, yo):
        pl.semaphore_signal(barrier, inc=1, device_id=d, device_id_type=MESH)
    loads = []
    order = (2, 1, 3, 0)
    for r in order:
        pair = []
        for k, (src, dst) in enumerate(((fx.at[0, r], sx.at[r]), (fz.at[0, r], sz.at[r]),
                         (dn.at[:, :, (z + r) % 4, core], sd.at[r]))):
            c = pltpu.make_async_copy(src, dst, load_sem.at[r * 3 + k])
            c.start()
            pair.append(c)
        loads.append(pair)
    pl.semaphore_wait(barrier, 6)
    sems = Sems(send_sem, recv_sem)
    cores = []
    for r in order:
        pair = []
        for src, dst in ((fx.at[1, r], rx.at[r]), (fz.at[1, r], rz.at[r]),
                         (dn.at[:, :, (z + r) % 4, 1 - core], rd.at[r])):
            c = sems.copy(src, dst, sib)
            c.start()
            pair.append(c)
        cores.append(pair)

    def summed(k):
        r = order[k]
        for j, (s, got) in enumerate(((sx, rx), (sz, rz), (sd, rd))):
            loads[k][j].wait()
            cores[k][j].wait_recv()
            if j == 2:
                def body(i, _):
                    s[r, i // 2, i % 2] = s[r, i // 2, i % 2] + got[r, i // 2, i % 2]
                    return 0
                lax.fori_loop(0, 8, body, 0)
            else:
                add_rows(s.at[r], got.at[r], s.shape[1])

    rows_x, cut_x = 80, 48
    def d_copy(src, dst, lo, dev):
        return sems.copy(src.at[pl.ds(lo, 2)], dst.at[pl.ds(lo, 2)], dev)

    def d_add(dst, got, lo):
        def body(i, _):
            a, b = lo + i // 2, i % 2
            dst[a, b] = dst[a, b] + got[a, b]
            return 0
        lax.fori_loop(0, 4, body, 0)

    summed(0)
    a = []
    a.append((sems.copy(sx.at[2, pl.ds(0, 48)], ax.at[0, pl.ds(0, 48)], xp), sems.copy(sx.at[2, pl.ds(48, 32)], ax.at[1, pl.ds(48, 32)], xm)))
    a.append((sems.copy(sz.at[2, pl.ds(0, 48)], az.at[0, pl.ds(0, 48)], zp), sems.copy(sz.at[2, pl.ds(48, 32)], az.at[1, pl.ds(48, 32)], zm)))
    a.append((d_copy(sd.at[2], ad.at[0], 0, zp), d_copy(sd.at[2], ad.at[1], 2, zm)))
    for p in a:
        p[0].start(); p[1].start()
    summed(1)
    b = [[sems.copy(sx.at[1, pl.ds(48, 32)], bx.at[0, pl.ds(48, 32)], xp)],
         [sems.copy(sz.at[1, pl.ds(48, 32)], bz.at[0, pl.ds(48, 32)], zp)],
         [d_copy(sd.at[1], bd.at[0], 2, zp)]]
    for p in b:
        p[0].start()
    summed(2)
    b[0].append(sems.copy(sx.at[3, pl.ds(0, 48)], bx.at[1, pl.ds(0, 48)], xm))
    b[1].append(sems.copy(sz.at[3, pl.ds(0, 48)], bz.at[1, pl.ds(0, 48)], zm))
    b[2].append(d_copy(sd.at[3], bd.at[1], 0, zm))
    for p in b:
        p[1].start()
    c = []
    for j, (s, ba, bb, plus, minus) in enumerate(((sx, ax, bx, xp, xm), (sz, az, bz, zp, zm))):
        a[j][0].wait_recv()
        add_rows(s.at[1, pl.ds(0, 48)], ba.at[0, pl.ds(0, 48)], 48)
        cp = sems.copy(s.at[1, pl.ds(0, 48)], bb.at[0, pl.ds(0, 48)], plus)
        cp.start()
        a[j][1].wait_recv()
        add_rows(s.at[3, pl.ds(48, 32)], ba.at[1, pl.ds(48, 32)], 32)
        cm = sems.copy(s.at[3, pl.ds(48, 32)], bb.at[1, pl.ds(48, 32)], minus)
        cm.start()
        c.append((cp, cm))
    a[2][0].wait_recv()
    d_add(sd.at[1], ad.at[0], 0)
    cp = d_copy(sd.at[1], bd.at[0], 0, zp)
    cp.start()
    a[2][1].wait_recv()
    d_add(sd.at[3], ad.at[1], 2)
    cm = d_copy(sd.at[3], bd.at[1], 2, zm)
    cm.start()
    c.append((cp, cm))
    summed(3)

    second = []
    for j, (s, bb, t, ba2, bb2, plus, minus) in enumerate(((sx, bx, tx, ax2, bx2, zp, zm), (sz, bz, tz, az2, bz2, xp, xm))):
        for k in (*b[j], *c[j]):
            k.wait_recv()
        for r in range(4):
            got = (s[0, pl.ds(20 * r, 20)].astype(jnp.float32) + bb[0, pl.ds(20 * r, 20)].astype(jnp.float32) + bb[1, pl.ds(20 * r, 20)].astype(jnp.float32))
            t[r] = jnp.concatenate([got, jnp.zeros((12, got.shape[1]), jnp.float32)], axis=0).astype(jnp.bfloat16)
        second.append(ring_start(sems, t, ba2, bb2, 16, 32, plus, minus))
    for k in (*b[2], *c[2]):
        k.wait_recv()

    def body(i, _):
        p, q = i // 2, i % 2
        sd[0, p, q] = sd[0, p, q] + bd[0, p, q] + bd[1, p, q]
        return 0
    lax.fori_loop(0, 8, body, 0)
    def chunk(r, q):
        return sd.at[0, (x + r) % 4, q]
    dsec = [sems.copy(chunk(2, 0), ad2.at[0], xp), sems.copy(chunk(2, 1), ad2.at[1], xm),
            sems.copy(chunk(1, 1), bd2.at[0, 1], xp), sems.copy(chunk(3, 0), bd2.at[1, 0], xm)]
    for k in dsec:
        k.start()
    third = []
    for j, (t, ba2, bb2, plus, minus) in enumerate(((tx, ax2, bx2, zp, zm), (tz, az2, bz2, xp, xm))):
        third.append(ring_middle(sems, second[j], t, ba2, bb2, 16, 32, plus, minus))
    dsec[0].wait_recv()
    sd[0, (x + 1) % 4, 0] = sd[0, (x + 1) % 4, 0] + ad2[0]
    dc = [sems.copy(chunk(1, 0), bd2.at[0, 0], xp)]
    dc[0].start()
    dsec[1].wait_recv()
    sd[0, (x + 3) % 4, 1] = sd[0, (x + 3) % 4, 1] + ad2[1]
    dc.append(sems.copy(chunk(3, 1), bd2.at[1, 1], xm))
    dc[1].start()
    ys = []
    for j, (t, bb2, yb, o) in enumerate(((tx, bx2, yx, ox), (tz, bz2, yz, oz))):
        ring_end((*second[j], *third[j]))
        f = t[0].astype(jnp.float32) + bb2[0].astype(jnp.float32) + bb2[1].astype(jnp.float32)
        yb[0] = f[10:26].astype(jnp.bfloat16)
        o[...] = f[0:10]
        k = sems.copy(yb.at[0], yb.at[1], yo)
        k.start()
        ys.append(k)
    for k in (dsec[2], dsec[3], *dc):
        k.wait_recv()
    def full(q):
        return (sd[0, x, q].astype(jnp.float32) + bd2[0, q].astype(jnp.float32) + bd2[1, q].astype(jnp.float32))
    yd[0] = full(1 - y).astype(jnp.bfloat16)
    k = sems.copy(yd.at[0], yd.at[1], yo)
    k.start()
    ys.append(k)
    od[...] = full(y)
    for k, yb, o in zip(ys, (yx, yz, yd), (ox, oz, od)):
        k.wait_recv()
        o[...] = o[...] + yb[1][: o.shape[0]].astype(jnp.float32)
    for group in (*cores, *a, *b, *c, *second, *third, dsec, dc, ys):
        ring_sent(group)


def reduce_scatter(fx, fz, dn):
    nx, nz = fx.shape[1], fz.shape[1]
    bf, f32 = jnp.bfloat16, jnp.float32
    V = pltpu.VMEM
    def feature(n):
        return [V((4, 80, n), bf), V((4, 80, n), bf), V((2, 80, n), bf), V((2, 80, n), bf),
                V((4, 32, n), bf), V((2, 32, n), bf), V((2, 32, n), bf), V((2, 16, n), bf)]
    w = dn.shape[1]
    down = [V((4, 4, 2, 48, w), bf), V((4, 4, 2, 48, w), bf), V((2, 4, 2, 48, w), bf), V((2, 4, 2, 48, w), bf),
            V((2, 48, w), bf), V((2, 2, 48, w), bf), V((2, 48, w), bf)]
    return pl.pallas_call(
        rs_kernel,
        out_shape=(jax.ShapeDtypeStruct((10, nx), f32), jax.ShapeDtypeStruct((10, nz), f32), jax.ShapeDtypeStruct((48, w), f32)),
        in_specs=[pl.BlockSpec(memory_space=pl.ANY)] * 3,
        out_specs=[pl.BlockSpec(memory_space=pltpu.VMEM)] * 3,
        scratch_shapes=[*feature(nx), *feature(nz), *down,
                        pltpu.SemaphoreType.DMA((12,)), pltpu.SemaphoreType.DMA((51,)), pltpu.SemaphoreType.DMA((51,))],
        compiler_params=pltpu.CompilerParams(collective_id=0, has_side_effects=True, vmem_limit_bytes=60 * 1024 * 1024),
        name="sum_gradients",
    )(fx.reshape(2, 4, 80, nx), fz.reshape(2, 4, 80, nz), dn.reshape(4, 2, 4, 2, 48, w))


def project(barrier_operand, weight_matrix):
    return jnp.einsum(
        "ayb,bc->ayc", barrier_operand, weight_matrix, preferred_element_type=jnp.float32
    )


def project_back(incoming_gradient, weight_matrix):
    return jnp.einsum(
        "zhn,rn->zhr", incoming_gradient, weight_matrix, preferred_element_type=jnp.float32
    )


def weight_grad(barrier_operand, incoming_gradient):
    return jnp.einsum(
        "jxy,jxz->yz", barrier_operand, incoming_gradient, preferred_element_type=jnp.float32
    )


def gelu_slope(hidden):
    normal_cdf = 0.5 * (1.0 + lax.erf(hidden * 0.7071067811865476))
    density = jnp.exp(-0.5 * hidden * hidden) * 0.3989422804014327
    return normal_cdf + hidden * density


def layer_norm(values, norm_gain, feat_mask, live_width):
    average = jnp.sum(values * feat_mask, -1, keepdims=True) / live_width
    centred = (values - average) * feat_mask
    spread = jnp.sum(centred * centred, -1, keepdims=True) / live_width
    inverse = lax.rsqrt(spread + EPSILON)
    normed = centred * inverse
    return (normed * norm_gain, normed, inverse)


def norm_back(incoming_gradient, norm_gain, normed, inverse, feat_mask, live_width):
    dnormed = incoming_gradient * norm_gain * feat_mask
    first_mean = jnp.sum(dnormed, -1, keepdims=True) / live_width
    second_moment_mean = jnp.sum(dnormed * normed, -1, keepdims=True) / live_width
    d_values = inverse * (dnormed - (first_mean + normed * second_moment_mean) * feat_mask)
    return (d_values, jnp.sum(incoming_gradient * normed, axis=(0, 1)))


def split_heads(values):
    return values.reshape(values.shape[0], values.shape[1], HEADS, HEAD_DIM)


def scores_of(queries, key_rows, permitted_mask):
    scaled = jnp.einsum(
        "sqhd,skhd->shqk",
        split_heads(queries),
        split_heads(key_rows),
        preferred_element_type=jnp.float32,
    ) * HEAD_DIM ** (-0.5)
    return jnp.where(permitted_mask, scaled, NEGATIVE)


def attend(queries, key_rows, value_rows, permitted_mask):
    scores = scores_of(queries, key_rows, permitted_mask)
    highest = jnp.max(scores, -1, keepdims=True)
    exponent = jnp.exp(scores - highest)
    summed = jnp.sum(exponent, -1, keepdims=True)
    attention = (exponent / summed).astype(jnp.bfloat16)
    blended = jnp.einsum(
        "shqk,skhd->sqhd", attention, split_heads(value_rows), preferred_element_type=jnp.float32
    )
    return (blended.reshape(queries.shape[0], queries.shape[1], -1), highest + jnp.log(summed))


def attend_back(d_blended, queries, key_rows, value_rows, permitted_mask, logsum):
    scores = scores_of(queries, key_rows, permitted_mask)
    attention = jnp.exp(scores - logsum)
    d_heads = split_heads(d_blended)
    d_values = jnp.einsum(
        "shqk,sqhd->skhd",
        attention.astype(jnp.bfloat16),
        d_heads,
        preferred_element_type=jnp.float32,
    )
    d_attention = jnp.einsum(
        "sqhd,skhd->shqk", d_heads, split_heads(value_rows), preferred_element_type=jnp.float32
    )
    d_scores = (
        attention * (d_attention - jnp.sum(attention * d_attention, -1, keepdims=True))
    ).astype(jnp.bfloat16)
    factor = HEAD_DIM ** (-0.5)
    d_queries = (
        jnp.einsum(
            "shqk,skhd->sqhd", d_scores, split_heads(key_rows), preferred_element_type=jnp.float32
        )
        * factor
    )
    d_keys = (
        jnp.einsum(
            "shqk,sqhd->skhd", d_scores, split_heads(queries), preferred_element_type=jnp.float32
        )
        * factor
    )
    return (
        d_queries.reshape(queries.shape),
        d_keys.reshape(key_rows.shape),
        d_values.reshape(key_rows.shape),
    )


def self_forward(inputs, norm_gain, w_qkv, w_out, permitted_mask, meta, rows):
    live_width, feat_mask, head_mask = (meta[0], meta[1], meta[2])
    normed_out, normed, inverse = layer_norm(inputs, norm_gain, feat_mask, live_width)
    barrier_operand = normed_out.astype(jnp.bfloat16)
    triple = project(barrier_operand, w_qkv).astype(jnp.bfloat16)
    queries, key_rows, value_rows = jnp.split(triple, 3, axis=-1)
    blended, logsum = attend(queries, key_rows, value_rows, permitted_mask)
    heads_out = (blended * head_mask).astype(jnp.bfloat16)
    after = inputs + project(heads_out, w_out) * feat_mask * rows
    return (
        after,
        (normed, inverse, barrier_operand, queries, key_rows, value_rows, logsum, heads_out),
    )


def self_backward(d_after, cache, norm_gain, w_qkv, w_out, permitted_mask, meta, rows, order_x, order_z):
    live_width, feat_mask, head_mask = (meta[0], meta[1], meta[2])
    normed, inverse, barrier_operand, queries, key_rows, value_rows, logsum, heads_out = cache
    d_branch = (d_after * feat_mask * rows).astype(jnp.bfloat16)
    dw_out = weight_grad16(layer_part(heads_out, order_z), d_branch)
    d_heads = (project_back(d_branch, w_out) * head_mask).astype(jnp.bfloat16)
    d_queries, d_keys, d_values = attend_back(
        d_heads, queries, key_rows, value_rows, permitted_mask, logsum
    )
    d_triple = jnp.concatenate([d_queries, d_keys, d_values], axis=-1).astype(jnp.bfloat16)
    dw_x = weight_grad16(layer_part(barrier_operand, order_x), d_triple[..., :1280])
    dw_z = weight_grad16(layer_part(barrier_operand, order_z), d_triple[..., 1280:])
    d_inputs, d_gain = norm_back(
        project_back(d_triple, w_qkv), norm_gain, normed, inverse, feat_mask, live_width
    )
    return (d_after + d_inputs, d_gain, dw_x, dw_z, dw_out)


def feed_forward(inputs, norm_gain, w_up, w_down, meta, rows):
    live_width, feat_mask, unit_mask = (meta[0], meta[1], meta[3])
    normed_out, normed, inverse = layer_norm(inputs, norm_gain, feat_mask, live_width)
    barrier_operand = normed_out.astype(jnp.bfloat16)
    hidden = project(barrier_operand, w_up)
    activated = (jax.nn.gelu(hidden, approximate=False) * unit_mask).astype(jnp.bfloat16)
    after = inputs + project(activated, w_down) * feat_mask * rows
    return (after, (normed, inverse, barrier_operand, hidden, activated))


def ffn_back(d_after, cache, norm_gain, w_up, w_down, meta, rows, order_x):
    live_width, feat_mask, unit_mask = (meta[0], meta[1], meta[3])
    normed, inverse, barrier_operand, hidden, activated = cache
    d_branch = (d_after * feat_mask * rows).astype(jnp.bfloat16)
    dw_down = weight_grad16(activated, d_branch)
    d_hidden = (project_back(d_branch, w_down) * unit_mask * gelu_slope(hidden)).astype(
        jnp.bfloat16
    )
    dw_up = weight_grad16(layer_part(barrier_operand, order_x), d_hidden)
    d_inputs, d_gain = norm_back(
        project_back(d_hidden, w_up), norm_gain, normed, inverse, feat_mask, live_width
    )
    return (d_after + d_inputs, d_gain, dw_up, dw_down)


def cross_forward(inputs, norm_gain, w_cross, key_value, permitted_mask, meta, rows):
    live_width, feat_mask, head_mask = (meta[0], meta[1], meta[2])
    model_width = inputs.shape[-1]
    normed_out, normed, inverse = layer_norm(inputs, norm_gain, feat_mask, live_width)
    barrier_operand = normed_out.astype(jnp.bfloat16)
    queries = project(barrier_operand, w_cross[:, :model_width]).astype(jnp.bfloat16)
    key_rows = jnp.concatenate(
        [key_value[0, :, :, :model_width], key_value[1, :, :, :model_width]], axis=1
    )
    value_rows = jnp.concatenate(
        [key_value[0, :, :, model_width:], key_value[1, :, :, model_width:]], axis=1
    )
    blended, logsum = attend(queries, key_rows, value_rows, permitted_mask)
    heads_out = (blended * head_mask).astype(jnp.bfloat16)
    after = inputs + project(heads_out, w_cross[:, model_width:]) * feat_mask * rows
    return (
        after,
        (normed, inverse, barrier_operand, queries, key_rows, value_rows, logsum, heads_out),
    )


def cross_backward(d_after, cache, norm_gain, w_cross, permitted_mask, meta, rows, order_x):
    live_width, feat_mask, head_mask = (meta[0], meta[1], meta[2])
    normed, inverse, barrier_operand, queries, key_rows, value_rows, logsum, heads_out = cache
    model_width = d_after.shape[-1]
    d_branch = (d_after * feat_mask * rows).astype(jnp.bfloat16)
    dw_output = weight_grad16(layer_part(heads_out, order_x), d_branch)
    d_heads = (project_back(d_branch, w_cross[:, model_width:]) * head_mask).astype(jnp.bfloat16)
    d_queries, d_keys, d_values = attend_back(
        d_heads, queries, key_rows, value_rows, permitted_mask, logsum
    )
    d_queries = d_queries.astype(jnp.bfloat16)
    dw_query = weight_grad16(layer_part(barrier_operand, order_x), d_queries)
    d_inputs, d_gain = norm_back(
        project_back(d_queries, w_cross[:, :model_width]),
        norm_gain,
        normed,
        inverse,
        feat_mask,
        live_width,
    )
    half = d_keys.shape[1] // 2
    d_key_value = jnp.stack(
        [
            jnp.concatenate([d_keys[:, :half], d_values[:, :half]], axis=-1),
            jnp.concatenate([d_keys[:, half:], d_values[:, half:]], axis=-1),
        ]
    ).astype(jnp.bfloat16)
    return (d_after + d_inputs, d_gain, jnp.concatenate([dw_query, dw_output], axis=1), d_key_value)


def layer_part(values, order):
    picks = (jnp.arange(640, dtype=jnp.int32)[:, None] == order[None, :]).astype(jnp.bfloat16)
    return jnp.einsum("ayb,bc->ayc", values, picks, preferred_element_type=jnp.float32).astype(jnp.bfloat16)


def weight_grad16(operand, gradient):
    return weight_grad(operand, gradient).astype(jnp.bfloat16)


def shards(stream, cotangent, lengths, pieces, configs, gains, attn_qkv, attn_out, ffn_up, ffn_down, cross_proj):
    f32, bf16 = jnp.float32, jnp.bfloat16
    micro, length, width = stream.shape[1], stream.shape[3], stream.shape[4]
    hidden_width = ffn_up.shape[2]
    later = lax.axis_index("section") == 1
    rows_in = stream.reshape(micro, length, width)
    cot = cotangent.reshape(micro, length, width).astype(f32)
    norm_gain = gains[0].astype(f32)
    w_qkv, w_out, w_up, w_down, w_cross = attn_qkv[0], attn_out[0], ffn_up[0], ffn_down[0], cross_proj[0]
    enc_rows = lax.ppermute(rows_in, "section", [(0, 1)])
    enc_gain = lax.ppermute(gains[0, 2:3], "section", [(0, 1)]).astype(f32)[0]
    enc_cross = lax.ppermute(w_cross, "section", [(0, 1)])
    chosen = configs[pieces[:, 0]]
    lens = lengths[:, :, 0]
    own = jnp.where(later, lens[1], lens[0])
    heads_full = (chosen[:, 1] == HEADS).astype(jnp.int32)
    wide_two = (chosen[:, 2] > FF_BLOCK).astype(jnp.int32)
    wide_three = (chosen[:, 2] > 2 * FF_BLOCK).astype(jnp.int32)
    counts = jnp.stack([jnp.sum(own), jnp.sum(own * heads_full), jnp.sum(own * wide_two), jnp.sum(own * wide_three)])
    counts = lax.psum(counts, "dp")

    places = jnp.arange(length, dtype=jnp.int32)
    feature = jnp.arange(width, dtype=jnp.int32)
    live_width = chosen[:, 0].astype(f32)[:, None, None]
    feat_mask = (feature[None, None, :] < chosen[:, 0, None, None]).astype(f32)
    head_mask = ((feature // HEAD_DIM)[None, None, :] < chosen[:, 1, None, None]).astype(f32)
    unit_mask = (jnp.arange(hidden_width, dtype=jnp.int32)[None, None, :] < chosen[:, 2, None, None]).astype(f32)
    rows = (places[None, :] < own[:, None]).astype(f32)[:, :, None]
    self_allowed = (places[None, None, None, :] < own[:, None, None, None]) & (
        (places[None, None, None, :] <= places[None, None, :, None]) | jnp.logical_not(later))
    key_slots = jnp.arange(2 * length, dtype=jnp.int32)
    cross_allowed = ((key_slots % length)[None, None, None, :] < lens[0][:, None, None, None]) & (
        (key_slots // length)[None, None, None, :] < chosen[:, 3, None, None, None])
    meta = (live_width, feat_mask, head_mask, unit_mask)

    x = rows_in.astype(f32)
    x1, self_cache = self_forward(x, norm_gain[0], w_qkv, w_out, self_allowed, meta, rows)

    def enc_a():
        x2, _ = feed_forward(x1, norm_gain[1], w_up, w_down, meta, rows)
        fresh, _, _ = layer_norm(x2, norm_gain[2], feat_mask, live_width)
        return x2, fresh.astype(bf16)

    x2, fresh = lax.cond(later, lambda: (x1, jnp.zeros(rows_in.shape, bf16)), enc_a)
    fresh = lax.ppermute(fresh, "section", [(0, 1)])

    order_x, order_z = relative_order("x"), relative_order("z")

    def dec_b():
        old, _, _ = layer_norm(enc_rows.astype(f32), enc_gain, feat_mask, live_width)
        encoded = jnp.stack([fresh, old.astype(bf16)])
        key_value = jnp.einsum("jsld,de->jsle", encoded, enc_cross, preferred_element_type=f32).astype(bf16)
        y2, cross_cache = cross_forward(x1, norm_gain[1], w_cross, key_value, cross_allowed, meta, rows)
        y3, ffn_cache = feed_forward(y2, norm_gain[2], w_up, w_down, meta, rows)
        d_y2, gain_ffn, d_up, d_down = ffn_back(cot, ffn_cache, norm_gain[2], w_up, w_down, meta, rows, order_x)
        d_y1, gain_cross, d_cross, d_kv = cross_backward(d_y2, cross_cache, norm_gain[1], w_cross, cross_allowed, meta, rows, order_x)
        d_enc = jnp.einsum("jsle,de->jsld", d_kv, enc_cross, preferred_element_type=f32).astype(bf16)
        d_wc = weight_grad16(layer_part(encoded.reshape(-1, length, width), order_z), d_kv.reshape(-1, length, 2 * width))
        return y3, d_y1, gain_cross, gain_ffn, d_up, d_down, d_cross, d_wc, d_enc

    def enc_b():
        z = jnp.zeros
        return (x2, x1, z(width, f32), z(width, f32), z((width, hidden_width), bf16), z((hidden_width, width), bf16),
                z((width, 2 * width), bf16), z((width, 2 * width), bf16), z((2, *rows_in.shape), bf16))

    out, d_y1, gain_b, gain_c, d_up, d_down, d_cross, d_wc, d_enc = lax.cond(later, dec_b, enc_b)
    back = lax.ppermute(d_enc, "section", [(1, 0)])

    def enc_c():
        _, hat_new, inv_new = layer_norm(x2, norm_gain[2], feat_mask, live_width)
        _, hat_old, inv_old = layer_norm(x, norm_gain[2], feat_mask, live_width)
        _, ffn_cache = feed_forward(x1, norm_gain[1], w_up, w_down, meta, rows)
        d_new, gain_new = norm_back(back[0].astype(f32), norm_gain[2], hat_new, inv_new, feat_mask, live_width)
        d_old, gain_old = norm_back(back[1].astype(f32), norm_gain[2], hat_old, inv_old, feat_mask, live_width)
        d_x1, gain_ffn, du, dd = ffn_back(cot + d_new, ffn_cache, norm_gain[1], w_up, w_down, meta, rows, order_x)
        return d_x1, d_old, gain_ffn, gain_new + gain_old, du, dd

    d_x1, d_old, gain_b, gain_c, d_up, d_down = lax.cond(
        later, lambda: (d_y1, jnp.zeros_like(x), gain_b, gain_c, d_up, d_down), enc_c)
    d_in, gain_a, d_qkv_x, d_qkv_z, d_out = self_backward(
        d_x1, self_cache, norm_gain[0], w_qkv, w_out, self_allowed, meta, rows, order_x, order_z)
    d_in = d_in + d_old
    gain_t = jnp.stack([gain_a, gain_b, gain_c])
    picks = (feature[:, None] == order_z[None, :]).astype(f32)
    gain_t = jnp.einsum("gf,fp->pg", gain_t, picks, precision=lax.Precision.HIGHEST).astype(bf16)
    gain_t = jnp.pad(gain_t, ((0, 0), (0, 125)))
    fx = jnp.concatenate([d_up, d_qkv_x, d_cross], axis=1)
    fz = jnp.concatenate([d_out, d_qkv_z, gain_t, d_wc], axis=1)
    ox, oz, od = reduce_scatter(fx, fz, d_down)
    enc_cross_grad = lax.ppermute(oz[:, 1408:2688], "section", [(1, 0)])

    tokens_all = micro * lax.axis_size("dp") * length
    rates = tokens_all / (counts + tokens_all // 8)
    qkv_cols = jnp.arange(3 * width, dtype=jnp.int32) % width // HEAD_DIM >= HEADS // 2
    out_count = width // lax.axis_size("dp")
    out_rows = (lax.axis_index("dp") * out_count + jnp.arange(out_count, dtype=jnp.int32)) // HEAD_DIM >= HEADS // 2
    up_block = jnp.arange(hidden_width, dtype=jnp.int32) // FF_BLOCK
    up_rate = jnp.where(up_block == 0, rates[0], jnp.where(up_block == 1, rates[2], rates[3]))
    down_count = hidden_width // lax.axis_size("dp")
    down_block = (lax.axis_index("dp") * down_count + jnp.arange(down_count, dtype=jnp.int32)) // FF_BLOCK
    down_rate = jnp.where(down_block == 0, rates[0], jnp.where(down_block == 1, rates[2], rates[3]))
    layer_out = out.astype(bf16).reshape(stream.shape)
    stream_grad = d_in.astype(bf16).reshape(stream.shape)
    gain_grad = oz[:, 1280:1283].T[None]
    qkv_grad = (jnp.concatenate([ox[:, 3072:4352], oz[:, 640:1280]], axis=1) * jnp.where(qkv_cols, rates[1], rates[0])[None, :])[None]
    out_grad = (oz[:, :640] * jnp.where(out_rows, rates[1], rates[0])[:, None])[None]
    up_grad = (ox[:, :3072] * up_rate[None, :])[None]
    down_grad = (od * down_rate[:, None])[None]
    cross_grad = jnp.where(later, ox[:, 4352:5632], enc_cross_grad)[None]
    return (layer_out, stream_grad, gain_grad, qkv_grad, out_grad, up_grad, down_grad, cross_grad)


def solution(mesh):
    in_specs = (
        P("section", None, "dp", None, None),
        P("section", None, "dp", None, None),
        P(None, None, "dp"),
        P(None, "dp"),
        P(),
        P("section", None, None),
        P("section", None, None),
        P("section", None, None),
        P("section", None, None),
        P("section", None, None),
        P("section", None, None),
    )
    out_specs = (
        P("section", None, "dp", None, None),
        P("section", None, "dp", None, None),
        P("section", None, "dp"),
        P("section", "dp", None),
        P("section", "dp", None),
        P("section", "dp", None),
        P("section", "dp", None),
        P("section", "dp", None),
    )
    return jax.shard_map(shards, mesh=mesh, in_specs=in_specs, out_specs=out_specs, check_vma=False)
```

```python
import functools

import jax
import jax.numpy as jnp
from jax import lax
from jax.experimental import pallas as pl
from jax.experimental.pallas import tpu as pltpu
from jax.sharding import PartitionSpec as P

F32, BF16 = jnp.float32, jnp.bfloat16
D, HEADS, HEAD_DIM, FF, FF_BLOCK = 640, 8, 80, 3072, 1024
SEQ, SENTENCES = 128, 4
ROWS = SEQ * SENTENCES
HALF = ROWS // 2
TILE = 512
EPSILON = 1e-05
NEGATIVE = -1e30
SCALE = HEAD_DIM ** (-0.5)
LOG2E = 1.4426950408889634
MESH = pl.DeviceIdType.MESH
VMEM_LIMIT = 62 * 1024 * 1024
NX, NY, NZ, CORES = 4, 2, 4, 2


def place():
    me = lax.axis_index("dp")
    core = me % CORES
    z = me // CORES % NZ
    y = me // (CORES * NZ) % NY
    x = me // (CORES * NZ * NY)
    return x, y, z, core


def device_at(x, y, z, core):
    return {"dp": ((x * NY + y) * NZ + z) * CORES + core}


def relative_order(first):
    x, y, z, core = place()
    spot = jnp.arange(D, dtype=jnp.int32)
    rc, ra, rb, ry, t = spot // 320, spot // 80 % 4, spot // 20 % 4, spot // 10 % 2, spot % 10
    rx, rz = (ra, rb) if first == "x" else (rb, ra)
    cx, cy, cz, cc = (x + rx) % 4, (y + ry) % 2, (z + rz) % 4, (core + rc) % 2
    return (((cx * 2 + cy) * 4 + cz) * 2 + cc) * 10 + t


def mm(a, b):
    return lax.dot_general(a, b, (((1,), (0,)), ((), ())), preferred_element_type=F32)


def mm_nt(a, b):
    return lax.dot_general(a, b, (((1,), (1,)), ((), ())), preferred_element_type=F32)


def mm_tn(a, b):
    return lax.dot_general(a, b, (((0,), (0,)), ((), ())), preferred_element_type=F32)


def block(m, size=SEQ):
    if isinstance(m, int):
        return pl.ds(m * size, size)
    return pl.ds(pl.multiple_of(m * size, size), size)


def each(lo, count, body):
    def step(i, _):
        body(lo + i)
        return 0

    lax.fori_loop(0, count, step, 0)


def normalize(v, mask, inv_width):
    centred = (v - jnp.sum(v * mask, -1, keepdims=True) * inv_width) * mask
    spread = jnp.sum(centred * centred, -1, keepdims=True) * inv_width
    inverse = lax.rsqrt(spread + EPSILON)
    return centred * inverse, inverse


def normalize_back(dn, normed, inverse, mask, inv_width):
    dn = dn * mask
    first = jnp.sum(dn, -1, keepdims=True) * inv_width
    second = jnp.sum(dn * normed, -1, keepdims=True) * inv_width
    return inverse * (dn - (first + normed * second) * mask)


def window(h):
    return HEAD_DIM * h // 128 * 128, -(-HEAD_DIM * (h + 1) // 128) * 128


def head_lanes(h):
    lo, hi = window(h)
    lanes = lax.broadcasted_iota(jnp.int32, (1, hi - lo), 1) + lo
    return ((lanes >= HEAD_DIM * h) & (lanes < HEAD_DIM * (h + 1))).astype(F32).astype(BF16)


class Tiles:
    def __init__(self):
        self.tile = {}

    def add(self, h, value):
        lo, hi = window(h)
        for j in range(lo // 128, hi // 128):
            part = value[:, j * 128 - lo : j * 128 - lo + 128]
            self.tile[j] = self.tile[j] + part if j in self.tile else part

    def whole(self):
        return jnp.concatenate([self.tile[j] for j in range(D // 128)], axis=1)


class Sentence:
    def __init__(self, meta, m):
        self.meta, self.m = meta, m
        lanes = lax.broadcasted_iota(jnp.int32, (1, D), 1)
        self.mask = (lanes < meta[m, 0]).astype(F32)
        self.heads = (lanes < meta[m, 1]).astype(F32)
        self.inv = 1.0 / meta[m, 0].astype(F32)

    def rows(self):
        return (lax.broadcasted_iota(jnp.int32, (SEQ, 1), 0) < self.meta[self.m, 4]).astype(F32)

    def self_bias(self):
        k = lax.broadcasted_iota(jnp.int32, (SEQ, SEQ), 0)
        q = lax.broadcasted_iota(jnp.int32, (SEQ, SEQ), 1)
        allowed = (k < self.meta[self.m, 4]) & (k <= q + (1 - self.meta[self.m, 6]) * SEQ)
        return jnp.where(allowed, 0.0, NEGATIVE)

    def cross_bias(self):
        k = lax.broadcasted_iota(jnp.int32, (2 * SEQ, 1), 0)
        allowed = (jnp.where(k < SEQ, k, k - SEQ) < self.meta[self.m, 5]) & (k < self.meta[self.m, 3])
        return jnp.where(allowed, 0.0, NEGATIVE)


def softmax_columns(scores, bias):
    scores = scores + bias
    exponent = jnp.exp2((scores - jnp.max(scores, 0, keepdims=True)) * (SCALE * LOG2E))
    return (exponent * (1.0 / jnp.sum(exponent, 0, keepdims=True))).astype(BF16)


def attend(query, keys, values, bias, keep):
    scores = [mm_nt(keys(h), query(h) * head_lanes(h)) for h in range(HEADS)]
    weights = [softmax_columns(s, bias) for s in scores]
    out = Tiles()
    for h in range(HEADS):
        keep(h, weights[h])
        out.add(h, mm_tn(weights[h], values(h) * head_lanes(h)))
    return out.whole()


def attend_back(d_out, query, keys, values, weights):
    d_weights = [mm_nt(values(h), d_out(h) * head_lanes(h)) for h in range(HEADS)]
    d_values = Tiles()
    for h in range(HEADS):
        d_values.add(h, mm(weights(h), d_out(h) * head_lanes(h)))
    d_values = d_values.whole().astype(BF16)
    d_scores = []
    for h in range(HEADS):
        p = weights(h).astype(F32)
        product = p * d_weights[h]
        d_scores.append((product - p * jnp.sum(product, 0, keepdims=True)).astype(BF16))
    d_keys = Tiles()
    for h in range(HEADS):
        d_keys.add(h, mm(d_scores[h], query(h) * head_lanes(h)))
    d_keys = (d_keys.whole() * SCALE).astype(BF16)
    d_query = Tiles()
    for h in range(HEADS):
        d_query.add(h, mm_tn(d_scores[h], keys(h) * head_lanes(h)))
    return (d_query.whole() * SCALE).astype(BF16), d_keys, d_values


def gelu_pair(z):
    cdf = 0.5 + 0.5 * lax.erf(z * 0.7071067811865476)
    density = jnp.exp2(z * z * (-0.5 * LOG2E)) * 0.3989422804014327
    return z * cdf, cdf + z * density


def shape(*dims, dtype=BF16):
    return jax.ShapeDtypeStruct(dims, dtype)


IN_VMEM = pl.BlockSpec(memory_space=pltpu.VMEM)
IN_SMEM = pl.BlockSpec(memory_space=pltpu.SMEM)
IN_HBM = pl.BlockSpec(memory_space=pl.ANY)


def layers_kernel(meta, x_hbm, cot_hbm, gain_ref, wqkv_hbm, wout_hbm, wup_hbm, wdn_hbm, wcross_hbm, picks_hbm,
                  out_hbm, dx_hbm, extra_hbm, a_hbm, qkv_hbm, o_hbm, p_hbm, gsum_ref, dup_hbm, ddn_hbm, dcross_hbm, dwc_hbm,
                  x, cot, xenc, genc, wqkv, wout, wup, wdn, wcross, wc, picks,
                  a, qkv, o, p, x1, c, qc, ebuf, sbuf, kv, oc, pc, mid, b, u, g, lo, dbr, dbrc, dx, tmp, stage_up, stage_dn,
                  load_sem, out_sem, send_sem, recv_sem):
    section = lax.axis_index("section")
    px, py, pz, core = place()
    partner = {"section": 1 - section, "dp": lax.axis_index("dp")}
    across = {"section": 1 - section, **device_at(px, 1 - py, pz, core)}
    sibling = {"section": section, **device_at(px, py, pz, 1 - core)}
    barrier = pltpu.get_barrier_semaphore()
    for d in (partner, across, sibling):
        pl.semaphore_signal(barrier, inc=1, device_id=d, device_id_type=MESH)

    def load(k, src, dst):
        return pltpu.make_async_copy(src, dst, load_sem.at[k])

    def store(k, src, dst):
        return pltpu.make_async_copy(src, dst, out_sem.at[k])

    def remote(k, src, dst, device):
        return pltpu.make_async_remote_copy(
            src_ref=src, dst_ref=dst, send_sem=send_sem.at[k], recv_sem=recv_sem.at[k], device_id=device, device_id_type=MESH)

    get_x, get_qkv, get_out = load(0, x_hbm, x), load(1, wqkv_hbm, wqkv), load(2, wout_hbm, wout)
    get_up, get_dn, get_cross = load(3, wup_hbm, wup), load(4, wdn_hbm, wdn), load(5, wcross_hbm, wcross)
    get_cot, get_picks = load(6, cot_hbm, cot), load(7, picks_hbm, picks)
    for k in (get_x, get_qkv, get_out, get_up, get_dn, get_cross, get_cot, get_picks):
        k.start()
    pl.semaphore_wait(barrier, 3)
    part = pl.ds(pl.multiple_of(core * 320, 320), 320)
    rest = pl.ds(pl.multiple_of((1 - core) * 320, 320), 320)
    send_x = remote(0, x_hbm, xenc, partner)
    send_gain = remote(1, gain_ref, genc, partner)
    send_wc = remote(2, wcross_hbm.at[part], wc.at[part], across)
    share_wc = remote(3, wc.at[part], wc.at[part], sibling)

    def send_new(m):
        return remote(4 + m, sbuf.at[m, pl.ds(0, SEQ)], ebuf.at[m, pl.ds(0, SEQ)], partner)

    def send_old(m):
        return remote(8 + m, sbuf.at[m, pl.ds(SEQ, SEQ)], ebuf.at[m, pl.ds(SEQ, SEQ)], partner)

    @pl.when(section == 0)
    def _():
        send_gain.start()
        send_wc.start()
        send_x.start()

    gsum_ref[...] = jnp.zeros_like(gsum_ref)
    gain = [gain_ref[i : i + 1] for i in range(3)]

    get_x.wait()

    def norm_x(m):
        s = Sentence(meta, m)
        a[block(m)] = (normalize(x[block(m)].astype(F32), s.mask, s.inv)[0] * gain[0]).astype(BF16)

    each(0, SENTENCES, norm_x)
    get_qkv.wait()

    def project(j):
        qkv[:, block(j, D)] = mm(a[...], wqkv[:, block(j, D)]).astype(BF16)

    each(0, 3, project)
    keep = [store(0, a, a_hbm), store(1, qkv, qkv_hbm)]
    for k in keep:
        k.start()

    def self_attention(m):
        s = Sentence(meta, m)
        rows = block(m)

        def keep_p(h, value):
            p[m * HEADS + h] = value

        blended = attend(
            lambda h: qkv[rows, slice(*window(h))],
            lambda h: qkv[rows, D + window(h)[0] : D + window(h)[1]],
            lambda h: qkv[rows, 2 * D + window(h)[0] : 2 * D + window(h)[1]],
            s.self_bias(), keep_p)
        o[rows] = (blended * s.heads).astype(BF16)

    each(0, SENTENCES, self_attention)
    keep += [store(2, o, o_hbm), store(3, p, p_hbm)]
    for k in keep[2:]:
        k.start()
    get_out.wait()
    x1[...] = mm(o[...], wout[...])

    def add_attention(m):
        s = Sentence(meta, m)
        rows = block(m)
        x1[rows] = x[rows].astype(F32) + x1[rows] * s.mask * s.rows()

    each(0, SENTENCES, add_attention)

    def ffn_forward(half, base, g_row, finish):
        rows = block(half, HALF)

        def norm(m):
            s = Sentence(meta, m)
            b[block(m)] = (normalize(base[block(m)], s.mask, s.inv)[0] * gain[g_row]).astype(BF16)

        each(2 * half, 2, norm)
        live = [[(t * TILE < meta[2 * half + i, 2]).astype(F32) for t in range(FF // TILE)] for i in range(2)]
        z = mm(b[rows], wup[:, 0:TILE])
        for t in range(FF // TILE):
            after = mm(b[rows], wup[:, (t + 1) * TILE : (t + 2) * TILE]) if t + 1 < FF // TILE else None
            cols = pl.ds(t * TILE, TILE)
            for i in range(2):
                value, slope = gelu_pair(z[i * SEQ : (i + 1) * SEQ])
                u[block(2 * half + i), cols] = (value * live[i][t]).astype(BF16)
                g[block(2 * half + i), cols] = (slope * live[i][t]).astype(BF16)
            z = after
        tmp[...] = mm(u[rows], wdn[...])

        def result(i):
            m = 2 * half + i
            s = Sentence(meta, m)
            value = base[block(m)] + tmp[block(i)] * s.mask * s.rows()
            lo[block(m)] = value.astype(BF16)
            finish(m, s, value)

        each(0, 2, result)

    def ffn_back(half, base, g_row):
        rows = block(half, HALF)
        for t in range(FF // TILE):
            cols = pl.ds(t * TILE, TILE)
            g[rows, cols] = (mm_nt(dbr[rows], wdn[cols]) * g[rows, cols].astype(F32)).astype(BF16)
        tmp[...] = mm_nt(g[rows], wup[...])

        def result(i):
            m = 2 * half + i
            s = Sentence(meta, m)
            n, r = normalize(base[block(m)], s.mask, s.inv)
            dy = tmp[block(i)]
            gsum_ref[g_row : g_row + 1] += jnp.sum(dy * n, 0, keepdims=True)
            dx[block(m)] += normalize_back(dy * gain[g_row], n, r, s.mask, s.inv)

        each(0, 2, result)

    def turned(k, value):
        return mm_nt(picks[k], value).astype(BF16)

    def ffn_weights():
        bt = turned(0, b[...])
        pieces = []
        for t in range(FF // FF_BLOCK):
            slot = t % 2
            cols = pl.ds(t * FF_BLOCK, FF_BLOCK)
            if t >= 2:
                for k in pieces[2 * (t - 2) : 2 * (t - 1)]:
                    k.wait()
            stage_dn[slot] = mm_tn(u[:, cols], dbr[...]).astype(BF16)
            stage_up[slot] = mm(bt, g[:, cols]).astype(BF16)
            pieces += [store(4 + 2 * t, stage_dn.at[slot], ddn_hbm.at[cols]), store(5 + 2 * t, stage_up.at[slot], dup_hbm.at[:, cols])]
            for k in pieces[-2:]:
                k.start()
        return pieces[2:]

    @pl.when(section == 0)
    def _():
        get_up.wait()
        get_dn.wait()

        def forward(half):
            def finish(m, s, value):
                mid[block(m)] = value
                sbuf[m, 0:SEQ] = (normalize(value, s.mask, s.inv)[0] * gain[2]).astype(BF16)
                send_new(m).start()

            ffn_forward(half, x1, 1, finish)

        each(0, 2, forward)
        put_out = store(10, lo, out_hbm)
        put_out.start()
        get_cot.wait()

        def backward(half):
            def start(i):
                m = 2 * half + i
                s = Sentence(meta, m)
                send_new(m).wait_recv()
                n, r = normalize(mid[block(m)], s.mask, s.inv)
                dy = ebuf[m, 0:SEQ].astype(F32)
                gsum_ref[2:3] += jnp.sum(dy * n, 0, keepdims=True)
                d = cot[block(m)].astype(F32) + normalize_back(dy * gain[2], n, r, s.mask, s.inv)
                dx[block(m)] = d
                dbr[block(m)] = (d * s.mask * s.rows()).astype(BF16)

            each(0, 2, start)
            ffn_back(half, x1, 1)

        each(0, 2, backward)
        get_picks.wait()
        put_dx = store(11, dx, dx_hbm)
        put_dx.start()
        pieces = ffn_weights()

        def old(m):
            s = Sentence(meta, m)
            send_old(m).wait_recv()
            n, r = normalize(x[block(m)].astype(F32), s.mask, s.inv)
            dy = ebuf[m, SEQ : 2 * SEQ].astype(F32)
            gsum_ref[2:3] += jnp.sum(dy * n, 0, keepdims=True)
            mid[block(m)] = normalize_back(dy * gain[2], n, r, s.mask, s.inv)

        each(0, SENTENCES, old)
        put_extra = store(12, mid, extra_hbm)
        put_extra.start()
        get_cross.wait()
        for k in (put_out, put_dx, put_extra, *pieces):
            k.wait()
        send_x.wait_send()
        send_gain.wait_send()
        send_wc.wait_send()
        each(0, SENTENCES, lambda m: send_new(m).wait_send())

    @pl.when(section == 1)
    def _():
        get_cross.wait()

        def norm(m):
            s = Sentence(meta, m)
            c[block(m)] = (normalize(x1[block(m)], s.mask, s.inv)[0] * gain[1]).astype(BF16)

        each(0, SENTENCES, norm)
        qc[...] = mm(c[...], wcross[:, 0:D]).astype(BF16)
        send_gain.wait_recv()
        send_x.wait_recv()

        def old(m):
            s = Sentence(meta, m)
            ebuf[m, SEQ : 2 * SEQ] = (normalize(xenc[block(m)].astype(F32), s.mask, s.inv)[0] * genc[2:3]).astype(BF16)

        each(0, SENTENCES, old)
        send_wc.wait_recv()
        share_wc.start()
        share_wc.wait_recv()

        def old_kv(m):
            kv[m, SEQ : 2 * SEQ] = mm(ebuf[m, SEQ : 2 * SEQ], wc[...]).astype(BF16)

        each(0, SENTENCES, old_kv)
        get_cot.wait()
        get_up.wait()
        get_dn.wait()

        def start_back(m):
            s = Sentence(meta, m)
            d = cot[block(m)].astype(F32)
            dx[block(m)] = d
            dbr[block(m)] = (d * s.mask * s.rows()).astype(BF16)

        each(0, SENTENCES, start_back)

        def middle(half):
            rows = block(half, HALF)

            def new_kv(m):
                send_new(m).wait_recv()
                kv[m, 0:SEQ] = mm(ebuf[m, 0:SEQ], wc[...]).astype(BF16)

            each(2 * half, 2, new_kv)

            def cross(m):
                s = Sentence(meta, m)

                def keep_p(h, value):
                    pc[m * HEADS + h] = value

                blended = attend(
                    lambda h: qc[block(m), slice(*window(h))],
                    lambda h: kv[m, :, slice(*window(h))],
                    lambda h: kv[m, :, D + window(h)[0] : D + window(h)[1]],
                    s.cross_bias(), keep_p)
                oc[block(m)] = (blended * s.heads).astype(BF16)

            each(2 * half, 2, cross)
            tmp[...] = mm(oc[rows], wcross[:, D : 2 * D])

            def add_cross(i):
                m = 2 * half + i
                s = Sentence(meta, m)
                mid[block(m)] = x1[block(m)] + tmp[block(i)] * s.mask * s.rows()

            each(0, 2, add_cross)
            ffn_forward(half, mid, 2, lambda m, s, value: None)
            ffn_back(half, mid, 2)

            def branch(m):
                s = Sentence(meta, m)
                dbrc[block(m)] = (dx[block(m)] * s.mask * s.rows()).astype(BF16)

            each(2 * half, 2, branch)
            tmp[...] = mm_nt(dbrc[rows], wcross[:, D : 2 * D])

            def cross_back(i):
                m = 2 * half + i
                s = Sentence(meta, m)
                sbuf[m, 0:SEQ] = (tmp[block(i)] * s.heads).astype(BF16)
                dq, dk, dv = attend_back(
                    lambda h: sbuf[m, 0:SEQ, slice(*window(h))],
                    lambda h: qc[block(m), slice(*window(h))],
                    lambda h: kv[m, :, slice(*window(h))],
                    lambda h: kv[m, :, D + window(h)[0] : D + window(h)[1]],
                    lambda h: pc[m * HEADS + h])
                qc[block(m)] = dq
                kv[m, :, 0:D] = dk
                kv[m, :, D : 2 * D] = dv
                sbuf[m] = mm_nt(kv[m], wc[...]).astype(BF16)
                send_new(m).start()

            each(0, 2, cross_back)
            each(2 * half, 2, lambda m: send_old(m).start())
            tmp[...] = mm_nt(qc[rows], wcross[:, 0:D])

            def first_norm(i):
                m = 2 * half + i
                s = Sentence(meta, m)
                n, r = normalize(x1[block(m)], s.mask, s.inv)
                dy = tmp[block(i)]
                gsum_ref[1:2] += jnp.sum(dy * n, 0, keepdims=True)
                dx[block(m)] += normalize_back(dy * gain[1], n, r, s.mask, s.inv)

            each(0, 2, first_norm)

        each(0, 2, middle)
        put_out = store(10, lo, out_hbm)
        put_out.start()
        put_dx = store(11, dx, dx_hbm)
        put_dx.start()
        get_picks.wait()
        pieces = ffn_weights()
        for k in pieces:
            k.wait()
        stage_up[0, :, 0:D] = mm(turned(0, c[...]), qc[...]).astype(BF16)
        put_q = store(13, stage_up.at[0, :, pl.ds(0, D)], dcross_hbm.at[:, pl.ds(0, D)])
        put_q.start()
        stage_up[1, :, 0:D] = mm(turned(0, oc[...]), dbrc[...]).astype(BF16)
        put_o = store(14, stage_up.at[1, :, pl.ds(0, D)], dcross_hbm.at[:, pl.ds(D, D)])
        put_o.start()
        et = turned(1, ebuf[...].reshape(2 * ROWS, D))
        wcross[...] = mm(et, kv[...].reshape(2 * ROWS, 2 * D)).astype(BF16)
        put_wc = store(12, wcross, dwc_hbm)
        put_wc.start()
        for k in (put_out, put_dx, put_q, put_o, put_wc):
            k.wait()
        share_wc.wait_send()
        each(0, SENTENCES, lambda m: send_new(m).wait_send())
        each(0, SENTENCES, lambda m: send_old(m).wait_send())

    for k in keep:
        k.wait()


def layers(meta, x, cot, gains, w_qkv, w_out, w_up, w_down, w_cross, picks):
    V, S = pltpu.VMEM, pltpu.SemaphoreType.DMA
    rows16 = V((ROWS, D), BF16)
    rows32 = V((ROWS, D), F32)
    scratch = [
        rows16, rows16, rows16, V((8, D), F32), V((D, 3 * D), BF16), V((D, D), BF16), V((D, FF), BF16), V((FF, D), BF16),
        V((D, 2 * D), BF16), V((D, 2 * D), BF16), V((2, D, D), BF16),
        rows16, V((ROWS, 3 * D), BF16), rows16, V((SENTENCES * HEADS, SEQ, SEQ), BF16), rows32, rows16, rows16,
        V((SENTENCES, 2 * SEQ, D), BF16), V((SENTENCES, 2 * SEQ, D), BF16), V((SENTENCES, 2 * SEQ, 2 * D), BF16), rows16,
        V((SENTENCES * HEADS, 2 * SEQ, SEQ), BF16), rows32, rows16, V((ROWS, FF), BF16), V((ROWS, FF), BF16), rows16, rows16, rows16, rows32,
        V((HALF, D), F32), V((2, D, FF_BLOCK), BF16), V((2, FF_BLOCK, D), BF16),
        S((8,)), S((15,)), S((12,)), S((12,))]
    return pl.pallas_call(
        layers_kernel,
        name="layers",
        out_shape=(
            shape(ROWS, D), shape(ROWS, D, dtype=F32), shape(ROWS, D, dtype=F32), shape(ROWS, D), shape(ROWS, 3 * D), shape(ROWS, D),
            shape(SENTENCES * HEADS, SEQ, SEQ), shape(8, D, dtype=F32), shape(D, FF), shape(FF, D), shape(D, 2 * D), shape(D, 2 * D)),
        in_specs=[IN_SMEM, IN_HBM, IN_HBM, IN_VMEM] + [IN_HBM] * 6,
        out_specs=[IN_HBM] * 7 + [IN_VMEM] + [IN_HBM] * 4,
        scratch_shapes=scratch,
        compiler_params=pltpu.CompilerParams(collective_id=1, has_side_effects=True, vmem_limit_bytes=VMEM_LIMIT),
    )(meta, x, cot, gains, w_qkv, w_out, w_up, w_down, w_cross, picks)


class Copies:
    def __init__(self, send, recv):
        self.send, self.recv, self.count = send, recv, 0

    def make(self, src, dst, device):
        k = self.count
        self.count += 1
        return pltpu.make_async_remote_copy(
            src_ref=src, dst_ref=dst, send_sem=self.send.at[k], recv_sem=self.recv.at[k], device_id=device, device_id_type=MESH)


def add_rows(dst, src, count, step=16):
    def body(i):
        at = block(i, step)
        dst[at] = dst[at] + src[at]

    each(0, count // step, body)


def total_rows(*refs):
    return sum(r.astype(F32) for r in refs)


class RowGroup:
    def __init__(self, copies, mine, theirs, loads, bufs, out, sibling, first, second, across):
        self.copies, self.mine, self.theirs, self.loads, self.out = copies, mine, theirs, loads, out
        self.got, self.a, self.b, self.t, self.a2, self.b2, self.y = bufs
        self.sibling, self.plus, self.minus = sibling, *first
        self.plus2, self.minus2 = second
        self.across = across
        self.core = {r: copies.make(theirs(r), self.got.at[r], sibling) for r in (2, 1, 3, 0)}
        top, low = pl.ds(0, 48), pl.ds(48, 32)
        mk = copies.make
        self.a_p, self.a_m = mk(mine.at[2, top], self.a.at[0, top], self.plus), mk(mine.at[2, low], self.a.at[1, low], self.minus)
        self.b_p, self.b_m = mk(mine.at[1, low], self.b.at[0, low], self.plus), mk(mine.at[3, top], self.b.at[1, top], self.minus)
        self.c_p, self.c_m = mk(mine.at[1, top], self.b.at[0, top], self.plus), mk(mine.at[3, low], self.b.at[1, low], self.minus)
        top, low = pl.ds(0, 16), pl.ds(16, 16)
        t, a2, b2 = self.t, self.a2, self.b2
        self.d_p, self.d_m = mk(t.at[2, top], a2.at[0, top], self.plus2), mk(t.at[2, low], a2.at[1, low], self.minus2)
        self.e_p, self.e_m = mk(t.at[1, low], b2.at[0, low], self.plus2), mk(t.at[3, top], b2.at[1, top], self.minus2)
        self.f_p, self.f_m = mk(t.at[1, top], b2.at[0, top], self.plus2), mk(t.at[3, low], b2.at[1, low], self.minus2)
        self.last = mk(self.y.at[0], self.y.at[1], across)

    def load(self):
        for k in self.loads.values():
            k.start()

    def start(self):
        for k in self.core.values():
            k.start()

    def summed(self, r):
        if r in self.loads:
            self.loads[r].wait()
        self.core[r].wait_recv()
        add_rows(self.mine.at[r], self.got.at[r], 80)

    def first(self):
        self.summed(2)
        self.a_p.start()
        self.a_m.start()
        self.summed(1)
        self.b_p.start()
        self.summed(3)
        self.b_m.start()

    def second(self):
        top, low = pl.ds(0, 48), pl.ds(48, 32)
        self.a_p.wait_recv()
        add_rows(self.mine.at[1, top], self.a.at[0, top], 48)
        self.c_p.start()
        self.a_m.wait_recv()
        add_rows(self.mine.at[3, low], self.a.at[1, low], 32)
        self.c_m.start()
        self.summed(0)

    def third(self):
        for k in (self.b_p, self.b_m, self.c_p, self.c_m):
            k.wait_recv()
        for r in range(4):
            at = pl.ds(20 * r, 20)
            got = total_rows(self.mine[0, at], self.b[0, at], self.b[1, at])
            self.t[r] = jnp.concatenate([got, jnp.zeros((12, got.shape[1]), F32)], axis=0).astype(BF16)
        for k in (self.d_p, self.d_m, self.e_p, self.e_m):
            k.start()

    def fourth(self):
        top, low = pl.ds(0, 16), pl.ds(16, 16)
        self.d_p.wait_recv()
        add_rows(self.t.at[1, top], self.a2.at[0, top], 16)
        self.f_p.start()
        self.d_m.wait_recv()
        add_rows(self.t.at[3, low], self.a2.at[1, low], 16)
        self.f_m.start()

    def fifth(self):
        for k in (self.e_p, self.e_m, self.f_p, self.f_m):
            k.wait_recv()
        got = total_rows(self.t[0], self.b2[0], self.b2[1])
        self.y[0] = got[10:26].astype(BF16)
        self.last.start()
        self.out[...] = got[0:10]

    def sixth(self):
        self.last.wait_recv()
        self.out[...] = self.out[...] + self.y[1, 0:10].astype(F32)

    def drain(self):
        for k in (*self.core.values(), self.a_p, self.a_m, self.b_p, self.b_m, self.c_p, self.c_m,
                  self.d_p, self.d_m, self.e_p, self.e_m, self.f_p, self.f_m, self.last):
            k.wait_send()


class DownGroup:
    def __init__(self, copies, mine, theirs, loads, bufs, out, sibling, first, second, across, x, y):
        self.mine, self.loads, self.out, self.x, self.y_at = mine, loads, out, x, y
        self.got, self.a, self.b, self.a2, self.b2, self.y = bufs
        mk = copies.make
        plus, minus = first
        plus2, minus2 = second
        self.core = {r: mk(theirs(r), self.got.at[r], sibling) for r in (2, 1, 3, 0)}
        top, low = pl.ds(0, 2), pl.ds(2, 2)
        self.a_p, self.a_m = mk(mine.at[2, top], self.a.at[0, top], plus), mk(mine.at[2, low], self.a.at[1, low], minus)
        self.b_p, self.b_m = mk(mine.at[1, low], self.b.at[0, low], plus), mk(mine.at[3, top], self.b.at[1, top], minus)
        self.c_p, self.c_m = mk(mine.at[1, top], self.b.at[0, top], plus), mk(mine.at[3, low], self.b.at[1, low], minus)
        at = lambda r: (x + r) % 4
        self.at = at
        self.d_p, self.d_m = mk(mine.at[0, at(2), 0], self.a2.at[0], plus2), mk(mine.at[0, at(2), 1], self.a2.at[1], minus2)
        self.e_p, self.e_m = mk(mine.at[0, at(1), 1], self.b2.at[0, 1], plus2), mk(mine.at[0, at(3), 0], self.b2.at[1, 0], minus2)
        self.f_p, self.f_m = mk(mine.at[0, at(1), 0], self.b2.at[0, 0], plus2), mk(mine.at[0, at(3), 1], self.b2.at[1, 1], minus2)
        self.last = mk(self.y.at[0], self.y.at[1], across)

    load, start, drain = RowGroup.load, RowGroup.start, RowGroup.drain

    def add(self, dst, src, lo, count):
        def body(i):
            dst[lo + i // 2, i % 2] = dst[lo + i // 2, i % 2] + src[lo + i // 2, i % 2]

        each(0, 2 * count, body)

    def summed(self, r):
        self.loads[r].wait()
        self.core[r].wait_recv()
        self.add(self.mine.at[r], self.got.at[r], 0, 4)

    first = RowGroup.first

    def second(self):
        self.a_p.wait_recv()
        self.add(self.mine.at[1], self.a.at[0], 0, 2)
        self.c_p.start()
        self.a_m.wait_recv()
        self.add(self.mine.at[3], self.a.at[1], 2, 2)
        self.c_m.start()
        self.summed(0)

    def third(self):
        for k in (self.b_p, self.b_m, self.c_p, self.c_m):
            k.wait_recv()

        def body(i):
            p, q = i // 2, i % 2
            self.mine[0, p, q] = total_rows(self.mine[0, p, q], self.b[0, p, q], self.b[1, p, q]).astype(BF16)

        each(0, 8, body)
        for k in (self.d_p, self.d_m, self.e_p, self.e_m):
            k.start()

    def fourth(self):
        self.d_p.wait_recv()
        self.mine[0, self.at(1), 0] = self.mine[0, self.at(1), 0] + self.a2[0]
        self.f_p.start()
        self.d_m.wait_recv()
        self.mine[0, self.at(3), 1] = self.mine[0, self.at(3), 1] + self.a2[1]
        self.f_m.start()

    def fifth(self):
        for k in (self.e_p, self.e_m, self.f_p, self.f_m):
            k.wait_recv()
        full = lambda q: total_rows(self.mine[0, self.x, q], self.b2[0, q], self.b2[1, q])
        self.y[0] = full(1 - self.y_at).astype(BF16)
        self.last.start()
        self.out[...] = full(self.y_at)

    def sixth(self):
        self.last.wait_recv()
        self.out[...] = self.out[...] + self.y[1].astype(F32)


GAIN_COLS = 128
CROSS_ROWS = 16


def gradients_kernel(meta, digits, x_hbm, gain_ref, wqkv_hbm, wout_hbm, picks_hbm, dx_hbm, extra_hbm, a_hbm, qkv_hbm, o_hbm, p_hbm,
                     gsum_in, dup_hbm, ddn_hbm, dcross_hbm, dwc_hbm,
                     dstream_hbm, up_out, down_out, qkv_out, rest_out, cross_out, *scratch):
    (x, wqkv, wout, picks, dx, extra, a, qkv, o, p, dbr, d_o, dqkv, tmp, gpad, fx2, fz2, wc_out, wc_send,
     up_mine, down_mine, cross_mine, wc_mine, up_bufs, down_bufs, cross_bufs, wc_bufs, x2_bufs, z2_bufs,
     load_sem, group_sem, out_sem, send_sem, recv_sem) = scratch
    section = lax.axis_index("section")
    px, py, pz, core = place()
    partner = {"section": 1 - section, "dp": lax.axis_index("dp")}
    own = {"section": section}
    sibling = {**own, **device_at(px, py, pz, 1 - core)}
    x_ring = [{**own, **device_at((px + r) % 4, py, pz, core)} for r in (1, 3)]
    z_ring = [{**own, **device_at(px, py, (pz + r) % 4, core)} for r in (1, 3)]
    across = {**own, **device_at(px, 1 - py, pz, core)}
    barrier = pltpu.get_barrier_semaphore()
    for d in (sibling, *x_ring, *z_ring, across, partner):
        pl.semaphore_signal(barrier, inc=1, device_id=d, device_id_type=MESH)

    copies = Copies(send_sem, recv_sem)

    def local(k, src, dst):
        return pltpu.make_async_copy(src, dst, group_sem.at[k])

    def from_hbm(at, hbm, mine):
        return {r: local(at + r, hbm.at[0, r], mine.at[r]) for r in (2, 1, 3, 0)}

    up = RowGroup(copies, up_mine, lambda r: dup_hbm.at[1, r], from_hbm(0, dup_hbm, up_mine), up_bufs, up_out, sibling, x_ring, z_ring, across)
    down = DownGroup(
        copies, down_mine, lambda r: ddn_hbm.at[:, :, (pz + r) % 4, 1 - core],
        {r: local(4 + r, ddn_hbm.at[:, :, (pz + r) % 4, core], down_mine.at[r]) for r in (2, 1, 3, 0)},
        down_bufs, down_out, sibling, z_ring, x_ring, across, px, py)
    cross = RowGroup(copies, cross_mine, lambda r: dcross_hbm.at[1, r], from_hbm(8, dcross_hbm, cross_mine), cross_bufs, cross_out, sibling, x_ring, z_ring, across)
    encoded = RowGroup(copies, wc_mine, lambda r: dwc_hbm.at[1, r], from_hbm(12, dwc_hbm, wc_mine), wc_bufs, wc_out, sibling, z_ring, x_ring, across)
    late_x = RowGroup(copies, fx2, lambda r: fx2.at[4 + r], {}, x2_bufs, qkv_out, sibling, x_ring, z_ring, across)
    late_z = RowGroup(copies, fz2, lambda r: fz2.at[4 + r], {}, z2_bufs, rest_out, sibling, z_ring, x_ring, across)
    send_cross = copies.make(wc_send.at[0], wc_send.at[1], partner)

    def decoder(*steps):
        @pl.when(section == 1)
        def _():
            for step in steps:
                step()

    gets = [pltpu.make_async_copy(src, dst, load_sem.at[i]) for i, (src, dst) in enumerate((
        (dx_hbm, dx), (wout_hbm, wout), (p_hbm, p), (qkv_hbm, qkv), (o_hbm, o), (a_hbm, a), (picks_hbm, picks), (wqkv_hbm, wqkv), (x_hbm, x), (extra_hbm, extra)))]
    get_dx, get_out, get_p, get_qkv, get_o, get_a, get_picks, get_wqkv, get_x, get_extra = gets
    get_dx.start()
    get_out.start()
    up.load()
    down.load()
    decoder(cross.load, encoded.load)
    for k in gets[2:]:
        k.start()
    pl.semaphore_wait(barrier, 7)
    up.start()
    down.start()
    decoder(cross.start, encoded.start)

    gain = gain_ref[0:1]
    get_dx.wait()

    def branch(m):
        s = Sentence(meta, m)
        dbr[block(m)] = (dx[block(m)] * s.mask * s.rows()).astype(BF16)

    each(0, SENTENCES, branch)
    get_out.wait()
    tmp[...] = mm_nt(dbr[...], wout[...])
    up.first()
    down.first()
    get_p.wait()
    get_qkv.wait()

    def attention(m):
        s = Sentence(meta, m)
        rows = block(m)
        d_o[rows] = (tmp[rows] * s.heads).astype(BF16)
        dq, dk, dv = attend_back(
            lambda h: d_o[rows, slice(*window(h))],
            lambda h: qkv[rows, slice(*window(h))],
            lambda h: qkv[rows, D + window(h)[0] : D + window(h)[1]],
            lambda h: qkv[rows, 2 * D + window(h)[0] : 2 * D + window(h)[1]],
            lambda h: p[m * HEADS + h])
        dqkv[rows, 0:D] = dq
        dqkv[rows, D : 2 * D] = dk
        dqkv[rows, 2 * D : 3 * D] = dv

    each(0, SENTENCES, attention)
    get_a.wait()
    get_picks.wait()
    turn = lambda k, value: mm_nt(picks[k], value).astype(BF16)
    fx2[...] = mm(turn(0, a[...]), dqkv[:, 0 : 2 * D]).astype(BF16).reshape(fx2.shape)
    late_x.start()
    decoder(cross.first, encoded.first)
    up.second()
    down.second()
    get_wqkv.wait()
    tmp[...] = mm_nt(dqkv[...], wqkv[...])
    get_x.wait()
    gpad[...] = jnp.zeros_like(gpad)
    get_extra.wait()

    @pl.when(section == 1)
    def _():
        extra[...] = jnp.zeros_like(extra)

    def finish(m):
        s = Sentence(meta, m)
        rows = block(m)
        n, r = normalize(x[rows].astype(F32), s.mask, s.inv)
        dy = tmp[rows]
        gpad[0:1] += jnp.sum(dy * n, 0, keepdims=True)
        d = dx[rows] + normalize_back(dy * gain, n, r, s.mask, s.inv) + extra[rows]
        d_o[rows] = d.astype(BF16)

    get_o.wait()
    zt = turn(1, o[...])
    fz2[:, :, 0:D] = mm(zt, dbr[...]).astype(BF16).reshape(8, 80, D)
    fz2[:, :, D : 2 * D] = mm(turn(1, a[...]), dqkv[:, 2 * D : 3 * D]).astype(BF16).reshape(8, 80, D)
    each(0, SENTENCES, finish)
    put = pltpu.make_async_copy(d_o, dstream_hbm, out_sem.at[0])
    put.start()
    gpad[1:3] = gsum_in[1:3]
    gains_t = turn(1, gpad[...].astype(BF16)).astype(F32) + digits[0:1]
    fz2[:, :, 2 * D : 2 * D + GAIN_COLS] = gains_t.astype(BF16).reshape(8, 80, GAIN_COLS)
    late_z.start()
    decoder(cross.second, encoded.second)
    late_x.first()
    late_z.first()
    up.third()
    down.third()
    decoder(cross.third, encoded.third)
    late_x.second()
    late_z.second()
    up.fourth()
    down.fourth()
    decoder(cross.fourth, encoded.fourth)
    late_x.third()
    late_z.third()
    up.fifth()
    down.fifth()
    decoder(cross.fifth, encoded.fifth)
    late_x.fourth()
    late_z.fourth()
    up.sixth()
    down.sixth()

    @pl.when(section == 1)
    def _():
        cross.sixth()
        encoded.sixth()
        wc_send[0, 0:10] = wc_out[...]
        send_cross.start()

    late_x.fifth()
    late_z.fifth()
    late_x.sixth()
    late_z.sixth()

    @pl.when(section == 0)
    def _():
        send_cross.wait_recv()
        cross_out[...] = wc_send[1, 0:10]

    for group in (up, down, late_x, late_z):
        group.drain()
    decoder(cross.drain, encoded.drain, send_cross.wait_send)
    put.wait()


def row_bufs(n):
    V = pltpu.VMEM
    return [V((4, 80, n), BF16), V((2, 80, n), BF16), V((2, 80, n), BF16), V((4, 32, n), BF16), V((2, 32, n), BF16), V((2, 32, n), BF16), V((2, 16, n), BF16)]


def gradients(meta, digits, x, gains, w_qkv, w_out, picks, dx, extra, a, qkv, o, p, gsum, dup, ddn, dcross, dwc):
    V, S = pltpu.VMEM, pltpu.SemaphoreType.DMA
    rows16, rows32 = V((ROWS, D), BF16), V((ROWS, D), F32)
    late = 2 * D + GAIN_COLS
    scratch = [
        rows16, V((D, 3 * D), BF16), V((D, D), BF16), V((2, D, D), BF16), rows32, rows32, rows16, V((ROWS, 3 * D), BF16), rows16,
        V((SENTENCES * HEADS, SEQ, SEQ), BF16), rows16, rows16, V((ROWS, 3 * D), BF16), rows32, V((GAIN_COLS, D), F32),
        V((8, 80, 2 * D), BF16), V((8, 80, late), BF16), V((10, 2 * D), F32), V((2, CROSS_ROWS, 2 * D), F32),
        V((4, 80, FF), BF16), V((4, 4, 2, 48, D), BF16), V((4, 80, 2 * D), BF16), V((4, 80, 2 * D), BF16),
        row_bufs(FF),
        [V((4, 4, 2, 48, D), BF16), V((2, 4, 2, 48, D), BF16), V((2, 4, 2, 48, D), BF16), V((2, 48, D), BF16), V((2, 2, 48, D), BF16), V((2, 48, D), BF16)],
        row_bufs(2 * D), row_bufs(2 * D), row_bufs(2 * D), row_bufs(late),
        S((10,)), S((16,)), S((1,)), S((103,)), S((103,))]
    f32 = functools.partial(shape, dtype=F32)
    return pl.pallas_call(
        gradients_kernel,
        name="gradients",
        out_shape=(shape(ROWS, D), f32(10, FF), f32(48, D), f32(10, 2 * D), f32(10, late), f32(10, 2 * D)),
        in_specs=[IN_SMEM, IN_VMEM, IN_HBM, IN_VMEM] + [IN_HBM] * 9 + [IN_VMEM] + [IN_HBM] * 4,
        out_specs=[IN_HBM] + [IN_VMEM] * 5,
        scratch_shapes=scratch,
        compiler_params=pltpu.CompilerParams(collective_id=0, has_side_effects=True, vmem_limit_bytes=VMEM_LIMIT),
    )(meta, digits, x, gains, w_qkv, w_out, picks, dx, extra, a, qkv, o, p, gsum,
      dup.reshape(2, 4, 80, FF), ddn.reshape(4, 2, 4, 2, 48, D), dcross.reshape(2, 4, 80, 2 * D), dwc.reshape(2, 4, 80, 2 * D))


DIGITS = 5


def shards(stream, cotangent, lengths, pieces, configs, gains, attn_qkv, attn_out, ffn_up, ffn_down, cross_proj):
    later = lax.axis_index("section").astype(jnp.int32)
    x = stream.reshape(ROWS, D)
    cot = cotangent.reshape(ROWS, D)
    onehot = (pieces == jnp.arange(configs.shape[0], dtype=jnp.int32)[None, :]).astype(jnp.int32)
    chosen = jnp.sum(onehot[:, :, None] * configs[None], axis=1)
    lens = lengths[:, :, 0]
    own = jnp.where(later == 1, lens[1], lens[0])
    meta = jnp.stack(
        [chosen[:, 0], chosen[:, 1] * HEAD_DIM, chosen[:, 2], chosen[:, 3] * SEQ, own, lens[0], jnp.broadcast_to(later, own.shape), own], axis=1)
    counts = jnp.stack([
        jnp.sum(own), jnp.sum(own * (chosen[:, 1] == HEADS)), jnp.sum(own * (chosen[:, 2] > FF_BLOCK)), jnp.sum(own * (chosen[:, 2] > 2 * FF_BLOCK))])
    powers = 4 ** jnp.arange(DIGITS, dtype=jnp.int32)
    digits = (counts[:, None] // powers[None, :]) % 4
    digits = jnp.pad(digits.reshape(1, -1).astype(F32), ((0, 7), (3, GAIN_COLS - 3 - 4 * DIGITS)))
    feature = jnp.arange(D, dtype=jnp.int32)
    picks = jnp.stack([(relative_order(k)[:, None] == feature[None, :]).astype(BF16) for k in ("x", "z")])
    gains_in = jnp.pad(gains[0].astype(F32), ((0, 5), (0, 0)))
    w = (attn_qkv[0], attn_out[0], ffn_up[0], ffn_down[0], cross_proj[0])
    layer_out, dx, extra, a, qkv, o, p, gsum, dup, ddn, dcross, dwc = layers(meta, x, cot, gains_in, *w, picks)
    dstream, up, down, qkv_x, rest, cross = gradients(
        meta, digits, x, gains_in, w[0], w[1], picks, dx, extra, a, qkv, o, p, gsum, dup, ddn, dcross, dwc)

    sums = rest[0, 2 * D + 3 : 2 * D + 3 + 4 * DIGITS].reshape(4, DIGITS)
    totals = jnp.sum(sums * powers[None, :].astype(F32), axis=1)
    devices = lax.axis_size("dp")
    tokens_all = float(ROWS * devices)
    rates = tokens_all / (totals + float(ROWS * devices // 8))
    me = lax.axis_index("dp")
    qkv_cols = jnp.arange(3 * D, dtype=jnp.int32) % D // HEAD_DIM >= HEADS // 2
    out_count = D // devices
    out_rows = (me * out_count + jnp.arange(out_count, dtype=jnp.int32)) // HEAD_DIM >= HEADS // 2
    up_block = jnp.arange(FF, dtype=jnp.int32) // FF_BLOCK
    by_block = lambda k: jnp.where(k == 0, rates[0], jnp.where(k == 1, rates[2], rates[3]))
    down_count = FF // devices
    down_block = (me * down_count + jnp.arange(down_count, dtype=jnp.int32)) // FF_BLOCK
    qkv_grad = jnp.concatenate([qkv_x, rest[:, D : 2 * D]], axis=1) * jnp.where(qkv_cols, rates[1], rates[0])[None, :]
    out_grad = rest[:, 0:D] * jnp.where(out_rows, rates[1], rates[0])[:, None]
    up_grad = up * by_block(up_block)[None, :]
    down_grad = down * by_block(down_block)[:, None]
    gain_grad = rest[:, 2 * D : 2 * D + 3].T
    return (layer_out.reshape(stream.shape), dstream.reshape(stream.shape), gain_grad[None], qkv_grad[None], out_grad[None],
            up_grad[None], down_grad[None], cross[None])


def solution(mesh):
    in_specs = (
        P("section", None, "dp", None, None),
        P("section", None, "dp", None, None),
        P(None, None, "dp"),
        P(None, "dp"),
        P(),
        P("section", None, None),
        P("section", None, None),
        P("section", None, None),
        P("section", None, None),
        P("section", None, None),
        P("section", None, None),
    )
    out_specs = (
        P("section", None, "dp", None, None),
        P("section", None, "dp", None, None),
        P("section", None, "dp"),
        P("section", "dp", None),
        P("section", "dp", None),
        P("section", "dp", None),
        P("section", "dp", None),
        P("section", "dp", None),
    )
    return jax.shard_map(shards, mesh=mesh, in_specs=in_specs, out_specs=out_specs, check_vma=False)
```

```python
import functools

import jax
import jax.numpy as jnp
from jax import lax
from jax.experimental import pallas as pl
from jax.experimental.pallas import tpu as pltpu
from jax.sharding import PartitionSpec as P

F32, BF16 = jnp.float32, jnp.bfloat16
D, HEADS, HEAD_DIM, FF, FF_BLOCK = 640, 8, 80, 3072, 1024
SEQ, SENTENCES = 128, 4
ROWS = SEQ * SENTENCES
HALF = ROWS // 2
TILE = 512
EPSILON = 1e-05
NEGATIVE = -1e30
SCALE = HEAD_DIM ** (-0.5)
LOG2E = 1.4426950408889634
MESH = pl.DeviceIdType.MESH
VMEM_LIMIT = 63 * 1024 * 1024
NX, NY, NZ, CORES = 4, 2, 4, 2


def place():
    me = lax.axis_index("dp")
    core = me % CORES
    z = me // CORES % NZ
    y = me // (CORES * NZ) % NY
    x = me // (CORES * NZ * NY)
    return x, y, z, core


def device_at(x, y, z, core):
    return {"dp": ((x * NY + y) * NZ + z) * CORES + core}


def relative_order(x_first):
    x, y, z, core = (v.astype(F32) for v in place())
    f = lax.broadcasted_iota(jnp.int32, (1, D), 1).astype(F32)
    digit = lambda size, count: (jnp.floor((f + 0.5) / size) - count * jnp.floor((f + 0.5) / (size * count)))
    away = lambda value, count: jnp.where(value < 0, value + count, value)
    rc, rx, rz, ry = away(digit(10, 2) - core, 2), away(digit(160, 4) - x, 4), away(digit(20, 4) - z, 4), away(digit(80, 2) - y, 2)
    first, second = (rx, rz) if x_first else (rz, rx)
    return rc * 320 + first * 80 + second * 20 + ry * 10 + digit(1, 10)


def mm(a, b):
    return lax.dot_general(a, b, (((1,), (0,)), ((), ())), preferred_element_type=F32)


def mm_nt(a, b):
    return lax.dot_general(a, b, (((1,), (1,)), ((), ())), preferred_element_type=F32)


def mm_tn(a, b):
    return lax.dot_general(a, b, (((0,), (0,)), ((), ())), preferred_element_type=F32)


def block(m, size=SEQ):
    if isinstance(m, int):
        return pl.ds(m * size, size)
    return pl.ds(pl.multiple_of(m * size, size), size)


def each(lo, count, body):
    def step(i, _):
        body(lo + i)
        return 0

    lax.fori_loop(0, count, step, 0)


def normalize(v, mask, inv_width):
    centred = (v - jnp.sum(v * mask, -1, keepdims=True) * inv_width) * mask
    spread = jnp.sum(centred * centred, -1, keepdims=True) * inv_width
    inverse = lax.rsqrt(spread + EPSILON)
    return centred * inverse, inverse


def normalize_back(dn, normed, inverse, mask, inv_width):
    dn = dn * mask
    first = jnp.sum(dn, -1, keepdims=True) * inv_width
    second = jnp.sum(dn * normed, -1, keepdims=True) * inv_width
    return inverse * (dn - (first + normed * second) * mask)


def window(h):
    return HEAD_DIM * h // 128 * 128, -(-HEAD_DIM * (h + 1) // 128) * 128


def head_lanes(h):
    lo, hi = window(h)
    lanes = lax.broadcasted_iota(jnp.int32, (1, hi - lo), 1) + lo
    return ((lanes >= HEAD_DIM * h) & (lanes < HEAD_DIM * (h + 1))).astype(F32).astype(BF16)


class Tiles:
    def __init__(self):
        self.tile = {}

    def add(self, h, value):
        lo, hi = window(h)
        for j in range(lo // 128, hi // 128):
            part = value[:, j * 128 - lo : j * 128 - lo + 128]
            self.tile[j] = self.tile[j] + part if j in self.tile else part

    def whole(self):
        return jnp.concatenate([self.tile[j] for j in range(D // 128)], axis=1)


class Sentence:
    def __init__(self, scalars, m):
        lengths, pieces, configs = scalars
        piece = pieces[0, m]
        section = lax.axis_index("section")
        self.width, self.units = configs[piece, 0], configs[piece, 2]
        self.full_heads = configs[piece, 1] == HEADS
        self.outputs = configs[piece, 3]
        self.source = lengths[0, 0, m]
        self.own = lengths[section, 0, m]
        self.causal = section
        lanes = lax.broadcasted_iota(jnp.int32, (1, D), 1)
        self.mask = (lanes < self.width).astype(F32)
        self.heads = (lanes < configs[piece, 1] * HEAD_DIM).astype(F32)
        self.inv = 1.0 / self.width.astype(F32)

    def rows(self):
        return (lax.broadcasted_iota(jnp.int32, (SEQ, 1), 0) < self.own).astype(F32)

    def self_bias(self):
        k = lax.broadcasted_iota(jnp.int32, (SEQ, SEQ), 0)
        q = lax.broadcasted_iota(jnp.int32, (SEQ, SEQ), 1)
        allowed = (k < self.own) & (k <= q + (1 - self.causal) * SEQ)
        return jnp.where(allowed, 0.0, NEGATIVE)

    def cross_bias(self):
        k = lax.broadcasted_iota(jnp.int32, (2 * SEQ, 1), 0)
        allowed = (jnp.where(k < SEQ, k, k - SEQ) < self.source) & (k < self.outputs * SEQ)
        return jnp.where(allowed, 0.0, NEGATIVE)


def softmax_columns(scores, bias):
    scores = scores + bias
    exponent = jnp.exp2((scores - jnp.max(scores, 0, keepdims=True)) * (SCALE * LOG2E))
    return (exponent * (1.0 / jnp.sum(exponent, 0, keepdims=True))).astype(BF16)


def attend(query, keys, values, bias, keep):
    scores = [mm_nt(keys(h), query(h) * head_lanes(h)) for h in range(HEADS)]
    weights = [softmax_columns(s, bias) for s in scores]
    out = Tiles()
    for h in range(HEADS):
        keep(h, weights[h])
        out.add(h, mm_tn(weights[h], values(h) * head_lanes(h)))
    return out.whole()


def attend_back(d_out, query, keys, values, weights):
    d_weights = [mm_nt(values(h), d_out(h) * head_lanes(h)) for h in range(HEADS)]
    d_values = Tiles()
    for h in range(HEADS):
        d_values.add(h, mm(weights(h), d_out(h) * head_lanes(h)))
    d_values = d_values.whole().astype(BF16)
    d_scores = []
    for h in range(HEADS):
        p = weights(h).astype(F32)
        product = p * d_weights[h]
        d_scores.append((product - p * jnp.sum(product, 0, keepdims=True)).astype(BF16))
    d_keys = Tiles()
    for h in range(HEADS):
        d_keys.add(h, mm(d_scores[h], query(h) * head_lanes(h)))
    d_keys = (d_keys.whole() * SCALE).astype(BF16)
    d_query = Tiles()
    for h in range(HEADS):
        d_query.add(h, mm_tn(d_scores[h], keys(h) * head_lanes(h)))
    return (d_query.whole() * SCALE).astype(BF16), d_keys, d_values


def gelu_pair(z):
    cdf = 0.5 + 0.5 * lax.erf(z * 0.7071067811865476)
    density = jnp.exp2(z * z * (-0.5 * LOG2E)) * 0.3989422804014327
    return z * cdf, cdf + z * density


def shape(*dims, dtype=BF16):
    return jax.ShapeDtypeStruct(dims, dtype)


IN_VMEM = pl.BlockSpec(memory_space=pltpu.VMEM)
IN_SMEM = pl.BlockSpec(memory_space=pltpu.SMEM)
IN_HBM = pl.BlockSpec(memory_space=pl.ANY)


class Copies:
    def __init__(self, send, recv):
        self.send, self.recv, self.count = send, recv, 0

    def make(self, src, dst, device):
        k = self.count
        self.count += 1
        return pltpu.make_async_remote_copy(
            src_ref=src, dst_ref=dst, send_sem=self.send.at[k], recv_sem=self.recv.at[k], device_id=device, device_id_type=MESH)


def add_rows(dst, src, count, step=16):
    def body(i):
        at = block(i, step)
        dst[at] = dst[at] + src[at]

    each(0, count // step, body)


def total_rows(*refs):
    return sum(r.astype(F32) for r in refs)


class RowGroup:
    def __init__(self, copies, ref, pieces, bufs, out, sibling, ring, owners):
        self.out = out
        self.ref = ref = ref.at[:, pl.ds(0, out.shape[1])]
        self.got, self.a, self.b, self.r = bufs
        plus, minus = ring
        mk = copies.make
        self.core = [mk(ref.at[pl.ds(320, 320), cols], self.got.at[:, cols], sibling) for cols in pieces]
        rows = lambda lo, count: ref.at[pl.ds(lo, count)]
        top, low = pl.ds(0, 48), pl.ds(48, 32)
        self.a_p, self.a_m = mk(rows(160, 48), self.a.at[top], plus), mk(rows(208, 32), self.a.at[low], minus)
        self.b_p, self.b_m = mk(rows(128, 32), self.b.at[0, low], plus), mk(rows(240, 48), self.b.at[1, top], minus)
        self.c_p, self.c_m = mk(rows(80, 48), self.b.at[0, top], plus), mk(rows(288, 32), self.b.at[1, low], minus)
        self.direct = [mk(self.got.at[pl.ds(16 * k, 16)], self.r.at[k - 1], owners[k]) for k in range(1, 8)]

    def summed(self, r, count=80):
        add_rows(self.ref.at[pl.ds(80 * r, count)], self.got.at[pl.ds(80 * r, count)], count)

    def first(self):
        for k in self.core:
            k.wait_recv()
        self.summed(2)
        self.a_p.start()
        self.a_m.start()
        self.summed(1)
        self.b_p.start()
        self.summed(3)
        self.b_m.start()
        self.summed(0)

    def second(self):
        self.a_p.wait_recv()
        add_rows(self.ref.at[pl.ds(80, 48)], self.a.at[pl.ds(0, 48)], 48)
        self.c_p.start()
        self.a_m.wait_recv()
        add_rows(self.ref.at[pl.ds(288, 32)], self.a.at[pl.ds(48, 32)], 32)
        self.c_m.start()

    def third(self):
        for k in (self.b_p, self.b_m, self.c_p, self.c_m):
            k.wait_recv()
        for k in range(8):
            at = pl.ds(10 * k, 10)
            got = total_rows(self.ref[at], self.b[0, at], self.b[1, at])
            if k == 0:
                self.out[...] = got
            else:
                self.got[16 * k : 16 * k + 16] = jnp.concatenate([got, jnp.zeros((6, got.shape[1]), F32)], axis=0).astype(BF16)
                self.direct[k - 1].start()

    def fourth(self):
        for k in self.direct:
            k.wait_recv()
        self.out[...] = self.out[...] + total_rows(*(self.r[k] for k in range(7)))[0:10]

    def drain(self):
        for k in (*self.core, self.a_p, self.a_m, self.b_p, self.b_m, self.c_p, self.c_m, *self.direct):
            k.wait_send()


class DownGroup:
    def __init__(self, copies, ref, bufs, out, sibling, ring, owners, x, y, z, core):
        self.ref, self.out, self.x, self.y, self.z, self.core_at = ref, out, x, y, z, core
        self.got, self.a, self.b, self.r = bufs
        mk = copies.make
        plus, minus = ring
        self.core = [mk(ref.at[i, :, :, 1 - core], self.got.at[i], sibling) for i in range(4)]
        part = lambda lo, r: ref.at[pl.ds(lo, 2), :, (z + r) % 4, core]
        top, low = pl.ds(0, 2), pl.ds(2, 2)
        self.a_p, self.a_m = mk(part(0, 2), self.a.at[top], plus), mk(part(2, 2), self.a.at[low], minus)
        self.b_p, self.b_m = mk(part(2, 1), self.b.at[0, low], plus), mk(part(0, 3), self.b.at[1, top], minus)
        self.c_p, self.c_m = mk(part(0, 1), self.b.at[0, top], plus), mk(part(2, 3), self.b.at[1, low], minus)
        self.direct = [mk(ref.at[(x + k // 2) % 4, (y + k % 2) % 2, z, core], self.r.at[k - 1], owners[k]) for k in range(1, 8)]

    def add(self, r, src, lo, count):
        zr = (self.z + r) % 4

        def body(i):
            p, q = lo + i // 2, i % 2
            self.ref[p, q, zr, self.core_at] = self.ref[p, q, zr, self.core_at] + src(p, q, zr)

        each(0, 2 * count, body)

    def summed(self, r):
        self.add(r, lambda p, q, zr: self.got[p, q, zr], 0, 4)

    first = RowGroup.first

    def second(self):
        self.a_p.wait_recv()
        self.add(1, lambda p, q, zr: self.a[p, q], 0, 2)
        self.c_p.start()
        self.a_m.wait_recv()
        self.add(3, lambda p, q, zr: self.a[p, q], 2, 2)
        self.c_m.start()

    def third(self):
        for k in (self.b_p, self.b_m, self.c_p, self.c_m):
            k.wait_recv()
        z, core = self.z, self.core_at
        for k in range(8):
            p, q = (self.x + k // 2) % 4, (self.y + k % 2) % 2
            got = total_rows(self.ref[p, q, z, core], self.b[0, p, q], self.b[1, p, q])
            if k == 0:
                self.out[...] = got
            else:
                self.ref[p, q, z, core] = got.astype(BF16)
                self.direct[k - 1].start()

    def fourth(self):
        for k in self.direct:
            k.wait_recv()
        self.out[...] = self.out[...] + total_rows(*(self.r[k] for k in range(7)))

    drain = RowGroup.drain


GAIN_COLS = 128
REST = 2 * D + GAIN_COLS
DIGITS = 5


def model_kernel(lengths, pieces, configs, x_hbm, cot_hbm, gain_in, wqkv_hbm, wout_hbm, wup_hbm, wdn_hbm, wcross_hbm,
                 out_hbm, dstream_hbm, up_out, down_out, qkv_out, rest_out, cross_out, *scratch):
    (x, xenc, gains, genc, wqkv, wout, wup, wdn6, wcross, wc, picks, a, qkv, o, p, x1, c, qc, ebuf, sbuf, kv, oc, pc, mid, b, u, g, dbr, dbrc,
     dx, tmp, d_o, gsum, gpad, wc_out, wc_send, up_bufs, down_bufs, cross_bufs, wc_bufs, x2_bufs, z2_bufs,
     load_sem, out_sem, send_sem, recv_sem) = scratch
    scalars = (lengths, pieces, configs)
    wdn = wdn6.reshape(FF, D)
    lo = xenc
    section = lax.axis_index("section")
    px, py, pz, core = place()
    own = {"section": section}
    partner = {"section": 1 - section, "dp": lax.axis_index("dp")}
    beyond = {"section": 1 - section, **device_at(px, 1 - py, pz, core)}
    sibling = {**own, **device_at(px, py, pz, 1 - core)}
    z_plane = [{**own, **device_at(px, (py + k % 2) % 2, (pz + k // 2) % 4, core)} for k in range(8)]
    x_plane = [{**own, **device_at((px + k // 2) % 4, (py + k % 2) % 2, pz, core)} for k in range(8)]
    x_ring, z_ring = (x_plane[2], x_plane[6]), (z_plane[2], z_plane[6])
    barrier = pltpu.get_barrier_semaphore()
    others = [partner, beyond, sibling, *z_plane[1:], *x_plane[2:]]
    for d in others:
        pl.semaphore_signal(barrier, inc=1, device_id=d, device_id_type=MESH)

    def load(k, src, dst):
        return pltpu.make_async_copy(src, dst, load_sem.at[k])

    get_x, get_qkv, get_out = load(0, x_hbm, x), load(1, wqkv_hbm, wqkv), load(2, wout_hbm, wout)
    get_up, get_dn, get_cross, get_cot = load(3, wup_hbm, wup), load(4, wdn_hbm, wdn6), load(5, wcross_hbm, wcross), load(6, cot_hbm, dbr)
    get_x.start()
    get_qkv.start()
    put_out = pltpu.make_async_copy(lo, out_hbm, out_sem.at[0])
    put_stream = pltpu.make_async_copy(b, dstream_hbm, out_sem.at[1])
    gains[0:3] = gain_in[...].astype(F32)
    gain = [gains[i : i + 1] for i in range(3)]
    gsum[...] = jnp.zeros_like(gsum)

    copies = Copies(send_sem, recv_sem)
    remote = copies.make
    part = pl.ds(pl.multiple_of(core * 320, 320), 320)
    send_x = remote(x_hbm, xenc, partner)
    send_gain = remote(gains, genc, partner)
    send_wc = remote(wcross_hbm.at[part], wc.at[part], beyond)
    share_wc = remote(wc.at[part], wc.at[part], sibling)
    first_new = copies.count
    copies.count += 2 * SENTENCES

    def send_new(m):
        return pltpu.make_async_remote_copy(
            src_ref=sbuf.at[m, pl.ds(0, SEQ)], dst_ref=ebuf.at[m, pl.ds(0, SEQ)], send_sem=send_sem.at[first_new + m],
            recv_sem=recv_sem.at[first_new + m], device_id=partner, device_id_type=MESH)

    def send_old(m):
        k = first_new + SENTENCES + m
        return pltpu.make_async_remote_copy(
            src_ref=sbuf.at[m, pl.ds(SEQ, SEQ)], dst_ref=ebuf.at[m, pl.ds(SEQ, SEQ)], send_sem=send_sem.at[k],
            recv_sem=recv_sem.at[k], device_id=partner, device_id_type=MESH)

    whole = [slice(None)]
    thirds = [pl.ds(t * FF_BLOCK, FF_BLOCK) for t in range(3)]
    up = RowGroup(copies, wup, thirds, up_bufs, up_out, sibling, x_ring, z_plane)
    down = DownGroup(copies, wdn6, down_bufs, down_out, sibling, z_ring, x_plane, px, py, pz, core)
    cross = RowGroup(copies, wcross, whole, cross_bufs, cross_out, sibling, x_ring, z_plane)
    encoded = RowGroup(copies, wc, whole, wc_bufs, wc_out, sibling, z_ring, x_plane)
    late_x = RowGroup(copies, kv, [pl.ds(0, 2 * D)], x2_bufs, qkv_out, sibling, x_ring, z_plane)
    late_z = RowGroup(copies, u, [pl.ds(0, REST)], z2_bufs, rest_out, sibling, z_ring, x_plane)
    send_cross = remote(wc_send.at[0], wc_send.at[1], partner)

    def decoder(*steps):
        @pl.when(section == 1)
        def _():
            for step in steps:
                step()

    get_x.wait()

    def norm_x(m):
        s = Sentence(scalars, m)
        a[block(m)] = (normalize(x[block(m)].astype(F32), s.mask, s.inv)[0] * gain[0]).astype(BF16)

    each(0, SENTENCES, norm_x)
    pl.semaphore_wait(barrier, len(others))

    @pl.when(section == 0)
    def _():
        send_gain.start()
        send_x.start()
        send_wc.start()

    get_qkv.wait()
    for k in (get_out, get_up, get_dn, get_cross, get_cot):
        k.start()

    def project(j):
        qkv[:, block(j, D)] = mm(a[...], wqkv[:, block(j, D)]).astype(BF16)

    each(0, 3, project)

    def self_attention(m):
        s = Sentence(scalars, m)
        rows = block(m)

        def keep_p(h, value):
            p[m * HEADS + h] = value

        blended = attend(
            lambda h: qkv[rows, slice(*window(h))],
            lambda h: qkv[rows, D + window(h)[0] : D + window(h)[1]],
            lambda h: qkv[rows, 2 * D + window(h)[0] : 2 * D + window(h)[1]],
            s.self_bias(), keep_p)
        o[rows] = (blended * s.heads).astype(BF16)

    each(0, SENTENCES, self_attention)
    get_out.wait()
    x1[...] = mm(o[...], wout[...])

    def add_attention(m):
        s = Sentence(scalars, m)
        rows = block(m)
        x1[rows] = x[rows].astype(F32) + x1[rows] * s.mask * s.rows()

    each(0, SENTENCES, add_attention)

    def ffn_forward(half, base, g_row, finish):
        rows = block(half, HALF)

        def norm(m):
            s = Sentence(scalars, m)
            b[block(m)] = (normalize(base[block(m)], s.mask, s.inv)[0] * gain[g_row]).astype(BF16)

        each(2 * half, 2, norm)
        units = [Sentence(scalars, 2 * half + i).units for i in range(2)]
        z = mm(b[rows], wup[:, 0:TILE])
        for t in range(FF // TILE):
            after = mm(b[rows], wup[:, (t + 1) * TILE : (t + 2) * TILE]) if t + 1 < FF // TILE else None
            cols = pl.ds(t * TILE, TILE)
            for i in range(2):
                live = (t * TILE < units[i]).astype(F32)
                value, slope = gelu_pair(z[i * SEQ : (i + 1) * SEQ])
                u[pl.ds(pl.multiple_of(t // 3 * ROWS + (2 * half + i) * SEQ, SEQ), SEQ), pl.ds(t % 3 * TILE, TILE)] = (value * live).astype(BF16)
                g[block(2 * half + i), cols] = (slope * live).astype(BF16)
            z = after
        tmp[...] = mm(u[rows], wdn[0 : FF // 2]) + mm(u[pl.ds(pl.multiple_of(ROWS + half * HALF, HALF), HALF)], wdn[FF // 2 : FF])

        def result(i):
            m = 2 * half + i
            s = Sentence(scalars, m)
            value = base[block(m)] + tmp[block(i)] * s.mask * s.rows()
            lo[block(m)] = value.astype(BF16)
            finish(m, s, value)

        each(0, 2, result)

    def through_norm(half, base, g_row):
        def result(i):
            m = 2 * half + i
            s = Sentence(scalars, m)
            n, r = normalize(base[block(m)].astype(F32), s.mask, s.inv)
            dy = tmp[block(i)]
            gsum[g_row : g_row + 1] += jnp.sum(dy * n, 0, keepdims=True)
            dx[block(m)] += normalize_back(dy * gain[g_row], n, r, s.mask, s.inv)

        each(0, 2, result)

    def ffn_back(half, base, g_row):
        rows = block(half, HALF)
        for t in range(FF // TILE):
            cols = pl.ds(t * TILE, TILE)
            g[rows, cols] = (mm_nt(dbr[rows], wdn[cols]) * g[rows, cols].astype(F32)).astype(BF16)
        tmp[...] = mm_nt(g[rows], wup[...])
        through_norm(half, base, g_row)

    def branch(half, dst):
        def body(m):
            s = Sentence(scalars, m)
            dst[block(m)] = (dx[block(m)] * s.mask * s.rows()).astype(BF16)

        each(2 * half, 2, body)

    def self_back(half):
        rows = block(half, HALF)
        branch(half, dbrc)
        tmp[...] = mm_nt(dbrc[rows], wout[...])

        def attention(i):
            m = 2 * half + i
            s = Sentence(scalars, m)
            at = block(m)
            d_o[...] = (tmp[block(i)] * s.heads).astype(BF16)
            dq, dk, dv = attend_back(
                lambda h: d_o[:, slice(*window(h))],
                lambda h: qkv[at, slice(*window(h))],
                lambda h: qkv[at, D + window(h)[0] : D + window(h)[1]],
                lambda h: qkv[at, 2 * D + window(h)[0] : 2 * D + window(h)[1]],
                lambda h: p[m * HEADS + h])
            c[at] = dq
            qc[at] = dk
            oc[at] = dv

        each(0, 2, attention)
        tmp[...] = mm_nt(c[rows], wqkv[:, 0:D]) + mm_nt(qc[rows], wqkv[:, D : 2 * D]) + mm_nt(oc[rows], wqkv[:, 2 * D : 3 * D])
        through_norm(half, x, 0)

    def turned(k, value):
        return mm_nt(picks[k], value).astype(BF16)

    def product(dst, at, left, right):
        for start, width in ((0, 256), (256, 256), (512, 128)):
            dst[0:D, at + start : at + start + width] = mm(left, right[:, start : start + width]).astype(BF16)

    def make_picks():
        for k in range(2):
            spot = relative_order(k == 0)

            def fill(i):
                places = (lax.broadcasted_iota(jnp.int32, (SEQ, 1), 0) + i * SEQ).astype(F32)
                picks[k, block(i)] = (places == spot).astype(F32).astype(BF16)

            each(0, D // SEQ, fill)

    def ffn_weights():
        bt = turned(0, b[...])
        for t in range(4):
            for k in (2 * t, 2 * t + 1):
                wdn[k * 384 : k * 384 + 384] = mm_tn(u[block(k // 4, ROWS), pl.ds(k % 4 * 384, 384)], dbr[...]).astype(BF16)
            down.core[t].start()
        for t in range(3):
            for cols in (pl.ds(t * FF_BLOCK, TILE), pl.ds(t * FF_BLOCK + TILE, TILE)):
                wup[:, cols] = mm(bt, g[:, cols]).astype(BF16)
            up.core[t].start()

    @pl.when(section == 0)
    def _():
        get_up.wait()
        get_dn.wait()

        def forward(half):
            def finish(m, s, value):
                mid[block(m)] = value
                sbuf[m, 0:SEQ] = (normalize(value, s.mask, s.inv)[0] * gain[2]).astype(BF16)
                send_new(m).start()

            ffn_forward(half, x1, 1, finish)

        each(0, 2, forward)
        put_out.start()
        make_picks()
        get_cot.wait()
        get_cross.wait()

        def widen(m):
            dx[block(m)] = dbr[block(m)].astype(F32)

        each(0, SENTENCES, widen)

        def start(half):
            def body(m):
                s = Sentence(scalars, m)
                send_new(m).wait_recv()
                n, r = normalize(mid[block(m)], s.mask, s.inv)
                dy = ebuf[m, 0:SEQ].astype(F32)
                gsum[2:3] += jnp.sum(dy * n, 0, keepdims=True)
                d = dx[block(m)] + normalize_back(dy * gain[2], n, r, s.mask, s.inv)
                dx[block(m)] = d
                dbr[block(m)] = (d * s.mask * s.rows()).astype(BF16)

            each(2 * half, 2, body)

        start(0)
        ffn_back(0, x1, 1)
        self_back(0)
        start(1)
        ffn_back(1, x1, 1)
        ffn_weights()
        self_back(1)

    @pl.when(section == 1)
    def _():
        get_cross.wait()

        def norm(m):
            s = Sentence(scalars, m)
            c[block(m)] = (normalize(x1[block(m)], s.mask, s.inv)[0] * gain[1]).astype(BF16)

        each(0, SENTENCES, norm)
        qc[...] = mm(c[...], wcross[:, 0:D]).astype(BF16)
        make_picks()
        get_cot.wait()

        def start_back(m):
            s = Sentence(scalars, m)
            d = dbr[block(m)].astype(F32)
            dx[block(m)] = d
            dbr[block(m)] = (d * s.mask * s.rows()).astype(BF16)

        each(0, SENTENCES, start_back)
        send_gain.wait_recv()
        send_x.wait_recv()

        def old(m):
            s = Sentence(scalars, m)
            ebuf[m, SEQ : 2 * SEQ] = (normalize(xenc[block(m)].astype(F32), s.mask, s.inv)[0] * genc[2:3]).astype(BF16)

        each(0, SENTENCES, old)
        get_up.wait()
        get_dn.wait()
        send_wc.wait_recv()
        share_wc.start()
        share_wc.wait_recv()

        def old_kv(m):
            kv[pl.ds(pl.multiple_of(m * 2 * SEQ + SEQ, SEQ), SEQ)] = mm(ebuf[m, SEQ : 2 * SEQ], wc[...]).astype(BF16)

        each(0, SENTENCES, old_kv)

        def middle(half):
            rows = block(half, HALF)

            def new_kv(m):
                send_new(m).wait_recv()
                kv[pl.ds(pl.multiple_of(m * 2 * SEQ, SEQ), SEQ)] = mm(ebuf[m, 0:SEQ], wc[...]).astype(BF16)

            each(2 * half, 2, new_kv)

            def cross_forward(m):
                s = Sentence(scalars, m)

                def keep_p(h, value):
                    pc[m * HEADS + h] = value

                blended = attend(
                    lambda h: qc[block(m), slice(*window(h))],
                    lambda h: kv[block(m, 2 * SEQ), slice(*window(h))],
                    lambda h: kv[block(m, 2 * SEQ), D + window(h)[0] : D + window(h)[1]],
                    s.cross_bias(), keep_p)
                oc[block(m)] = (blended * s.heads).astype(BF16)

            each(2 * half, 2, cross_forward)
            tmp[...] = mm(oc[rows], wcross[:, D : 2 * D])

            def add_cross(i):
                m = 2 * half + i
                s = Sentence(scalars, m)
                mid[block(m)] = x1[block(m)] + tmp[block(i)] * s.mask * s.rows()

            each(0, 2, add_cross)
            ffn_forward(half, mid, 2, lambda m, s, value: None)
            ffn_back(half, mid, 2)
            branch(half, dbrc)
            tmp[...] = mm_nt(dbrc[rows], wcross[:, D : 2 * D])

            def cross_back(i):
                m = 2 * half + i
                s = Sentence(scalars, m)
                d_o[...] = (tmp[block(i)] * s.heads).astype(BF16)
                at = block(m, 2 * SEQ)
                dq, dk, dv = attend_back(
                    lambda h: d_o[:, slice(*window(h))],
                    lambda h: qc[block(m), slice(*window(h))],
                    lambda h: kv[at, slice(*window(h))],
                    lambda h: kv[at, D + window(h)[0] : D + window(h)[1]],
                    lambda h: pc[m * HEADS + h])
                qc[block(m)] = dq
                kv[at, 0:D] = dk
                kv[at, D : 2 * D] = dv
                sbuf[m] = mm_nt(kv[at], wc[...]).astype(BF16)
                send_new(m).start()

            each(0, 2, cross_back)

        each(0, 2, middle)
        each(0, SENTENCES, lambda m: send_old(m).start())
        put_out.start()
        for half in range(2):
            tmp[...] = mm_nt(qc[block(half, HALF)], wcross[:, 0:D])
            through_norm(half, x1, 1)
        ffn_weights()
        product(wcross, 0, turned(0, c[...]), qc)
        product(wcross, D, turned(0, oc[...]), dbrc)
        cross.core[0].start()
        share_wc.wait_send()
        et = [turned(1, ebuf[2 * i : 2 * i + 2].reshape(ROWS, D)) for i in range(2)]
        for cols in [pl.ds(256 * k, 256) for k in range(5)]:
            wc[:, cols] = (mm(et[0], kv[0:ROWS, cols]) + mm(et[1], kv[ROWS : 2 * ROWS, cols])).astype(BF16)
        encoded.core[0].start()

        each(0, 2, self_back)

    down.first()
    up.first()
    decoder(cross.first, encoded.first)
    at = turned(0, a[...])
    product(kv, 0, at, c)
    product(kv, D, at, qc)
    late_x.core[0].start()
    product(u, 0, turned(1, o[...]), dbrc)
    product(u, D, turned(1, a[...]), oc)

    @pl.when(section == 0)
    def _():
        def old(m):
            s = Sentence(scalars, m)
            send_old(m).wait_recv()
            n, r = normalize(x[block(m)].astype(F32), s.mask, s.inv)
            dy = ebuf[m, SEQ : 2 * SEQ].astype(F32)
            gsum[2:3] += jnp.sum(dy * n, 0, keepdims=True)
            dx[block(m)] += normalize_back(dy * gain[2], n, r, s.mask, s.inv)

        each(0, SENTENCES, old)

    gpad[...] = jnp.zeros_like(gpad)
    gpad[0:3] = gsum[0:3]
    counts = [jnp.int32(0)] * 4
    for m in range(SENTENCES):
        s = Sentence(scalars, m)
        for i, uses in enumerate((True, s.full_heads, s.units > FF_BLOCK, s.units > 2 * FF_BLOCK)):
            counts[i] = counts[i] + jnp.where(uses, s.own, 0)
    lane = lax.broadcasted_iota(jnp.int32, (1, GAIN_COLS), 1)
    digits = jnp.zeros((1, GAIN_COLS), F32)
    for i in range(4):
        for k in range(DIGITS):
            digits = jnp.where(lane == 3 + i * DIGITS + k, (counts[i] // 4**k % 4).astype(F32), digits)
    u[0:D, 2 * D : REST] = (turned(1, gpad[...].astype(BF16)).astype(F32) + digits).astype(BF16)
    late_z.core[0].start()
    down.second()
    up.second()
    decoder(cross.second, encoded.second)
    late_x.first()
    late_z.first()
    down.third()
    up.third()
    decoder(cross.third, encoded.third)
    late_x.second()
    late_z.second()

    def finish(m):
        b[block(m)] = dx[block(m)].astype(BF16)

    each(0, SENTENCES, finish)
    put_stream.start()
    down.fourth()
    up.fourth()

    @pl.when(section == 1)
    def _():
        cross.fourth()
        encoded.fourth()
        wc_send[0, 0:10] = wc_out[...]
        send_cross.start()

    late_x.third()
    late_z.third()
    late_x.fourth()
    late_z.fourth()

    @pl.when(section == 0)
    def _():
        send_cross.wait_recv()
        cross_out[...] = wc_send[1, 0:10]
        send_x.wait_send()
        send_gain.wait_send()
        send_wc.wait_send()
        each(0, SENTENCES, lambda m: send_new(m).wait_send())

    @pl.when(section == 1)
    def _():
        cross.drain()
        encoded.drain()
        send_cross.wait_send()
        each(0, SENTENCES, lambda m: send_new(m).wait_send())
        each(0, SENTENCES, lambda m: send_old(m).wait_send())

    for group in (up, down, late_x, late_z):
        group.drain()
    put_out.wait()
    put_stream.wait()


def model(lengths, pieces, configs, x, cot, gains, w_qkv, w_out, w_up, w_down, w_cross):
    V, S = pltpu.VMEM, pltpu.SemaphoreType.DMA
    rows16, rows32 = V((ROWS, D), BF16), V((ROWS, D), F32)

    def row_bufs(n):
        return [V((320, n), BF16), V((80, n), BF16), V((2, 80, n), BF16), V((7, 16, n), BF16)]

    scratch = [
        rows16, rows16, V((8, D), F32), V((8, D), F32), V((D, 3 * D), BF16), V((D, D), BF16), V((D, FF), BF16), V((4, 2, 4, 2, 48, D), BF16),
        V((D, 2 * D), BF16), V((D, 2 * D), BF16), V((2, D, D), BF16), rows16, V((ROWS, 3 * D), BF16), rows16, V((SENTENCES * HEADS, SEQ, SEQ), BF16),
        rows32, rows16, rows16, V((SENTENCES, 2 * SEQ, D), BF16), V((SENTENCES, 2 * SEQ, D), BF16), V((2 * ROWS, 2 * D), BF16), rows16,
        V((SENTENCES * HEADS, 2 * SEQ, SEQ), BF16), rows32, rows16, V((2 * ROWS, FF // 2), BF16), V((ROWS, FF), BF16), rows16, rows16,
        rows32, V((HALF, D), F32), V((SEQ, D), BF16), V((8, D), F32), V((GAIN_COLS, D), F32),
        V((10, 2 * D), F32), V((2, 16, 2 * D), F32),
        row_bufs(FF), [V((4, 2, 4, 48, D), BF16), V((4, 2, 48, D), BF16), V((2, 4, 2, 48, D), BF16), V((7, 48, D), BF16)],
        row_bufs(2 * D), row_bufs(2 * D), row_bufs(2 * D), row_bufs(REST),
        S((7,)), S((2,)), S((COPIES,)), S((COPIES,))]
    f32 = functools.partial(shape, dtype=F32)
    return pl.pallas_call(
        model_kernel,
        name="model",
        out_shape=(shape(ROWS, D), shape(ROWS, D), f32(10, FF), f32(48, D), f32(10, 2 * D), f32(10, REST), f32(10, 2 * D)),
        in_specs=[IN_SMEM] * 3 + [IN_HBM] * 2 + [IN_VMEM] + [IN_HBM] * 5,
        out_specs=[IN_HBM] * 2 + [IN_VMEM] * 5,
        scratch_shapes=scratch,
        compiler_params=pltpu.CompilerParams(collective_id=0, has_side_effects=True, vmem_limit_bytes=VMEM_LIMIT),
    )(lengths, pieces, configs, x, cot, gains, w_qkv, w_out, w_up, w_down.reshape(4, 2, 4, 2, 48, D), w_cross)


COPIES = 12 + 16 + 17 + 4 * 14 + 1


def finish_kernel(out_hbm, stream_hbm, up, down, qkv_x, rest, cross, out_new, stream_new, gain_new, qkv_new, wout_new, up_new, down_new, cross_new, held, sem):
    ins = [pltpu.make_async_copy(src, held.at[i], sem.at[i]) for i, src in enumerate((out_hbm, stream_hbm))]
    outs = [pltpu.make_async_copy(held.at[i], dst, sem.at[2 + i]) for i, dst in enumerate((out_new, stream_new))]
    for k in ins:
        k.start()
    devices = lax.axis_size("dp")
    me = lax.axis_index("dp")
    lane = lax.broadcasted_iota(jnp.int32, (1, GAIN_COLS), 1)
    digits = rest[0:1, 2 * D : REST]
    tokens_all = float(ROWS * devices)
    rates = []
    for i in range(4):
        total = jnp.zeros((1, 1), F32)
        for k in range(DIGITS):
            total = total + jnp.sum(jnp.where(lane == 3 + i * DIGITS + k, digits, 0.0), 1, keepdims=True) * float(4**k)
        rates.append(tokens_all / (total + tokens_all / 8))
    for k, move in zip(ins, outs):
        k.wait()
        move.start()
    halves = jnp.where(lax.broadcasted_iota(jnp.int32, (1, D), 1) >= D // 2, rates[1], rates[0])
    for r in range(10):
        row = pl.ds(r, 1)
        cross_new[r] = cross[row]
        qkv_new[r, :, 0:D] = qkv_x[row, 0:D] * halves
        qkv_new[r, :, D : 2 * D] = qkv_x[row, D : 2 * D] * halves
        qkv_new[r, :, 2 * D : 3 * D] = rest[row, D : 2 * D] * halves
        wout_new[r] = rest[row, 0:D] * jnp.where(me * 10 + r >= D // 2, rates[1], rates[0])
        for t, rate in enumerate((rates[0], rates[2], rates[3])):
            cols = slice(t * FF_BLOCK, (t + 1) * FF_BLOCK)
            up_new[r, :, cols] = up[row, cols] * rate
    unit = lax.broadcasted_iota(jnp.int32, (48, 1), 0) + me * 48
    down_new[...] = down[...] * jnp.where(unit < FF_BLOCK, rates[0], jnp.where(unit < 2 * FF_BLOCK, rates[2], rates[3]))
    gains = jnp.concatenate([rest[:, 2 * D : REST], jnp.zeros((GAIN_COLS - 10, GAIN_COLS), F32)], axis=0).T
    for r in range(3):
        gain_new[r] = gains[r : r + 1, 0:10]
    for k in outs:
        k.wait()


def finish(*results):
    f32 = functools.partial(shape, dtype=F32)
    return pl.pallas_call(
        finish_kernel,
        name="finish",
        out_shape=(shape(ROWS, D), shape(ROWS, D), f32(3, 1, 10), f32(10, 1, 3 * D), f32(10, 1, D), f32(10, 1, FF), f32(48, D), f32(10, 1, 2 * D)),
        in_specs=[IN_HBM] * 2 + [IN_VMEM] * 5,
        out_specs=[IN_HBM] * 2 + [IN_VMEM] * 6,
        scratch_shapes=[pltpu.VMEM((2, ROWS, D), BF16), pltpu.SemaphoreType.DMA((4,))],
        compiler_params=pltpu.CompilerParams(vmem_limit_bytes=VMEM_LIMIT),
    )(*results)


def shards(stream, cotangent, lengths, pieces, configs, gains, attn_qkv, attn_out, ffn_up, ffn_down, cross_proj):
    results = model(
        lengths.transpose(0, 2, 1), pieces.T, configs, stream.reshape(ROWS, D), cotangent.reshape(ROWS, D), gains[0], attn_qkv[0], attn_out[0], ffn_up[0], ffn_down[0],
        cross_proj[0])
    layer_out, stream_grad, gain, qkv, wout, up, down, cross = finish(*results)
    rows = lambda v: v.transpose(1, 0, 2)
    return (layer_out.reshape(stream.shape), stream_grad.reshape(stream.shape), rows(gain), rows(qkv), rows(wout), rows(up), down[None], rows(cross))


def solution(mesh):
    in_specs = (
        P("section", None, "dp", None, None),
        P("section", None, "dp", None, None),
        P(None, None, "dp"),
        P(None, "dp"),
        P(),
        P("section", None, None),
        P("section", None, None),
        P("section", None, None),
        P("section", None, None),
        P("section", None, None),
        P("section", None, None),
    )
    out_specs = (
        P("section", None, "dp", None, None),
        P("section", None, "dp", None, None),
        P("section", None, "dp"),
        P("section", "dp", None),
        P("section", "dp", None),
        P("section", "dp", None),
        P("section", "dp", None),
        P("section", "dp", None),
    )
    return jax.shard_map(shards, mesh=mesh, in_specs=in_specs, out_specs=out_specs, check_vma=False)
```

```python
import functools

import jax
import jax.numpy as jnp
from jax import lax
from jax.experimental import pallas as pl
from jax.experimental.pallas import tpu as pltpu
from jax.sharding import PartitionSpec as P

F32, BF16 = jnp.float32, jnp.bfloat16
D, HEADS, HEAD_DIM, FF, FF_BLOCK = 640, 8, 80, 3072, 1024
SEQ, SENTENCES = 128, 4
ROWS = SEQ * SENTENCES
HALF = ROWS // 2
TILE = 512
EPSILON = 1e-05
NEGATIVE = -1e30
SCALE = HEAD_DIM ** (-0.5)
LOG2E = 1.4426950408889634
MESH = pl.DeviceIdType.MESH
VMEM_LIMIT = 63 * 1024 * 1024
NX, NY, NZ, CORES = 4, 2, 4, 2


def place():
    me = lax.axis_index("dp")
    core = me % CORES
    z = me // CORES % NZ
    y = me // (CORES * NZ) % NY
    x = me // (CORES * NZ * NY)
    return x, y, z, core


def device_at(x, y, z, core):
    return {"dp": ((x * NY + y) * NZ + z) * CORES + core}


def relative_order(x_first):
    x, y, z, core = (v.astype(F32) for v in place())
    f = lax.broadcasted_iota(jnp.int32, (1, D), 1).astype(F32)
    digit = lambda size, count: (jnp.floor((f + 0.5) / size) - count * jnp.floor((f + 0.5) / (size * count)))
    away = lambda value, count: jnp.where(value < 0, value + count, value)
    rc, rx, rz, ry = away(digit(10, 2) - core, 2), away(digit(160, 4) - x, 4), away(digit(20, 4) - z, 4), away(digit(80, 2) - y, 2)
    first, second = (rx, rz) if x_first else (rz, rx)
    return rc * 320 + first * 80 + second * 20 + ry * 10 + digit(1, 10)


def mm(a, b):
    return lax.dot_general(a, b, (((1,), (0,)), ((), ())), preferred_element_type=F32)


def mm_nt(a, b):
    return lax.dot_general(a, b, (((1,), (1,)), ((), ())), preferred_element_type=F32)


def mm_tn(a, b):
    return lax.dot_general(a, b, (((0,), (0,)), ((), ())), preferred_element_type=F32)


def block(m, size=SEQ):
    if isinstance(m, int):
        return pl.ds(m * size, size)
    return pl.ds(pl.multiple_of(m * size, size), size)


def each(lo, count, body):
    def step(i, _):
        body(lo + i)
        return 0

    lax.fori_loop(0, count, step, 0)


def normalize(v, mask, inv_width):
    centred = (v - jnp.sum(v * mask, -1, keepdims=True) * inv_width) * mask
    spread = jnp.sum(centred * centred, -1, keepdims=True) * inv_width
    inverse = lax.rsqrt(spread + EPSILON)
    return centred * inverse, inverse


def normalize_back(dn, normed, inverse, mask, inv_width):
    dn = dn * mask
    first = jnp.sum(dn, -1, keepdims=True) * inv_width
    second = jnp.sum(dn * normed, -1, keepdims=True) * inv_width
    return inverse * (dn - (first + normed * second) * mask)


def window(h):
    return HEAD_DIM * h // 128 * 128, -(-HEAD_DIM * (h + 1) // 128) * 128


class Tiles:
    def __init__(self):
        self.tile = {}

    def add(self, h, value):
        lo, hi = window(h)
        for j in range(lo // 128, hi // 128):
            part = value[:, j * 128 - lo : j * 128 - lo + 128]
            self.tile[j] = self.tile[j] + part if j in self.tile else part

    def whole(self):
        return jnp.concatenate([self.tile[j] for j in range(D // 128)], axis=1)


class Sentence:
    def __init__(self, scalars, m):
        lengths, pieces, configs = scalars
        piece = pieces[0, m]
        section = lax.axis_index("section")
        self.width, self.units = configs[piece, 0], configs[piece, 2]
        self.full_heads = configs[piece, 1] == HEADS
        self.outputs = configs[piece, 3]
        self.source = lengths[0, 0, m]
        self.own = lengths[section, 0, m]
        self.causal = section
        lanes = lax.broadcasted_iota(jnp.int32, (1, D), 1)
        self.mask = (lanes < self.width).astype(F32)
        self.heads = (lanes < configs[piece, 1] * HEAD_DIM).astype(F32)
        self.inv = 1.0 / self.width.astype(F32)

    def rows(self):
        return (lax.broadcasted_iota(jnp.int32, (SEQ, 1), 0) < self.own).astype(F32)

    def self_bias(self):
        k = lax.broadcasted_iota(jnp.int32, (SEQ, SEQ), 0)
        q = lax.broadcasted_iota(jnp.int32, (SEQ, SEQ), 1)
        allowed = (k < self.own) & (k <= q + (1 - self.causal) * SEQ)
        return jnp.where(allowed, 0.0, NEGATIVE)

    def cross_bias(self):
        k = lax.broadcasted_iota(jnp.int32, (2 * SEQ, 1), 0)
        allowed = (jnp.where(k < SEQ, k, k - SEQ) < self.source) & (k < self.outputs * SEQ)
        return jnp.where(allowed, 0.0, NEGATIVE)


def softmax_columns(scores, bias):
    scores = scores + bias
    exponent = jnp.exp2((scores - jnp.max(scores, 0, keepdims=True)) * (SCALE * LOG2E))
    return (exponent * (1.0 / jnp.sum(exponent, 0, keepdims=True))).astype(BF16)


def attend(query, keys, values, bias, keep, lanes):
    scores = [mm_nt(keys(h), query(h) * lanes(h)) for h in range(HEADS)]
    weights = [softmax_columns(s, bias) for s in scores]
    out = Tiles()
    for h in range(HEADS):
        keep(h, weights[h])
        out.add(h, mm_tn(weights[h], values(h) * lanes(h)))
    return out.whole()


def attend_back(d_out, query, keys, values, weights, lanes):
    d_weights = [mm_nt(values(h), d_out(h) * lanes(h)) for h in range(HEADS)]
    d_values = Tiles()
    for h in range(HEADS):
        d_values.add(h, mm(weights(h), d_out(h) * lanes(h)))
    d_values = d_values.whole().astype(BF16)
    d_scores = []
    for h in range(HEADS):
        p = weights(h).astype(F32)
        product = p * d_weights[h]
        d_scores.append((product - p * jnp.sum(product, 0, keepdims=True)).astype(BF16))
    d_keys = Tiles()
    for h in range(HEADS):
        d_keys.add(h, mm(d_scores[h], query(h) * lanes(h)))
    d_keys = (d_keys.whole() * SCALE).astype(BF16)
    d_query = Tiles()
    for h in range(HEADS):
        d_query.add(h, mm_tn(d_scores[h], keys(h) * lanes(h)))
    return (d_query.whole() * SCALE).astype(BF16), d_keys, d_values


def gelu_pair(z):
    cdf = 0.5 + 0.5 * lax.erf(z * 0.7071067811865476)
    density = jnp.exp2(z * z * (-0.5 * LOG2E)) * 0.3989422804014327
    return z * cdf, cdf + z * density


def shape(*dims, dtype=BF16):
    return jax.ShapeDtypeStruct(dims, dtype)


IN_VMEM = pl.BlockSpec(memory_space=pltpu.VMEM)
IN_SMEM = pl.BlockSpec(memory_space=pltpu.SMEM)
IN_HBM = pl.BlockSpec(memory_space=pl.ANY)


class Copies:
    def __init__(self, send, recv):
        self.send, self.recv, self.count = send, recv, 0

    def make(self, src, dst, device):
        k = self.count
        self.count += 1
        return pltpu.make_async_remote_copy(
            src_ref=src, dst_ref=dst, send_sem=self.send.at[k], recv_sem=self.recv.at[k], device_id=device, device_id_type=MESH)


def add_rows(dst, src, count, step=16):
    def body(i):
        at = block(i, step)
        dst[at] = dst[at] + src[at]

    each(0, count // step, body)


def total_rows(*refs):
    return sum(r.astype(F32) for r in refs)


class RowGroup:
    def __init__(self, copies, ref, pieces, bufs, out, sibling, ring, owners):
        self.out = out
        self.ref = ref = ref.at[:, pl.ds(0, out.shape[1])]
        self.got, self.a, self.b, self.r = bufs
        plus, minus = ring
        mk = copies.make
        self.core = [mk(ref.at[pl.ds(320, 320), cols], self.got.at[:, cols], sibling) for cols in pieces]
        rows = lambda lo, count: ref.at[pl.ds(lo, count)]
        top, low = pl.ds(0, 48), pl.ds(48, 32)
        self.a_p, self.a_m = mk(rows(160, 48), self.a.at[top], plus), mk(rows(208, 32), self.a.at[low], minus)
        self.b_p, self.b_m = mk(rows(128, 32), self.b.at[0, low], plus), mk(rows(240, 48), self.b.at[1, top], minus)
        self.c_p, self.c_m = mk(rows(80, 48), self.b.at[0, top], plus), mk(rows(288, 32), self.b.at[1, low], minus)
        self.direct = [mk(self.got.at[pl.ds(16 * k, 16)], self.r.at[k - 1], owners[k]) for k in range(1, 8)]

    def summed(self, r, count=80):
        add_rows(self.ref.at[pl.ds(80 * r, count)], self.got.at[pl.ds(80 * r, count)], count)

    def first(self):
        for k in self.core:
            k.wait_recv()
        self.summed(2)
        self.a_p.start()
        self.a_m.start()
        self.summed(1)
        self.b_p.start()
        self.summed(3)
        self.b_m.start()
        self.summed(0)

    def second(self):
        self.a_p.wait_recv()
        add_rows(self.ref.at[pl.ds(80, 48)], self.a.at[pl.ds(0, 48)], 48)
        self.c_p.start()
        self.a_m.wait_recv()
        add_rows(self.ref.at[pl.ds(288, 32)], self.a.at[pl.ds(48, 32)], 32)
        self.c_m.start()

    def third(self):
        for k in (self.b_p, self.b_m, self.c_p, self.c_m):
            k.wait_recv()
        for k in range(8):
            at = pl.ds(10 * k, 10)
            got = total_rows(self.ref[at], self.b[0, at], self.b[1, at])
            if k == 0:
                self.out[...] = got
            else:
                self.got[16 * k : 16 * k + 16] = jnp.concatenate([got, jnp.zeros((6, got.shape[1]), F32)], axis=0).astype(BF16)
                self.direct[k - 1].start()

    def fourth(self):
        for k in self.direct:
            k.wait_recv()
        self.out[...] = self.out[...] + total_rows(*(self.r[k] for k in range(7)))[0:10]

    def drain(self):
        for k in (*self.core, self.a_p, self.a_m, self.b_p, self.b_m, self.c_p, self.c_m, *self.direct):
            k.wait_send()


class DownGroup:
    def __init__(self, copies, ref, bufs, out, sibling, ring, owners, x, y, z, core):
        self.ref, self.out, self.x, self.y, self.z, self.core_at = ref, out, x, y, z, core
        self.got, self.a, self.b, self.r = bufs
        mk = copies.make
        plus, minus = ring
        self.core = [mk(ref.at[i, :, :, 1 - core], self.got.at[i], sibling) for i in range(4)]
        part = lambda lo, r: ref.at[pl.ds(lo, 2), :, (z + r) % 4, core]
        top, low = pl.ds(0, 2), pl.ds(2, 2)
        self.a_p, self.a_m = mk(part(0, 2), self.a.at[top], plus), mk(part(2, 2), self.a.at[low], minus)
        self.b_p, self.b_m = mk(part(2, 1), self.b.at[0, low], plus), mk(part(0, 3), self.b.at[1, top], minus)
        self.c_p, self.c_m = mk(part(0, 1), self.b.at[0, top], plus), mk(part(2, 3), self.b.at[1, low], minus)
        self.direct = [mk(ref.at[(x + k // 2) % 4, (y + k % 2) % 2, z, core], self.r.at[k - 1], owners[k]) for k in range(1, 8)]

    def add(self, r, src, lo, count):
        zr = (self.z + r) % 4

        def body(i):
            p, q = lo + i // 2, i % 2
            self.ref[p, q, zr, self.core_at] = self.ref[p, q, zr, self.core_at] + src(p, q, zr)

        each(0, 2 * count, body)

    def summed(self, r):
        self.add(r, lambda p, q, zr: self.got[p, q, zr], 0, 4)

    first = RowGroup.first

    def second(self):
        self.a_p.wait_recv()
        self.add(1, lambda p, q, zr: self.a[p, q], 0, 2)
        self.c_p.start()
        self.a_m.wait_recv()
        self.add(3, lambda p, q, zr: self.a[p, q], 2, 2)
        self.c_m.start()

    def third(self):
        for k in (self.b_p, self.b_m, self.c_p, self.c_m):
            k.wait_recv()
        z, core = self.z, self.core_at
        for k in range(8):
            p, q = (self.x + k // 2) % 4, (self.y + k % 2) % 2
            got = total_rows(self.ref[p, q, z, core], self.b[0, p, q], self.b[1, p, q])
            if k == 0:
                self.out[...] = got
            else:
                self.ref[p, q, z, core] = got.astype(BF16)
                self.direct[k - 1].start()

    def fourth(self):
        for k in self.direct:
            k.wait_recv()
        self.out[...] = self.out[...] + total_rows(*(self.r[k] for k in range(7)))

    drain = RowGroup.drain


GAIN_COLS = 128
REST = 2 * D + GAIN_COLS
DIGITS = 5


def model_kernel(lengths, pieces, configs, x_hbm, cot_hbm, gain_in, wqkv_hbm, wout_hbm, wup_hbm, wdn_hbm, wcross_hbm,
                 out_hbm, dstream_hbm, up_out, down_out, qkv_out, rest_out, cross_out, *scratch):
    (x, xenc, gains, genc, wqkv, wout, wup, wdn6, wcross, wc, picks, a, qkv, o, p, x1, c, qc, ebuf, sbuf, kv, oc, pc, mid, b, u, g, dbr, dbrc,
     dx, tmp, d_o, gsum, gpad, head_rows, wc_out, wc_send, up_bufs, down_bufs, cross_bufs, wc_bufs, x2_bufs, z2_bufs,
     load_sem, out_sem, send_sem, recv_sem) = scratch
    scalars = (lengths, pieces, configs)
    wdn = wdn6.reshape(FF, D)
    lo = xenc
    section = lax.axis_index("section")
    px, py, pz, core = place()
    own = {"section": section}
    partner = {"section": 1 - section, "dp": lax.axis_index("dp")}
    beyond = {"section": 1 - section, **device_at(px, 1 - py, pz, core)}
    sibling = {**own, **device_at(px, py, pz, 1 - core)}
    z_plane = [{**own, **device_at(px, (py + k % 2) % 2, (pz + k // 2) % 4, core)} for k in range(8)]
    x_plane = [{**own, **device_at((px + k // 2) % 4, (py + k % 2) % 2, pz, core)} for k in range(8)]
    x_ring, z_ring = (x_plane[2], x_plane[6]), (z_plane[2], z_plane[6])
    barrier = pltpu.get_barrier_semaphore()
    others = [partner, beyond, sibling, *z_plane[1:], *x_plane[2:]]
    for d in others:
        pl.semaphore_signal(barrier, inc=1, device_id=d, device_id_type=MESH)

    def load(k, src, dst):
        return pltpu.make_async_copy(src, dst, load_sem.at[k])

    get_x, get_qkv, get_out = load(0, x_hbm, x), load(1, wqkv_hbm, wqkv), load(2, wout_hbm, wout)
    get_up, get_dn, get_cross, get_cot = load(3, wup_hbm, wup), load(4, wdn_hbm, wdn6), load(5, wcross_hbm, wcross), load(6, cot_hbm, dbr)
    get_x.start()
    get_qkv.start()
    put_out = pltpu.make_async_copy(lo, out_hbm, out_sem.at[0])
    put_stream = pltpu.make_async_copy(b, dstream_hbm, out_sem.at[1])
    gains[0:3] = gain_in[...].astype(F32)
    gain = lambda i: gains[i : i + 1]
    for h in range(HEADS):
        low, high = window(h)
        lanes = lax.broadcasted_iota(jnp.int32, (1, high - low), 1) + low
        head_rows[h : h + 1, 0 : high - low] = ((lanes >= HEAD_DIM * h) & (lanes < HEAD_DIM * (h + 1))).astype(F32)

    def lanes_of(h):
        return head_rows[h : h + 1, 0 : window(h)[1] - window(h)[0]].astype(BF16)

    gsum[...] = jnp.zeros_like(gsum)

    copies = Copies(send_sem, recv_sem)
    remote = copies.make
    part = pl.ds(pl.multiple_of(core * 320, 320), 320)
    send_x = remote(x_hbm, xenc, partner)
    send_gain = remote(gains, genc, partner)
    send_wc = remote(wcross_hbm.at[part], wc.at[part], beyond)
    share_wc = remote(wc.at[part], wc.at[part], sibling)
    first_new = copies.count
    copies.count += 2 * SENTENCES

    def send_new(m):
        return pltpu.make_async_remote_copy(
            src_ref=sbuf.at[m, pl.ds(0, SEQ)], dst_ref=ebuf.at[m, pl.ds(0, SEQ)], send_sem=send_sem.at[first_new + m],
            recv_sem=recv_sem.at[first_new + m], device_id=partner, device_id_type=MESH)

    def send_old(m):
        k = first_new + SENTENCES + m
        return pltpu.make_async_remote_copy(
            src_ref=sbuf.at[m, pl.ds(SEQ, SEQ)], dst_ref=ebuf.at[m, pl.ds(SEQ, SEQ)], send_sem=send_sem.at[k],
            recv_sem=recv_sem.at[k], device_id=partner, device_id_type=MESH)

    whole = [slice(None)]
    thirds = [pl.ds(t * FF_BLOCK, FF_BLOCK) for t in range(3)]
    up = RowGroup(copies, wup, thirds, up_bufs, up_out, sibling, x_ring, z_plane)
    down = DownGroup(copies, wdn6, down_bufs, down_out, sibling, z_ring, x_plane, px, py, pz, core)
    cross = RowGroup(copies, wcross, whole, cross_bufs, cross_out, sibling, x_ring, z_plane)
    encoded = RowGroup(copies, wc, whole, wc_bufs, wc_out, sibling, z_ring, x_plane)
    late_x = RowGroup(copies, kv, [pl.ds(0, 2 * D)], x2_bufs, qkv_out, sibling, x_ring, z_plane)
    late_z = RowGroup(copies, u, [pl.ds(0, REST)], z2_bufs, rest_out, sibling, z_ring, x_plane)
    send_cross = remote(wc_send.at[0], wc_send.at[1], partner)

    def decoder(*steps):
        @pl.when(section == 1)
        def _():
            for step in steps:
                step()

    get_x.wait()

    def norm_x(m):
        s = Sentence(scalars, m)
        a[block(m)] = (normalize(x[block(m)].astype(F32), s.mask, s.inv)[0] * gain(0)).astype(BF16)

    each(0, SENTENCES, norm_x)
    pl.semaphore_wait(barrier, len(others))

    @pl.when(section == 0)
    def _():
        send_gain.start()
        send_x.start()
        send_wc.start()

    get_qkv.wait()
    for k in (get_out, get_up, get_dn, get_cross, get_cot):
        k.start()

    def project(j):
        qkv[:, block(j, D)] = mm(a[...], wqkv[:, block(j, D)]).astype(BF16)

    each(0, 3, project)

    def self_attention(m):
        s = Sentence(scalars, m)
        rows = block(m)

        def keep_p(h, value):
            p[m * HEADS + h] = value

        blended = attend(
            lambda h: qkv[rows, slice(*window(h))],
            lambda h: qkv[rows, D + window(h)[0] : D + window(h)[1]],
            lambda h: qkv[rows, 2 * D + window(h)[0] : 2 * D + window(h)[1]],
            s.self_bias(), keep_p, lanes_of)
        o[rows] = (blended * s.heads).astype(BF16)

    each(0, SENTENCES, self_attention)
    get_out.wait()
    x1[...] = mm(o[...], wout[...])

    def add_attention(m):
        s = Sentence(scalars, m)
        rows = block(m)
        x1[rows] = x[rows].astype(F32) + x1[rows] * s.mask * s.rows()

    each(0, SENTENCES, add_attention)

    def ffn_forward(half, base, g_row, finish):
        rows = block(half, HALF)

        def norm(m):
            s = Sentence(scalars, m)
            b[block(m)] = (normalize(base[block(m)], s.mask, s.inv)[0] * gain(g_row)).astype(BF16)

        each(2 * half, 2, norm)
        units = [Sentence(scalars, 2 * half + i).units for i in range(2)]
        z = mm(b[rows], wup[:, 0:TILE])
        for t in range(FF // TILE):
            after = mm(b[rows], wup[:, (t + 1) * TILE : (t + 2) * TILE]) if t + 1 < FF // TILE else None
            cols = pl.ds(t * TILE, TILE)
            for i in range(2):
                live = (t * TILE < units[i]).astype(F32)
                value, slope = gelu_pair(z[i * SEQ : (i + 1) * SEQ])
                u[pl.ds(pl.multiple_of(t // 3 * ROWS + (2 * half + i) * SEQ, SEQ), SEQ), pl.ds(t % 3 * TILE, TILE)] = (value * live).astype(BF16)
                g[block(2 * half + i), cols] = (slope * live).astype(BF16)
            z = after
        tmp[...] = mm(u[rows], wdn[0 : FF // 2]) + mm(u[pl.ds(pl.multiple_of(ROWS + half * HALF, HALF), HALF)], wdn[FF // 2 : FF])

        def result(i):
            m = 2 * half + i
            s = Sentence(scalars, m)
            value = base[block(m)] + tmp[block(i)] * s.mask * s.rows()
            lo[block(m)] = value.astype(BF16)
            finish(m, s, value)

        each(0, 2, result)

    def through_norm(half, base, g_row):
        def result(i):
            m = 2 * half + i
            s = Sentence(scalars, m)
            n, r = normalize(base[block(m)].astype(F32), s.mask, s.inv)
            dy = tmp[block(i)]
            gsum[g_row : g_row + 1] += jnp.sum(dy * n, 0, keepdims=True)
            dx[block(m)] += normalize_back(dy * gain(g_row), n, r, s.mask, s.inv)

        each(0, 2, result)

    def ffn_back(half, base, g_row):
        rows = block(half, HALF)
        for t in range(FF // TILE):
            cols = pl.ds(t * TILE, TILE)
            g[rows, cols] = (mm_nt(dbr[rows], wdn[cols]) * g[rows, cols].astype(F32)).astype(BF16)
        tmp[...] = mm_nt(g[rows], wup[...])
        through_norm(half, base, g_row)

    def branch(half, dst):
        def body(m):
            s = Sentence(scalars, m)
            dst[block(m)] = (dx[block(m)] * s.mask * s.rows()).astype(BF16)

        each(2 * half, 2, body)

    def self_back(half):
        rows = block(half, HALF)
        branch(half, dbrc)
        tmp[...] = mm_nt(dbrc[rows], wout[...])

        def attention(i):
            m = 2 * half + i
            s = Sentence(scalars, m)
            at = block(m)
            d_o[...] = (tmp[block(i)] * s.heads).astype(BF16)
            dq, dk, dv = attend_back(
                lambda h: d_o[:, slice(*window(h))],
                lambda h: qkv[at, slice(*window(h))],
                lambda h: qkv[at, D + window(h)[0] : D + window(h)[1]],
                lambda h: qkv[at, 2 * D + window(h)[0] : 2 * D + window(h)[1]],
                lambda h: p[m * HEADS + h], lanes_of)
            c[at] = dq
            qc[at] = dk
            oc[at] = dv

        each(0, 2, attention)
        tmp[...] = mm_nt(c[rows], wqkv[:, 0:D]) + mm_nt(qc[rows], wqkv[:, D : 2 * D]) + mm_nt(oc[rows], wqkv[:, 2 * D : 3 * D])
        through_norm(half, x, 0)

    def turned(k, value):
        return mm_nt(picks[k], value).astype(BF16)

    def product(dst, at, left, right):
        for start, width in ((0, 256), (256, 256), (512, 128)):
            dst[0:D, at + start : at + start + width] = mm(left, right[:, start : start + width]).astype(BF16)

    def make_picks():
        for k in range(2):
            spot = relative_order(k == 0)

            def fill(i):
                places = (lax.broadcasted_iota(jnp.int32, (SEQ, 1), 0) + i * SEQ).astype(F32)
                picks[k, block(i)] = (places == spot).astype(F32).astype(BF16)

            each(0, D // SEQ, fill)

    def ffn_weights():
        bt = turned(0, b[...])
        for t in range(4):
            for k in (2 * t, 2 * t + 1):
                wdn[k * 384 : k * 384 + 384] = mm_tn(u[block(k // 4, ROWS), pl.ds(k % 4 * 384, 384)], dbr[...]).astype(BF16)
            down.core[t].start()
        for t in range(3):
            for cols in (pl.ds(t * FF_BLOCK, TILE), pl.ds(t * FF_BLOCK + TILE, TILE)):
                wup[:, cols] = mm(bt, g[:, cols]).astype(BF16)
            up.core[t].start()

    @pl.when(section == 0)
    def _():
        get_up.wait()
        get_dn.wait()

        def forward(half):
            def finish(m, s, value):
                mid[block(m)] = value
                sbuf[m, 0:SEQ] = (normalize(value, s.mask, s.inv)[0] * gain(2)).astype(BF16)
                send_new(m).start()

            ffn_forward(half, x1, 1, finish)

        each(0, 2, forward)
        put_out.start()
        make_picks()
        get_cot.wait()
        get_cross.wait()

        def widen(m):
            dx[block(m)] = dbr[block(m)].astype(F32)

        each(0, SENTENCES, widen)

    def encoder_back():
        def start(half):
            def body(m):
                s = Sentence(scalars, m)
                send_new(m).wait_recv()
                n, r = normalize(mid[block(m)], s.mask, s.inv)
                dy = ebuf[m, 0:SEQ].astype(F32)
                gsum[2:3] += jnp.sum(dy * n, 0, keepdims=True)
                d = dx[block(m)] + normalize_back(dy * gain(2), n, r, s.mask, s.inv)
                dx[block(m)] = d
                dbr[block(m)] = (d * s.mask * s.rows()).astype(BF16)

            each(2 * half, 2, body)

        def back(half):
            start(half)
            ffn_back(half, x1, 1)
            pl.when(half == 0)(lambda: self_back(half))

        each(0, 2, back)

    @pl.when(section == 1)
    def _():
        get_cross.wait()

        def norm(m):
            s = Sentence(scalars, m)
            c[block(m)] = (normalize(x1[block(m)], s.mask, s.inv)[0] * gain(1)).astype(BF16)

        each(0, SENTENCES, norm)
        qc[...] = mm(c[...], wcross[:, 0:D]).astype(BF16)
        make_picks()
        get_cot.wait()

        def start_back(m):
            s = Sentence(scalars, m)
            d = dbr[block(m)].astype(F32)
            dx[block(m)] = d
            dbr[block(m)] = (d * s.mask * s.rows()).astype(BF16)

        each(0, SENTENCES, start_back)
        send_gain.wait_recv()
        send_x.wait_recv()

        def old(m):
            s = Sentence(scalars, m)
            ebuf[m, SEQ : 2 * SEQ] = (normalize(xenc[block(m)].astype(F32), s.mask, s.inv)[0] * genc[2:3]).astype(BF16)

        each(0, SENTENCES, old)
        get_up.wait()
        get_dn.wait()
        send_wc.wait_recv()
        share_wc.start()
        share_wc.wait_recv()

        def old_kv(m):
            kv[pl.ds(pl.multiple_of(m * 2 * SEQ + SEQ, SEQ), SEQ)] = mm(ebuf[m, SEQ : 2 * SEQ], wc[...]).astype(BF16)

        each(0, SENTENCES, old_kv)

        def middle(half):
            rows = block(half, HALF)

            def new_kv(m):
                send_new(m).wait_recv()
                kv[pl.ds(pl.multiple_of(m * 2 * SEQ, SEQ), SEQ)] = mm(ebuf[m, 0:SEQ], wc[...]).astype(BF16)

            each(2 * half, 2, new_kv)

            def cross_forward(m):
                s = Sentence(scalars, m)

                def keep_p(h, value):
                    pc[m * HEADS + h] = value

                blended = attend(
                    lambda h: qc[block(m), slice(*window(h))],
                    lambda h: kv[block(m, 2 * SEQ), slice(*window(h))],
                    lambda h: kv[block(m, 2 * SEQ), D + window(h)[0] : D + window(h)[1]],
                    s.cross_bias(), keep_p, lanes_of)
                oc[block(m)] = (blended * s.heads).astype(BF16)

            each(2 * half, 2, cross_forward)
            tmp[...] = mm(oc[rows], wcross[:, D : 2 * D])

            def add_cross(i):
                m = 2 * half + i
                s = Sentence(scalars, m)
                mid[block(m)] = x1[block(m)] + tmp[block(i)] * s.mask * s.rows()

            each(0, 2, add_cross)
            ffn_forward(half, mid, 2, lambda m, s, value: None)
            ffn_back(half, mid, 2)
            branch(half, dbrc)
            tmp[...] = mm_nt(dbrc[rows], wcross[:, D : 2 * D])

            def cross_back(i):
                m = 2 * half + i
                s = Sentence(scalars, m)
                d_o[...] = (tmp[block(i)] * s.heads).astype(BF16)
                at = block(m, 2 * SEQ)
                dq, dk, dv = attend_back(
                    lambda h: d_o[:, slice(*window(h))],
                    lambda h: qc[block(m), slice(*window(h))],
                    lambda h: kv[at, slice(*window(h))],
                    lambda h: kv[at, D + window(h)[0] : D + window(h)[1]],
                    lambda h: pc[m * HEADS + h], lanes_of)
                qc[block(m)] = dq
                kv[at, 0:D] = dk
                kv[at, D : 2 * D] = dv
                sbuf[m] = mm_nt(kv[at], wc[...]).astype(BF16)
                send_new(m).start()

            each(0, 2, cross_back)

        each(0, 2, middle)
        each(0, SENTENCES, lambda m: send_old(m).start())
        put_out.start()
        for half in range(2):
            tmp[...] = mm_nt(qc[block(half, HALF)], wcross[:, 0:D])
            through_norm(half, x1, 1)

    pl.when(section == 0)(encoder_back)
    ffn_weights()
    down.first()
    up.first()

    @pl.when(section == 1)
    def _():
        product(wcross, 0, turned(0, c[...]), qc)
        product(wcross, D, turned(0, oc[...]), dbrc)
        cross.core[0].start()
        share_wc.wait_send()
        et = [turned(1, ebuf[2 * i : 2 * i + 2].reshape(ROWS, D)) for i in range(2)]
        for cols in [pl.ds(256 * k, 256) for k in range(5)]:
            wc[:, cols] = (mm(et[0], kv[0:ROWS, cols]) + mm(et[1], kv[ROWS : 2 * ROWS, cols])).astype(BF16)
        encoded.core[0].start()
        down.second()
        up.second()
        cross.first()
        encoded.first()

    each(1 - section, 1 + section, self_back)

    @pl.when(section == 0)
    def _():
        down.second()
        up.second()

    at = turned(0, a[...])
    product(kv, 0, at, c)
    product(kv, D, at, qc)
    late_x.core[0].start()
    product(u, 0, turned(1, o[...]), dbrc)
    product(u, D, turned(1, a[...]), oc)
    decoder(cross.second, encoded.second)
    late_x.first()

    @pl.when(section == 0)
    def _():
        def old(m):
            s = Sentence(scalars, m)
            send_old(m).wait_recv()
            n, r = normalize(x[block(m)].astype(F32), s.mask, s.inv)
            dy = ebuf[m, SEQ : 2 * SEQ].astype(F32)
            gsum[2:3] += jnp.sum(dy * n, 0, keepdims=True)
            dx[block(m)] += normalize_back(dy * gain(2), n, r, s.mask, s.inv)

        each(0, SENTENCES, old)

    gpad[...] = jnp.zeros_like(gpad)
    gpad[0:3] = gsum[0:3]
    counts = [jnp.int32(0)] * 4
    for m in range(SENTENCES):
        s = Sentence(scalars, m)
        for i, uses in enumerate((True, s.full_heads, s.units > FF_BLOCK, s.units > 2 * FF_BLOCK)):
            counts[i] = counts[i] + jnp.where(uses, s.own, 0)
    lane = lax.broadcasted_iota(jnp.int32, (1, GAIN_COLS), 1)
    digits = jnp.zeros((1, GAIN_COLS), F32)
    for i in range(4):
        for k in range(DIGITS):
            digits = jnp.where(lane == 3 + i * DIGITS + k, (counts[i] // 4**k % 4).astype(F32), digits)
    u[0:D, 2 * D : REST] = (turned(1, gpad[...].astype(BF16)).astype(F32) + digits).astype(BF16)
    late_z.core[0].start()
    down.third()
    up.third()
    late_z.first()
    late_x.second()
    decoder(cross.third, encoded.third)
    late_z.second()

    def finish(m):
        b[block(m)] = dx[block(m)].astype(BF16)

    each(0, SENTENCES, finish)
    put_stream.start()
    late_x.third()
    late_z.third()
    down.fourth()
    up.fourth()

    @pl.when(section == 1)
    def _():
        encoded.fourth()
        wc_send[0, 0:10] = wc_out[...]
        send_cross.start()
        cross.fourth()

    late_x.fourth()
    late_z.fourth()

    @pl.when(section == 0)
    def _():
        send_cross.wait_recv()
        cross_out[...] = wc_send[1, 0:10]
        send_x.wait_send()
        send_gain.wait_send()
        send_wc.wait_send()
        each(0, SENTENCES, lambda m: send_new(m).wait_send())

    @pl.when(section == 1)
    def _():
        cross.drain()
        encoded.drain()
        send_cross.wait_send()
        each(0, SENTENCES, lambda m: send_new(m).wait_send())
        each(0, SENTENCES, lambda m: send_old(m).wait_send())

    for group in (up, down, late_x, late_z):
        group.drain()
    put_out.wait()
    put_stream.wait()


def model(lengths, pieces, configs, x, cot, gains, w_qkv, w_out, w_up, w_down, w_cross):
    V, S = pltpu.VMEM, pltpu.SemaphoreType.DMA
    rows16, rows32 = V((ROWS, D), BF16), V((ROWS, D), F32)

    def row_bufs(n):
        return [V((320, n), BF16), V((80, n), BF16), V((2, 80, n), BF16), V((7, 16, n), BF16)]

    scratch = [
        rows16, rows16, V((8, D), F32), V((8, D), F32), V((D, 3 * D), BF16), V((D, D), BF16), V((D, FF), BF16), V((4, 2, 4, 2, 48, D), BF16),
        V((D, 2 * D), BF16), V((D, 2 * D), BF16), V((2, D, D), BF16), rows16, V((ROWS, 3 * D), BF16), rows16, V((SENTENCES * HEADS, SEQ, SEQ), BF16),
        rows32, rows16, rows16, V((SENTENCES, 2 * SEQ, D), BF16), V((SENTENCES, 2 * SEQ, D), BF16), V((2 * ROWS, 2 * D), BF16), rows16,
        V((SENTENCES * HEADS, 2 * SEQ, SEQ), BF16), rows32, rows16, V((2 * ROWS, FF // 2), BF16), V((ROWS, FF), BF16), rows16, rows16,
        rows32, V((HALF, D), F32), V((SEQ, D), BF16), V((8, D), F32), V((GAIN_COLS, D), F32), V((HEADS, 256), F32),
        V((10, 2 * D), F32), V((2, 16, 2 * D), F32),
        row_bufs(FF), [V((4, 2, 4, 48, D), BF16), V((4, 2, 48, D), BF16), V((2, 4, 2, 48, D), BF16), V((7, 48, D), BF16)],
        row_bufs(2 * D), row_bufs(2 * D), row_bufs(2 * D), row_bufs(REST),
        S((7,)), S((2,)), S((COPIES,)), S((COPIES,))]
    f32 = functools.partial(shape, dtype=F32)
    return pl.pallas_call(
        model_kernel,
        name="model",
        out_shape=(shape(ROWS, D), shape(ROWS, D), f32(10, FF), f32(48, D), f32(10, 2 * D), f32(10, REST), f32(10, 2 * D)),
        in_specs=[IN_SMEM] * 3 + [IN_HBM] * 2 + [IN_VMEM] + [IN_HBM] * 5,
        out_specs=[IN_HBM] * 2 + [IN_VMEM] * 5,
        scratch_shapes=scratch,
        compiler_params=pltpu.CompilerParams(collective_id=0, has_side_effects=True, vmem_limit_bytes=VMEM_LIMIT),
    )(lengths, pieces, configs, x, cot, gains, w_qkv, w_out, w_up, w_down.reshape(4, 2, 4, 2, 48, D), w_cross)


COPIES = 12 + 16 + 17 + 4 * 14 + 1


def finish_kernel(out_hbm, stream_hbm, up, down, qkv_x, rest, cross, out_new, stream_new, gain_new, qkv_new, wout_new, up_new, down_new, cross_new, held, sem):
    ins = [pltpu.make_async_copy(src, held.at[i], sem.at[i]) for i, src in enumerate((out_hbm, stream_hbm))]
    outs = [pltpu.make_async_copy(held.at[i], dst, sem.at[2 + i]) for i, dst in enumerate((out_new, stream_new))]
    for k in ins:
        k.start()
    devices = lax.axis_size("dp")
    me = lax.axis_index("dp")
    lane = lax.broadcasted_iota(jnp.int32, (1, GAIN_COLS), 1)
    digits = rest[0:1, 2 * D : REST]
    tokens_all = float(ROWS * devices)
    rates = []
    for i in range(4):
        total = jnp.zeros((1, 1), F32)
        for k in range(DIGITS):
            total = total + jnp.sum(jnp.where(lane == 3 + i * DIGITS + k, digits, 0.0), 1, keepdims=True) * float(4**k)
        rates.append(tokens_all / (total + tokens_all / 8))
    for k, move in zip(ins, outs):
        k.wait()
        move.start()
    halves = jnp.where(lax.broadcasted_iota(jnp.int32, (1, D), 1) >= D // 2, rates[1], rates[0])
    for r in range(10):
        row = pl.ds(r, 1)
        cross_new[r] = cross[row]
        qkv_new[r, :, 0:D] = qkv_x[row, 0:D] * halves
        qkv_new[r, :, D : 2 * D] = qkv_x[row, D : 2 * D] * halves
        qkv_new[r, :, 2 * D : 3 * D] = rest[row, D : 2 * D] * halves
        wout_new[r] = rest[row, 0:D] * jnp.where(me * 10 + r >= D // 2, rates[1], rates[0])
        for t, rate in enumerate((rates[0], rates[2], rates[3])):
            cols = slice(t * FF_BLOCK, (t + 1) * FF_BLOCK)
            up_new[r, :, cols] = up[row, cols] * rate
    unit = lax.broadcasted_iota(jnp.int32, (48, 1), 0) + me * 48
    down_new[...] = down[...] * jnp.where(unit < FF_BLOCK, rates[0], jnp.where(unit < 2 * FF_BLOCK, rates[2], rates[3]))
    gains = jnp.concatenate([rest[:, 2 * D : REST], jnp.zeros((GAIN_COLS - 10, GAIN_COLS), F32)], axis=0).T
    for r in range(3):
        gain_new[r] = gains[r : r + 1, 0:10]
    for k in outs:
        k.wait()


def finish(*results):
    f32 = functools.partial(shape, dtype=F32)
    return pl.pallas_call(
        finish_kernel,
        name="finish",
        out_shape=(shape(ROWS, D), shape(ROWS, D), f32(3, 1, 10), f32(10, 1, 3 * D), f32(10, 1, D), f32(10, 1, FF), f32(48, D), f32(10, 1, 2 * D)),
        in_specs=[IN_HBM] * 2 + [IN_VMEM] * 5,
        out_specs=[IN_HBM] * 2 + [IN_VMEM] * 6,
        scratch_shapes=[pltpu.VMEM((2, ROWS, D), BF16), pltpu.SemaphoreType.DMA((4,))],
        compiler_params=pltpu.CompilerParams(vmem_limit_bytes=VMEM_LIMIT),
    )(*results)


def shards(stream, cotangent, lengths, pieces, configs, gains, attn_qkv, attn_out, ffn_up, ffn_down, cross_proj):
    results = model(
        lengths.transpose(0, 2, 1), pieces.T, configs, stream.reshape(ROWS, D), cotangent.reshape(ROWS, D), gains[0], attn_qkv[0], attn_out[0], ffn_up[0], ffn_down[0],
        cross_proj[0])
    layer_out, stream_grad, gain, qkv, wout, up, down, cross = finish(*results)
    rows = lambda v: v.transpose(1, 0, 2)
    return (layer_out.reshape(stream.shape), stream_grad.reshape(stream.shape), rows(gain), rows(qkv), rows(wout), rows(up), down[None], rows(cross))


def solution(mesh):
    in_specs = (
        P("section", None, "dp", None, None),
        P("section", None, "dp", None, None),
        P(None, None, "dp"),
        P(None, "dp"),
        P(),
        P("section", None, None),
        P("section", None, None),
        P("section", None, None),
        P("section", None, None),
        P("section", None, None),
        P("section", None, None),
    )
    out_specs = (
        P("section", None, "dp", None, None),
        P("section", None, "dp", None, None),
        P("section", None, "dp"),
        P("section", "dp", None),
        P("section", "dp", None),
        P("section", "dp", None),
        P("section", "dp", None),
        P("section", "dp", None),
    )
    return jax.shard_map(shards, mesh=mesh, in_specs=in_specs, out_specs=out_specs, check_vma=False)
```

```python
import functools

import jax
import jax.numpy as jnp
from jax import lax
from jax.experimental import pallas as pl
from jax.experimental.pallas import tpu as pltpu
from jax.sharding import PartitionSpec as P

F32, BF16 = jnp.float32, jnp.bfloat16
D, HEADS, HEAD_DIM, FF, FF_BLOCK = 640, 8, 80, 3072, 1024
SEQ, SENTENCES = 128, 4
ROWS = SEQ * SENTENCES
HALF = ROWS // 2
TILE = 512
EPSILON = 1e-05
NEGATIVE = -1e30
SCALE = HEAD_DIM ** (-0.5)
LOG2E = 1.4426950408889634
MESH = pl.DeviceIdType.MESH
VMEM_LIMIT = 63 * 1024 * 1024
NX, NY, NZ, CORES = 4, 2, 4, 2


def place():
    me = lax.axis_index("dp")
    core = me % CORES
    z = me // CORES % NZ
    y = me // (CORES * NZ) % NY
    x = me // (CORES * NZ * NY)
    return x, y, z, core


def device_at(x, y, z, core):
    return {"dp": ((x * NY + y) * NZ + z) * CORES + core}


def relative_order(x_first):
    x, y, z, core = (v.astype(F32) for v in place())
    f = lax.broadcasted_iota(jnp.int32, (1, D), 1).astype(F32)
    digit = lambda size, count: (jnp.floor((f + 0.5) / size) - count * jnp.floor((f + 0.5) / (size * count)))
    away = lambda value, count: jnp.where(value < 0, value + count, value)
    rc, rx, rz, ry = away(digit(10, 2) - core, 2), away(digit(160, 4) - x, 4), away(digit(20, 4) - z, 4), away(digit(80, 2) - y, 2)
    first, second = (rx, rz) if x_first else (rz, rx)
    return rc * 320 + first * 80 + second * 20 + ry * 10 + digit(1, 10)


def mm(a, b):
    return lax.dot_general(a, b, (((1,), (0,)), ((), ())), preferred_element_type=F32)


def mm_nt(a, b):
    return lax.dot_general(a, b, (((1,), (1,)), ((), ())), preferred_element_type=F32)


def mm_tn(a, b):
    return lax.dot_general(a, b, (((0,), (0,)), ((), ())), preferred_element_type=F32)


def block(m, size=SEQ):
    if isinstance(m, int):
        return pl.ds(m * size, size)
    return pl.ds(pl.multiple_of(m * size, size), size)


def each(lo, count, body):
    def step(i, _):
        body(lo + i)
        return 0

    lax.fori_loop(0, count, step, 0)


def normalize(v, mask, inv_width):
    centred = (v - jnp.sum(v * mask, -1, keepdims=True) * inv_width) * mask
    spread = jnp.sum(centred * centred, -1, keepdims=True) * inv_width
    inverse = lax.rsqrt(spread + EPSILON)
    return centred * inverse, inverse


def normalize_back(dn, normed, inverse, mask, inv_width):
    dn = dn * mask
    first = jnp.sum(dn, -1, keepdims=True) * inv_width
    second = jnp.sum(dn * normed, -1, keepdims=True) * inv_width
    return inverse * (dn - (first + normed * second) * mask)


def window(h):
    return HEAD_DIM * h // 128 * 128, -(-HEAD_DIM * (h + 1) // 128) * 128


class Tiles:
    def __init__(self):
        self.tile = {}

    def add(self, h, value):
        lo, hi = window(h)
        for j in range(lo // 128, hi // 128):
            part = value[:, j * 128 - lo : j * 128 - lo + 128]
            self.tile[j] = self.tile[j] + part if j in self.tile else part

    def whole(self):
        return jnp.concatenate([self.tile[j] for j in range(D // 128)], axis=1)


class Sentence:
    def __init__(self, scalars, m):
        lengths, pieces, configs = scalars
        piece = pieces[0, m]
        section = lax.axis_index("section")
        self.width, self.units = configs[piece, 0], configs[piece, 2]
        self.full_heads = configs[piece, 1] == HEADS
        self.outputs = configs[piece, 3]
        self.source = lengths[0, 0, m]
        self.own = lengths[section, 0, m]
        self.causal = section
        lanes = lax.broadcasted_iota(jnp.int32, (1, D), 1)
        self.mask = (lanes < self.width).astype(F32)
        self.heads = (lanes < configs[piece, 1] * HEAD_DIM).astype(F32)
        self.inv = 1.0 / self.width.astype(F32)

    def rows(self):
        return (lax.broadcasted_iota(jnp.int32, (SEQ, 1), 0) < self.own).astype(F32)

    def self_bias(self):
        k = lax.broadcasted_iota(jnp.int32, (SEQ, SEQ), 0)
        q = lax.broadcasted_iota(jnp.int32, (SEQ, SEQ), 1)
        allowed = (k < self.own) & (k <= q + (1 - self.causal) * SEQ)
        return jnp.where(allowed, 0.0, NEGATIVE)

    def cross_bias(self):
        k = lax.broadcasted_iota(jnp.int32, (2 * SEQ, 1), 0)
        allowed = (jnp.where(k < SEQ, k, k - SEQ) < self.source) & (k < self.outputs * SEQ)
        return jnp.where(allowed, 0.0, NEGATIVE)


def softmax_columns(scores, bias):
    scores = scores + bias
    exponent = jnp.exp2((scores - jnp.max(scores, 0, keepdims=True)) * (SCALE * LOG2E))
    return (exponent * (1.0 / jnp.sum(exponent, 0, keepdims=True))).astype(BF16)


def attend(query, keys, values, bias, keep, lanes):
    scores = [mm_nt(keys(h), query(h) * lanes(h)) for h in range(HEADS)]
    weights = [softmax_columns(s, bias) for s in scores]
    out = Tiles()
    for h in range(HEADS):
        keep(h, weights[h])
        out.add(h, mm_tn(weights[h], values(h) * lanes(h)))
    return out.whole()


def attend_back(d_out, query, keys, values, weights, lanes):
    d_weights = [mm_nt(values(h), d_out(h) * lanes(h)) for h in range(HEADS)]
    d_values = Tiles()
    for h in range(HEADS):
        d_values.add(h, mm(weights(h), d_out(h) * lanes(h)))
    d_values = d_values.whole().astype(BF16)
    d_scores = []
    for h in range(HEADS):
        p = weights(h).astype(F32)
        product = p * d_weights[h]
        d_scores.append((product - p * jnp.sum(product, 0, keepdims=True)).astype(BF16))
    d_keys = Tiles()
    for h in range(HEADS):
        d_keys.add(h, mm(d_scores[h], query(h) * lanes(h)))
    d_keys = (d_keys.whole() * SCALE).astype(BF16)
    d_query = Tiles()
    for h in range(HEADS):
        d_query.add(h, mm_tn(d_scores[h], keys(h) * lanes(h)))
    return (d_query.whole() * SCALE).astype(BF16), d_keys, d_values


def gelu_pair(z):
    cdf = 0.5 + 0.5 * lax.erf(z * 0.7071067811865476)
    density = jnp.exp2(z * z * (-0.5 * LOG2E)) * 0.3989422804014327
    return z * cdf, cdf + z * density


def shape(*dims, dtype=BF16):
    return jax.ShapeDtypeStruct(dims, dtype)


IN_VMEM = pl.BlockSpec(memory_space=pltpu.VMEM)
IN_SMEM = pl.BlockSpec(memory_space=pltpu.SMEM)
IN_HBM = pl.BlockSpec(memory_space=pl.ANY)


class Copies:
    def __init__(self, send, recv):
        self.send, self.recv, self.count = send, recv, 0

    def make(self, src, dst, device):
        k = self.count
        self.count += 1
        return pltpu.make_async_remote_copy(
            src_ref=src, dst_ref=dst, send_sem=self.send.at[k], recv_sem=self.recv.at[k], device_id=device, device_id_type=MESH)


def add_rows(dst, src, count, step=16):
    def body(i):
        at = block(i, step)
        dst[at] = dst[at] + src[at]

    each(0, count // step, body)


def total_rows(*refs):
    return sum(r.astype(F32) for r in refs)


class RowGroup:
    def __init__(self, copies, ref, pieces, bufs, out, sibling, ring, plane):
        self.out = out
        self.ref = ref = ref.at[:, pl.ds(0, out.shape[1])]
        self.got, self.a, self.b, self.r, self.tail, self.y = bufs
        self.fold = self.tail.shape[2]
        plus, minus = ring
        mk = copies.make
        self.core = [mk(ref.at[pl.ds(320, 320), cols], self.got.at[:, cols], sibling) for cols in pieces]
        rows = lambda lo, count: ref.at[pl.ds(lo, count)]
        top, low = pl.ds(0, 48), pl.ds(48, 32)
        self.a_p, self.a_m = mk(rows(160, 48), self.a.at[top], plus), mk(rows(208, 32), self.a.at[low], minus)
        self.b_p, self.b_m = mk(rows(128, 32), self.b.at[0, low], plus), mk(rows(240, 48), self.b.at[1, top], minus)
        self.c_p, self.c_m = mk(rows(80, 48), self.b.at[0, top], plus), mk(rows(288, 32), self.b.at[1, low], minus)
        self.direct = [(
            mk(self.got.at[pl.ds(16 * k, 16)], self.r.at[k - 1], plane[2 * k]),
            mk(self.got.at[pl.ds(64 + 16 * k, 16), pl.ds(0, self.fold)], self.tail.at[k - 1], plane[2 * k])) for k in range(1, 4)]
        self.last = mk(self.got.at[pl.ds(128, 16)], self.y, plane[1])

    def summed(self, r, count=80):
        add_rows(self.ref.at[pl.ds(80 * r, count)], self.got.at[pl.ds(80 * r, count)], count)

    def first(self):
        for k in self.core:
            k.wait_recv()
        self.summed(2)
        self.a_p.start()
        self.a_m.start()
        self.summed(1)
        self.b_p.start()
        self.summed(3)
        self.b_m.start()
        self.summed(0)

    def second(self):
        self.a_p.wait_recv()
        add_rows(self.ref.at[pl.ds(80, 48)], self.a.at[pl.ds(0, 48)], 48)
        self.c_p.start()
        self.a_m.wait_recv()
        add_rows(self.ref.at[pl.ds(288, 32)], self.a.at[pl.ds(48, 32)], 32)
        self.c_m.start()

    def third(self):
        for k in (self.b_p, self.b_m, self.c_p, self.c_m):
            k.wait_recv()
        n, fold = self.out.shape[1], self.fold
        for k in (1, 2, 3, 0):
            at = pl.ds(20 * k, 20)
            got = total_rows(self.ref[at], self.b[0, at], self.b[1, at])
            rest = jnp.concatenate([got[16:20], jnp.zeros((4, 4 * fold - n), F32)], axis=1) if 4 * fold > n else got[16:20]
            self.got[16 * k : 16 * k + 16] = got[0:16].astype(BF16)
            folded = jnp.concatenate([rest[:, j * fold : (j + 1) * fold] for j in range(4)], axis=0)
            self.got[64 + 16 * k : 80 + 16 * k, 0:fold] = folded.astype(BF16)
            if k > 0:
                for copy in self.direct[k - 1]:
                    copy.start()

    def fourth(self):
        for pair in self.direct:
            for copy in pair:
                copy.wait_recv()
        n, fold = self.out.shape[1], self.fold
        main = total_rows(self.got[0:16], *(self.r[k] for k in range(3)))
        folded = total_rows(self.got[64:80, 0:fold], *(self.tail[k] for k in range(3)))
        rest = jnp.concatenate([folded[4 * j : 4 * j + 4] for j in range(4)], axis=1)[:, 0:n]
        self.got[128:144] = jnp.concatenate([main[10:16], rest, jnp.zeros((6, n), F32)], axis=0).astype(BF16)
        self.last.start()
        self.out[...] = main[0:10]

    def fifth(self):
        self.last.wait_recv()
        self.out[...] = self.out[...] + self.y[0:10].astype(F32)

    def drain(self):
        for k in (*self.core, self.a_p, self.a_m, self.b_p, self.b_m, self.c_p, self.c_m, *(c for pair in self.direct for c in pair), self.last):
            k.wait_send()


class DownGroup:
    def __init__(self, copies, ref, bufs, out, sibling, ring, plane, x, y, z, core):
        self.ref, self.out, self.x, self.y, self.z, self.core_at = ref, out, x, y, z, core
        self.got, self.a, self.b, self.r, self.y_in = bufs
        mk = copies.make
        plus, minus = ring
        self.core = [mk(ref.at[i, :, :, 1 - core], self.got.at[i], sibling) for i in range(4)]
        part = lambda lo, r: ref.at[pl.ds(lo, 2), :, (z + r) % 4, core]
        top, low = pl.ds(0, 2), pl.ds(2, 2)
        self.a_p, self.a_m = mk(part(0, 2), self.a.at[top], plus), mk(part(2, 2), self.a.at[low], minus)
        self.b_p, self.b_m = mk(part(2, 1), self.b.at[0, low], plus), mk(part(0, 3), self.b.at[1, top], minus)
        self.c_p, self.c_m = mk(part(0, 1), self.b.at[0, top], plus), mk(part(2, 3), self.b.at[1, low], minus)
        self.direct = [(mk(ref.at[(x + k) % 4, :, z, core], self.r.at[k - 1], plane[2 * k]),) for k in range(1, 4)]
        self.last = mk(ref.at[x, 1 - y, z, core], self.y_in, plane[1])

    def add(self, r, src, lo, count):
        zr = (self.z + r) % 4

        def body(i):
            p, q = lo + i // 2, i % 2
            self.ref[p, q, zr, self.core_at] = self.ref[p, q, zr, self.core_at] + src(p, q, zr)

        each(0, 2 * count, body)

    def summed(self, r):
        self.add(r, lambda p, q, zr: self.got[p, q, zr], 0, 4)

    first = RowGroup.first

    def second(self):
        self.a_p.wait_recv()
        self.add(1, lambda p, q, zr: self.a[p, q], 0, 2)
        self.c_p.start()
        self.a_m.wait_recv()
        self.add(3, lambda p, q, zr: self.a[p, q], 2, 2)
        self.c_m.start()

    def third(self):
        for k in (self.b_p, self.b_m, self.c_p, self.c_m):
            k.wait_recv()
        z, core = self.z, self.core_at
        for k in (1, 2, 3, 0):
            p = (self.x + k) % 4
            for q in range(2):
                self.ref[p, q, z, core] = total_rows(self.ref[p, q, z, core], self.b[0, p, q], self.b[1, p, q]).astype(BF16)
            if k > 0:
                self.direct[k - 1][0].start()

    def fourth(self):
        for k in self.direct:
            k[0].wait_recv()
        x, y, z, core = self.x, self.y, self.z, self.core_at
        full = lambda q: total_rows(self.ref[x, q, z, core], *(self.r[k, q] for k in range(3)))
        self.ref[x, 1 - y, z, core] = full(1 - y).astype(BF16)
        self.last.start()
        self.out[...] = full(y)

    def fifth(self):
        self.last.wait_recv()
        self.out[...] = self.out[...] + self.y_in[...].astype(F32)

    drain = RowGroup.drain


GAIN_COLS = 128
REST = 2 * D + GAIN_COLS
DIGITS = 5


def model_kernel(lengths, pieces, configs, x_hbm, cot_hbm, gain_in, wqkv_hbm, wout_hbm, wup_hbm, wdn_hbm, wcross_hbm,
                 out_hbm, dstream_hbm, up_out, down_out, qkv_out, rest_out, cross_out, *scratch):
    (x, xenc, gains, genc, wqkv, wout, wup, wdn6, wcross, wc, picks, a, qkv, o, p, x1, c, qc, ebuf, sbuf, kv, oc, pc, mid, b, u, g, dbr, dbrc,
     dx, tmp, d_o, gsum, gpad, head_rows, wc_out, wc_send, up_bufs, down_bufs, cross_bufs, wc_bufs, x2_bufs, z2_bufs,
     load_sem, out_sem, send_sem, recv_sem) = scratch
    scalars = (lengths, pieces, configs)
    wdn = wdn6.reshape(FF, D)
    lo = xenc
    section = lax.axis_index("section")
    px, py, pz, core = place()
    own = {"section": section}
    partner = {"section": 1 - section, "dp": lax.axis_index("dp")}
    beyond = {"section": 1 - section, **device_at(px, 1 - py, pz, core)}
    sibling = {**own, **device_at(px, py, pz, 1 - core)}
    z_plane = [{**own, **device_at(px, (py + k % 2) % 2, (pz + k // 2) % 4, core)} for k in range(8)]
    x_plane = [{**own, **device_at((px + k // 2) % 4, (py + k % 2) % 2, pz, core)} for k in range(8)]
    x_ring, z_ring = (x_plane[2], x_plane[6]), (z_plane[2], z_plane[6])
    barrier = pltpu.get_barrier_semaphore()
    others = [partner, beyond, sibling, z_plane[1], *z_plane[2::2], *x_plane[2::2]]
    for d in others:
        pl.semaphore_signal(barrier, inc=1, device_id=d, device_id_type=MESH)

    def load(k, src, dst):
        return pltpu.make_async_copy(src, dst, load_sem.at[k])

    get_x, get_qkv, get_out = load(0, x_hbm, x), load(1, wqkv_hbm, wqkv), load(2, wout_hbm, wout)
    get_up, get_dn, get_cross, get_cot = load(3, wup_hbm, wup), load(4, wdn_hbm, wdn6), load(5, wcross_hbm, wcross), load(6, cot_hbm, dbr)
    get_x.start()
    get_qkv.start()
    put_out = pltpu.make_async_copy(lo, out_hbm, out_sem.at[0])
    put_stream = pltpu.make_async_copy(b, dstream_hbm, out_sem.at[1])
    gains[0:3] = gain_in[...].astype(F32)
    gain = lambda i: gains[i : i + 1]
    for h in range(HEADS):
        low, high = window(h)
        lanes = lax.broadcasted_iota(jnp.int32, (1, high - low), 1) + low
        head_rows[h : h + 1, 0 : high - low] = ((lanes >= HEAD_DIM * h) & (lanes < HEAD_DIM * (h + 1))).astype(F32)

    def lanes_of(h):
        return head_rows[h : h + 1, 0 : window(h)[1] - window(h)[0]].astype(BF16)

    gsum[...] = jnp.zeros_like(gsum)

    copies = Copies(send_sem, recv_sem)
    remote = copies.make
    part = pl.ds(pl.multiple_of(core * 320, 320), 320)
    far, near = pl.ds(pl.multiple_of(core * 320, 16), 272), pl.ds(pl.multiple_of(core * 320 + 272, 16), 48)
    send_gain = remote(gains, genc, partner)
    send_wc = [remote(wcross_hbm.at[far], wc.at[far], beyond), remote(wcross_hbm.at[near], wc.at[near], partner)]
    share_wc = remote(wc.at[part], wc.at[part], sibling)
    first_new = copies.count
    first_x = first_new + 2 * SENTENCES
    copies.count += 2 * SENTENCES + 2

    def send_x(half):
        rows = block(half, HALF)
        return pltpu.make_async_remote_copy(
            src_ref=x_hbm.at[rows], dst_ref=xenc.at[rows], send_sem=send_sem.at[first_x + half], recv_sem=recv_sem.at[first_x + half],
            device_id=partner, device_id_type=MESH)

    def send_new(m):
        return pltpu.make_async_remote_copy(
            src_ref=sbuf.at[m, pl.ds(0, SEQ)], dst_ref=ebuf.at[m, pl.ds(0, SEQ)], send_sem=send_sem.at[first_new + m],
            recv_sem=recv_sem.at[first_new + m], device_id=partner, device_id_type=MESH)

    def send_old(m):
        k = first_new + SENTENCES + m
        return pltpu.make_async_remote_copy(
            src_ref=sbuf.at[m, pl.ds(SEQ, SEQ)], dst_ref=ebuf.at[m, pl.ds(SEQ, SEQ)], send_sem=send_sem.at[k],
            recv_sem=recv_sem.at[k], device_id=partner, device_id_type=MESH)

    whole = [slice(None)]
    thirds = [pl.ds(t * FF_BLOCK, FF_BLOCK) for t in range(3)]
    up = RowGroup(copies, wup, thirds, up_bufs, up_out, sibling, x_ring, z_plane)
    down = DownGroup(copies, wdn6, down_bufs, down_out, sibling, z_ring, x_plane, px, py, pz, core)
    cross = RowGroup(copies, wcross, whole, cross_bufs, cross_out, sibling, x_ring, z_plane)
    encoded = RowGroup(copies, wc, whole, wc_bufs, wc_out, sibling, z_ring, x_plane)
    late_x = RowGroup(copies, kv, [pl.ds(0, 2 * D)], x2_bufs, qkv_out, sibling, x_ring, z_plane)
    late_z = RowGroup(copies, u, [pl.ds(0, REST)], z2_bufs, rest_out, sibling, z_ring, x_plane)
    send_cross = remote(wc_send.at[0], wc_send.at[1], partner)

    def decoder(*steps):
        @pl.when(section == 1)
        def _():
            for step in steps:
                step()

    get_x.wait()

    def norm_x(m):
        s = Sentence(scalars, m)
        a[block(m)] = (normalize(x[block(m)].astype(F32), s.mask, s.inv)[0] * gain(0)).astype(BF16)

    each(0, SENTENCES, norm_x)
    pl.semaphore_wait(barrier, len(others))

    @pl.when(section == 0)
    def _():
        send_gain.start()
        send_x(0).start()
        for k in send_wc:
            k.start()

    get_qkv.wait()
    for k in (get_out, get_up, get_dn, get_cross, get_cot):
        k.start()

    def project(j):
        qkv[:, block(j, D)] = mm(a[...], wqkv[:, block(j, D)]).astype(BF16)

    each(0, 3, project)

    def self_attention(m):
        s = Sentence(scalars, m)
        rows = block(m)

        def keep_p(h, value):
            p[m * HEADS + h] = value

        blended = attend(
            lambda h: qkv[rows, slice(*window(h))],
            lambda h: qkv[rows, D + window(h)[0] : D + window(h)[1]],
            lambda h: qkv[rows, 2 * D + window(h)[0] : 2 * D + window(h)[1]],
            s.self_bias(), keep_p, lanes_of)
        o[rows] = (blended * s.heads).astype(BF16)

    def add_attention(i, half):
        m = 2 * half + i
        s = Sentence(scalars, m)
        rows = block(m)
        x1[rows] = x[rows].astype(F32) + tmp[block(i)] * s.mask * s.rows()

    def ffn_forward(half, base, g_row, finish):
        rows = block(half, HALF)

        def norm(m):
            s = Sentence(scalars, m)
            b[block(m)] = (normalize(base[block(m)], s.mask, s.inv)[0] * gain(g_row)).astype(BF16)

        each(2 * half, 2, norm)
        units = [Sentence(scalars, 2 * half + i).units for i in range(2)]
        z = mm(b[rows], wup[:, 0:TILE])
        for t in range(FF // TILE):
            after = mm(b[rows], wup[:, (t + 1) * TILE : (t + 2) * TILE]) if t + 1 < FF // TILE else None
            cols = pl.ds(t * TILE, TILE)
            for i in range(2):
                live = (t * TILE < units[i]).astype(F32)
                value, slope = gelu_pair(z[i * SEQ : (i + 1) * SEQ])
                u[pl.ds(pl.multiple_of(t // 3 * ROWS + (2 * half + i) * SEQ, SEQ), SEQ), pl.ds(t % 3 * TILE, TILE)] = (value * live).astype(BF16)
                g[block(2 * half + i), cols] = (slope * live).astype(BF16)
            z = after
        tmp[...] = mm(u[rows], wdn[0 : FF // 2]) + mm(u[pl.ds(pl.multiple_of(ROWS + half * HALF, HALF), HALF)], wdn[FF // 2 : FF])

        def result(i):
            m = 2 * half + i
            s = Sentence(scalars, m)
            value = base[block(m)] + tmp[block(i)] * s.mask * s.rows()
            lo[block(m)] = value.astype(BF16)
            finish(m, s, value)

        each(0, 2, result)

    def through_norm(half, base, g_row):
        def result(i):
            m = 2 * half + i
            s = Sentence(scalars, m)
            n, r = normalize(base[block(m)].astype(F32), s.mask, s.inv)
            dy = tmp[block(i)]
            gsum[g_row : g_row + 1] += jnp.sum(dy * n, 0, keepdims=True)
            dx[block(m)] += normalize_back(dy * gain(g_row), n, r, s.mask, s.inv)

        each(0, 2, result)

    def ffn_back(half, base, g_row):
        rows = block(half, HALF)
        for t in range(FF // TILE):
            cols = pl.ds(t * TILE, TILE)
            g[rows, cols] = (mm_nt(dbr[rows], wdn[cols]) * g[rows, cols].astype(F32)).astype(BF16)
        tmp[...] = mm_nt(g[rows], wup[...])
        through_norm(half, base, g_row)

    def branch(half, dst):
        def body(m):
            s = Sentence(scalars, m)
            dst[block(m)] = (dx[block(m)] * s.mask * s.rows()).astype(BF16)

        each(2 * half, 2, body)

    def self_back(half):
        rows = block(half, HALF)
        branch(half, dbrc)
        tmp[...] = mm_nt(dbrc[rows], wout[...])

        def attention(i):
            m = 2 * half + i
            s = Sentence(scalars, m)
            at = block(m)
            d_o[...] = (tmp[block(i)] * s.heads).astype(BF16)
            dq, dk, dv = attend_back(
                lambda h: d_o[:, slice(*window(h))],
                lambda h: qkv[at, slice(*window(h))],
                lambda h: qkv[at, D + window(h)[0] : D + window(h)[1]],
                lambda h: qkv[at, 2 * D + window(h)[0] : 2 * D + window(h)[1]],
                lambda h: p[m * HEADS + h], lanes_of)
            c[at] = dq
            qc[at] = dk
            oc[at] = dv

        each(0, 2, attention)
        tmp[...] = mm_nt(c[rows], wqkv[:, 0:D]) + mm_nt(qc[rows], wqkv[:, D : 2 * D]) + mm_nt(oc[rows], wqkv[:, 2 * D : 3 * D])
        through_norm(half, x, 0)

    def turned(k, value):
        return mm_nt(picks[k], value).astype(BF16)

    def product(dst, at, left, right):
        for start, width in ((0, 256), (256, 256), (512, 128)):
            dst[0:D, at + start : at + start + width] = mm(left, right[:, start : start + width]).astype(BF16)

    def make_picks():
        for k in range(2):
            spot = relative_order(k == 0)

            def fill(i):
                places = (lax.broadcasted_iota(jnp.int32, (SEQ, 1), 0) + i * SEQ).astype(F32)
                picks[k, block(i)] = (places == spot).astype(F32).astype(BF16)

            each(0, D // SEQ, fill)

    def ffn_weights():
        bt = turned(0, b[...])
        for t in range(4):
            for k in (2 * t, 2 * t + 1):
                wdn[k * 384 : k * 384 + 384] = mm_tn(u[block(k // 4, ROWS), pl.ds(k % 4 * 384, 384)], dbr[...]).astype(BF16)
            down.core[t].start()
        for t in range(3):
            for cols in (pl.ds(t * FF_BLOCK, TILE), pl.ds(t * FF_BLOCK + TILE, TILE)):
                wup[:, cols] = mm(bt, g[:, cols]).astype(BF16)
            up.core[t].start()

    def first_part(half):
        each(2 * half, 2, self_attention)
        pl.when(half == 0)(lambda: get_out.wait())
        tmp[...] = mm(o[block(half, HALF)], wout[...])
        each(0, 2, lambda i: add_attention(i, half))

        @pl.when(section == 0)
        def _():
            @pl.when(half == 0)
            def _():
                get_up.wait()
                get_dn.wait()

            def finish(m, s, value):
                mid[block(m)] = value
                sbuf[m, 0:SEQ] = (normalize(value, s.mask, s.inv)[0] * gain(2)).astype(BF16)
                send_new(m).start()

            ffn_forward(half, x1, 1, finish)
            pl.when(half == 0)(lambda: send_x(1).start())

    each(0, 2, first_part)

    @pl.when(section == 0)
    def _():
        put_out.start()
        make_picks()
        get_cot.wait()
        get_cross.wait()

        def widen(m):
            dx[block(m)] = dbr[block(m)].astype(F32)

        each(0, SENTENCES, widen)

    def encoder_back():
        def start(half):
            def body(m):
                s = Sentence(scalars, m)
                send_new(m).wait_recv()
                n, r = normalize(mid[block(m)], s.mask, s.inv)
                dy = ebuf[m, 0:SEQ].astype(F32)
                gsum[2:3] += jnp.sum(dy * n, 0, keepdims=True)
                d = dx[block(m)] + normalize_back(dy * gain(2), n, r, s.mask, s.inv)
                dx[block(m)] = d
                dbr[block(m)] = (d * s.mask * s.rows()).astype(BF16)

            each(2 * half, 2, body)

        def back(half):
            start(half)
            ffn_back(half, x1, 1)
            pl.when(half == 0)(lambda: self_back(half))

        each(0, 2, back)

    @pl.when(section == 1)
    def _():
        get_cross.wait()

        def norm(m):
            s = Sentence(scalars, m)
            c[block(m)] = (normalize(x1[block(m)], s.mask, s.inv)[0] * gain(1)).astype(BF16)

        each(0, SENTENCES, norm)
        qc[...] = mm(c[...], wcross[:, 0:D]).astype(BF16)
        make_picks()
        get_cot.wait()

        def start_back(m):
            s = Sentence(scalars, m)
            d = dbr[block(m)].astype(F32)
            dx[block(m)] = d
            dbr[block(m)] = (d * s.mask * s.rows()).astype(BF16)

        each(0, SENTENCES, start_back)
        get_up.wait()
        get_dn.wait()
        send_gain.wait_recv()
        for k in send_wc:
            k.wait_recv()
        share_wc.start()
        share_wc.wait_recv()

        def middle(half):
            rows = block(half, HALF)
            send_x(half).wait_recv()

            def old(m):
                s = Sentence(scalars, m)
                ebuf[m, SEQ : 2 * SEQ] = (normalize(xenc[block(m)].astype(F32), s.mask, s.inv)[0] * genc[2:3]).astype(BF16)

            each(2 * half, 2, old)

            def both_kv(m):
                send_new(m).wait_recv()
                kv[block(m, 2 * SEQ)] = mm(ebuf[m], wc[...]).astype(BF16)

            each(2 * half, 2, both_kv)

            def cross_forward(m):
                s = Sentence(scalars, m)

                def keep_p(h, value):
                    pc[m * HEADS + h] = value

                blended = attend(
                    lambda h: qc[block(m), slice(*window(h))],
                    lambda h: kv[block(m, 2 * SEQ), slice(*window(h))],
                    lambda h: kv[block(m, 2 * SEQ), D + window(h)[0] : D + window(h)[1]],
                    s.cross_bias(), keep_p, lanes_of)
                oc[block(m)] = (blended * s.heads).astype(BF16)

            each(2 * half, 2, cross_forward)
            tmp[...] = mm(oc[rows], wcross[:, D : 2 * D])

            def add_cross(i):
                m = 2 * half + i
                s = Sentence(scalars, m)
                mid[block(m)] = x1[block(m)] + tmp[block(i)] * s.mask * s.rows()

            each(0, 2, add_cross)
            ffn_forward(half, mid, 2, lambda m, s, value: None)
            ffn_back(half, mid, 2)
            branch(half, dbrc)
            tmp[...] = mm_nt(dbrc[rows], wcross[:, D : 2 * D])

            def cross_back(i):
                m = 2 * half + i
                s = Sentence(scalars, m)
                d_o[...] = (tmp[block(i)] * s.heads).astype(BF16)
                at = block(m, 2 * SEQ)
                dq, dk, dv = attend_back(
                    lambda h: d_o[:, slice(*window(h))],
                    lambda h: qc[block(m), slice(*window(h))],
                    lambda h: kv[at, slice(*window(h))],
                    lambda h: kv[at, D + window(h)[0] : D + window(h)[1]],
                    lambda h: pc[m * HEADS + h], lanes_of)
                qc[block(m)] = dq
                kv[at, 0:D] = dk
                kv[at, D : 2 * D] = dv
                sbuf[m] = mm_nt(kv[at], wc[...]).astype(BF16)
                send_new(m).start()

            each(0, 2, cross_back)

        each(0, 2, middle)
        each(0, SENTENCES, lambda m: send_old(m).start())
        put_out.start()

    pl.when(section == 0)(encoder_back)
    ffn_weights()
    down.first()
    up.first()

    @pl.when(section == 1)
    def _():
        def first_norm(half):
            tmp[...] = mm_nt(qc[block(half, HALF)], wcross[:, 0:D])
            through_norm(half, x1, 1)

        each(0, 2, first_norm)
        product(wcross, 0, turned(0, c[...]), qc)
        product(wcross, D, turned(0, oc[...]), dbrc)
        cross.core[0].start()
        share_wc.wait_send()
        et = [turned(1, ebuf[2 * i : 2 * i + 2].reshape(ROWS, D)) for i in range(2)]
        for cols in [pl.ds(256 * k, 256) for k in range(5)]:
            wc[:, cols] = (mm(et[0], kv[0:ROWS, cols]) + mm(et[1], kv[ROWS : 2 * ROWS, cols])).astype(BF16)
        encoded.core[0].start()
        down.second()
        up.second()
        cross.first()
        encoded.first()

    each(1 - section, 1 + section, self_back)

    @pl.when(section == 0)
    def _():
        down.second()
        up.second()

    at = turned(0, a[...])
    product(kv, 0, at, c)
    product(kv, D, at, qc)
    late_x.core[0].start()
    product(u, 0, turned(1, o[...]), dbrc)
    product(u, D, turned(1, a[...]), oc)
    decoder(cross.second, encoded.second)
    late_x.first()

    @pl.when(section == 0)
    def _():
        def old(m):
            s = Sentence(scalars, m)
            send_old(m).wait_recv()
            n, r = normalize(x[block(m)].astype(F32), s.mask, s.inv)
            dy = ebuf[m, SEQ : 2 * SEQ].astype(F32)
            gsum[2:3] += jnp.sum(dy * n, 0, keepdims=True)
            dx[block(m)] += normalize_back(dy * gain(2), n, r, s.mask, s.inv)

        each(0, SENTENCES, old)

    gpad[...] = jnp.zeros_like(gpad)
    gpad[0:3] = gsum[0:3]
    counts = [jnp.int32(0)] * 4
    for m in range(SENTENCES):
        s = Sentence(scalars, m)
        for i, uses in enumerate((True, s.full_heads, s.units > FF_BLOCK, s.units > 2 * FF_BLOCK)):
            counts[i] = counts[i] + jnp.where(uses, s.own, 0)
    lane = lax.broadcasted_iota(jnp.int32, (1, GAIN_COLS), 1)
    digits = jnp.zeros((1, GAIN_COLS), F32)
    for i in range(4):
        for k in range(DIGITS):
            digits = jnp.where(lane == 3 + i * DIGITS + k, (counts[i] // 4**k % 4).astype(F32), digits)
    u[0:D, 2 * D : REST] = (turned(1, gpad[...].astype(BF16)).astype(F32) + digits).astype(BF16)
    late_z.core[0].start()
    down.third()
    up.third()
    late_z.first()
    late_x.second()
    decoder(cross.third, encoded.third)
    late_z.second()

    def finish(m):
        b[block(m)] = dx[block(m)].astype(BF16)

    each(0, SENTENCES, finish)
    put_stream.start()
    down.fourth()
    up.fourth()
    late_x.third()
    late_z.third()
    decoder(cross.fourth, encoded.fourth)
    late_x.fourth()
    late_z.fourth()
    down.fifth()
    up.fifth()

    @pl.when(section == 1)
    def _():
        encoded.fifth()
        wc_send[0, 0:10] = wc_out[...]
        send_cross.start()
        cross.fifth()

    late_x.fifth()
    late_z.fifth()

    @pl.when(section == 0)
    def _():
        send_cross.wait_recv()
        cross_out[...] = wc_send[1, 0:10]
        send_gain.wait_send()
        for k in (send_x(0), send_x(1), *send_wc):
            k.wait_send()
        each(0, SENTENCES, lambda m: send_new(m).wait_send())

    @pl.when(section == 1)
    def _():
        cross.drain()
        encoded.drain()
        send_cross.wait_send()
        each(0, SENTENCES, lambda m: send_new(m).wait_send())
        each(0, SENTENCES, lambda m: send_old(m).wait_send())

    for group in (up, down, late_x, late_z):
        group.drain()
    put_out.wait()
    put_stream.wait()


def model(lengths, pieces, configs, x, cot, gains, w_qkv, w_out, w_up, w_down, w_cross):
    V, S = pltpu.VMEM, pltpu.SemaphoreType.DMA
    rows16, rows32 = V((ROWS, D), BF16), V((ROWS, D), F32)

    def row_bufs(n):
        return [V((320, n), BF16), V((80, n), BF16), V((2, 80, n), BF16), V((3, 16, n), BF16), V((3, 16, -(-n // 512) * 128), BF16), V((16, n), BF16)]

    scratch = [
        rows16, rows16, V((8, D), F32), V((8, D), F32), V((D, 3 * D), BF16), V((D, D), BF16), V((D, FF), BF16), V((4, 2, 4, 2, 48, D), BF16),
        V((D, 2 * D), BF16), V((D, 2 * D), BF16), V((2, D, D), BF16), rows16, V((ROWS, 3 * D), BF16), rows16, V((SENTENCES * HEADS, SEQ, SEQ), BF16),
        rows32, rows16, rows16, V((SENTENCES, 2 * SEQ, D), BF16), V((SENTENCES, 2 * SEQ, D), BF16), V((2 * ROWS, 2 * D), BF16), rows16,
        V((SENTENCES * HEADS, 2 * SEQ, SEQ), BF16), rows32, rows16, V((2 * ROWS, FF // 2), BF16), V((ROWS, FF), BF16), rows16, rows16,
        rows32, V((HALF, D), F32), V((SEQ, D), BF16), V((8, D), F32), V((GAIN_COLS, D), F32), V((HEADS, 256), F32),
        V((10, 2 * D), F32), V((2, 16, 2 * D), F32),
        row_bufs(FF), [V((4, 2, 4, 48, D), BF16), V((4, 2, 48, D), BF16), V((2, 4, 2, 48, D), BF16), V((3, 2, 48, D), BF16), V((48, D), BF16)],
        row_bufs(2 * D), row_bufs(2 * D), row_bufs(2 * D), row_bufs(REST),
        S((7,)), S((2,)), S((COPIES,)), S((COPIES,))]
    f32 = functools.partial(shape, dtype=F32)
    return pl.pallas_call(
        model_kernel,
        name="model",
        out_shape=(shape(ROWS, D), shape(ROWS, D), f32(10, FF), f32(48, D), f32(10, 2 * D), f32(10, REST), f32(10, 2 * D)),
        in_specs=[IN_SMEM] * 3 + [IN_HBM] * 2 + [IN_VMEM] + [IN_HBM] * 5,
        out_specs=[IN_HBM] * 2 + [IN_VMEM] * 5,
        scratch_shapes=scratch,
        compiler_params=pltpu.CompilerParams(collective_id=0, has_side_effects=True, vmem_limit_bytes=VMEM_LIMIT),
    )(lengths, pieces, configs, x, cot, gains, w_qkv, w_out, w_up, w_down.reshape(4, 2, 4, 2, 48, D), w_cross)


COPIES = 14 + 16 + 14 + 4 * 14 + 1


def finish_kernel(out_hbm, stream_hbm, up, down, qkv_x, rest, cross, out_new, stream_new, gain_new, qkv_new, wout_new, up_new, down_new, cross_new, held, sem):
    ins = [pltpu.make_async_copy(src, held.at[i], sem.at[i]) for i, src in enumerate((out_hbm, stream_hbm))]
    outs = [pltpu.make_async_copy(held.at[i], dst, sem.at[2 + i]) for i, dst in enumerate((out_new, stream_new))]
    for k in ins:
        k.start()
    devices = lax.axis_size("dp")
    me = lax.axis_index("dp")
    lane = lax.broadcasted_iota(jnp.int32, (1, GAIN_COLS), 1)
    digits = rest[0:1, 2 * D : REST]
    tokens_all = float(ROWS * devices)
    rates = []
    for i in range(4):
        total = jnp.zeros((1, 1), F32)
        for k in range(DIGITS):
            total = total + jnp.sum(jnp.where(lane == 3 + i * DIGITS + k, digits, 0.0), 1, keepdims=True) * float(4**k)
        rates.append(tokens_all / (total + tokens_all / 8))
    for k, move in zip(ins, outs):
        k.wait()
        move.start()
    halves = jnp.where(lax.broadcasted_iota(jnp.int32, (1, D), 1) >= D // 2, rates[1], rates[0])
    for r in range(10):
        row = pl.ds(r, 1)
        cross_new[r] = cross[row]
        qkv_new[r, :, 0:D] = qkv_x[row, 0:D] * halves
        qkv_new[r, :, D : 2 * D] = qkv_x[row, D : 2 * D] * halves
        qkv_new[r, :, 2 * D : 3 * D] = rest[row, D : 2 * D] * halves
        wout_new[r] = rest[row, 0:D] * jnp.where(me * 10 + r >= D // 2, rates[1], rates[0])
        for t, rate in enumerate((rates[0], rates[2], rates[3])):
            cols = slice(t * FF_BLOCK, (t + 1) * FF_BLOCK)
            up_new[r, :, cols] = up[row, cols] * rate
    unit = lax.broadcasted_iota(jnp.int32, (48, 1), 0) + me * 48
    down_new[...] = down[...] * jnp.where(unit < FF_BLOCK, rates[0], jnp.where(unit < 2 * FF_BLOCK, rates[2], rates[3]))
    gains = jnp.concatenate([rest[:, 2 * D : REST], jnp.zeros((GAIN_COLS - 10, GAIN_COLS), F32)], axis=0).T
    for r in range(3):
        gain_new[r] = gains[r : r + 1, 0:10]
    for k in outs:
        k.wait()


def finish(*results):
    f32 = functools.partial(shape, dtype=F32)
    return pl.pallas_call(
        finish_kernel,
        name="finish",
        out_shape=(shape(ROWS, D), shape(ROWS, D), f32(3, 1, 10), f32(10, 1, 3 * D), f32(10, 1, D), f32(10, 1, FF), f32(48, D), f32(10, 1, 2 * D)),
        in_specs=[IN_HBM] * 2 + [IN_VMEM] * 5,
        out_specs=[IN_HBM] * 2 + [IN_VMEM] * 6,
        scratch_shapes=[pltpu.VMEM((2, ROWS, D), BF16), pltpu.SemaphoreType.DMA((4,))],
        compiler_params=pltpu.CompilerParams(vmem_limit_bytes=VMEM_LIMIT),
    )(*results)


def shards(stream, cotangent, lengths, pieces, configs, gains, attn_qkv, attn_out, ffn_up, ffn_down, cross_proj):
    results = model(
        lengths.transpose(0, 2, 1), pieces.T, configs, stream.reshape(ROWS, D), cotangent.reshape(ROWS, D), gains[0], attn_qkv[0], attn_out[0], ffn_up[0], ffn_down[0],
        cross_proj[0])
    layer_out, stream_grad, gain, qkv, wout, up, down, cross = finish(*results)
    rows = lambda v: v.transpose(1, 0, 2)
    return (layer_out.reshape(stream.shape), stream_grad.reshape(stream.shape), rows(gain), rows(qkv), rows(wout), rows(up), down[None], rows(cross))


def solution(mesh):
    in_specs = (
        P("section", None, "dp", None, None),
        P("section", None, "dp", None, None),
        P(None, None, "dp"),
        P(None, "dp"),
        P(),
        P("section", None, None),
        P("section", None, None),
        P("section", None, None),
        P("section", None, None),
        P("section", None, None),
        P("section", None, None),
    )
    out_specs = (
        P("section", None, "dp", None, None),
        P("section", None, "dp", None, None),
        P("section", None, "dp"),
        P("section", "dp", None),
        P("section", "dp", None),
        P("section", "dp", None),
        P("section", "dp", None),
        P("section", "dp", None),
    )
    return jax.shard_map(shards, mesh=mesh, in_specs=in_specs, out_specs=out_specs, check_vma=False)
```

```python
import functools

import jax
import jax.numpy as jnp
from jax import lax
from jax.experimental import pallas as pl
from jax.experimental.pallas import tpu as pltpu
from jax.sharding import PartitionSpec as P

F32, BF16 = jnp.float32, jnp.bfloat16
D, HEADS, HEAD_DIM, FF, FF_BLOCK = 640, 8, 80, 3072, 1024
SEQ, SENTENCES = 128, 4
ROWS = SEQ * SENTENCES
HALF = ROWS // 2
TILE = 512
EPSILON = 1e-05
NEGATIVE = -1e30
SCALE = HEAD_DIM ** (-0.5)
LOG2E = 1.4426950408889634
MESH = pl.DeviceIdType.MESH
VMEM_LIMIT = 63 * 1024 * 1024
NX, NY, NZ, CORES = 4, 2, 4, 2


def place():
    me = lax.axis_index("dp")
    core = me % CORES
    z = me // CORES % NZ
    y = me // (CORES * NZ) % NY
    x = me // (CORES * NZ * NY)
    return x, y, z, core


def device_at(x, y, z, core):
    return {"dp": ((x * NY + y) * NZ + z) * CORES + core}


def relative_order(x_first):
    x, y, z, core = (v.astype(F32) for v in place())
    f = lax.broadcasted_iota(jnp.int32, (1, D), 1).astype(F32)
    digit = lambda size, count: (jnp.floor((f + 0.5) / size) - count * jnp.floor((f + 0.5) / (size * count)))
    away = lambda value, count: jnp.where(value < 0, value + count, value)
    rc, rx, rz, ry = away(digit(10, 2) - core, 2), away(digit(160, 4) - x, 4), away(digit(20, 4) - z, 4), away(digit(80, 2) - y, 2)
    first, second = (rx, rz) if x_first else (rz, rx)
    return rc * 320 + first * 80 + second * 20 + ry * 10 + digit(1, 10)


def mm(a, b):
    return lax.dot_general(a, b, (((1,), (0,)), ((), ())), preferred_element_type=F32)


def mm_nt(a, b):
    return lax.dot_general(a, b, (((1,), (1,)), ((), ())), preferred_element_type=F32)


def mm_tn(a, b):
    return lax.dot_general(a, b, (((0,), (0,)), ((), ())), preferred_element_type=F32)


def block(m, size=SEQ):
    if isinstance(m, int):
        return pl.ds(m * size, size)
    return pl.ds(pl.multiple_of(m * size, size), size)


def each(lo, count, body):
    def step(i, _):
        body(lo + i)
        return 0

    lax.fori_loop(0, count, step, 0)


def normalize(v, mask, inv_width):
    centred = (v - jnp.sum(v * mask, -1, keepdims=True) * inv_width) * mask
    spread = jnp.sum(centred * centred, -1, keepdims=True) * inv_width
    inverse = lax.rsqrt(spread + EPSILON)
    return centred * inverse, inverse


def normalize_back(dn, normed, inverse, mask, inv_width):
    dn = dn * mask
    first = jnp.sum(dn, -1, keepdims=True) * inv_width
    second = jnp.sum(dn * normed, -1, keepdims=True) * inv_width
    return inverse * (dn - (first + normed * second) * mask)


def window(h):
    return HEAD_DIM * h // 128 * 128, -(-HEAD_DIM * (h + 1) // 128) * 128


class Tiles:
    def __init__(self):
        self.tile = {}

    def add(self, h, value):
        lo, hi = window(h)
        for j in range(lo // 128, hi // 128):
            part = value[:, j * 128 - lo : j * 128 - lo + 128]
            self.tile[j] = self.tile[j] + part if j in self.tile else part

    def whole(self):
        return jnp.concatenate([self.tile[j] for j in range(D // 128)], axis=1)


class Sentence:
    def __init__(self, scalars, m):
        lengths, pieces, configs = scalars
        piece = pieces[0, m]
        section = lax.axis_index("section")
        self.width, self.units = configs[piece, 0], configs[piece, 2]
        self.full_heads = configs[piece, 1] == HEADS
        self.outputs = configs[piece, 3]
        self.source = lengths[0, 0, m]
        self.own = lengths[section, 0, m]
        self.causal = section
        lanes = lax.broadcasted_iota(jnp.int32, (1, D), 1)
        self.mask = (lanes < self.width).astype(F32)
        self.heads = (lanes < configs[piece, 1] * HEAD_DIM).astype(F32)
        self.inv = 1.0 / self.width.astype(F32)

    def rows(self):
        return (lax.broadcasted_iota(jnp.int32, (SEQ, 1), 0) < self.own).astype(F32)

    def self_bias(self):
        k = lax.broadcasted_iota(jnp.int32, (SEQ, SEQ), 0)
        q = lax.broadcasted_iota(jnp.int32, (SEQ, SEQ), 1)
        allowed = (k < self.own) & (k <= q + (1 - self.causal) * SEQ)
        return jnp.where(allowed, 0.0, NEGATIVE)

    def cross_bias(self):
        k = lax.broadcasted_iota(jnp.int32, (2 * SEQ, 1), 0)
        allowed = (jnp.where(k < SEQ, k, k - SEQ) < self.source) & (k < self.outputs * SEQ)
        return jnp.where(allowed, 0.0, NEGATIVE)


def softmax_columns(scores, bias):
    scores = scores + bias
    exponent = jnp.exp2((scores - jnp.max(scores, 0, keepdims=True)) * (SCALE * LOG2E))
    return (exponent * (1.0 / jnp.sum(exponent, 0, keepdims=True))).astype(BF16)


def attend(query, keys, values, bias, keep, lanes):
    scores = [mm_nt(keys(h), query(h) * lanes(h)) for h in range(HEADS)]
    weights = [softmax_columns(s, bias) for s in scores]
    out = Tiles()
    for h in range(HEADS):
        keep(h, weights[h])
        out.add(h, mm_tn(weights[h], values(h) * lanes(h)))
    return out.whole()


def attend_back(d_out, query, keys, values, weights, lanes):
    d_weights = [mm_nt(values(h), d_out(h) * lanes(h)) for h in range(HEADS)]
    d_values = Tiles()
    for h in range(HEADS):
        d_values.add(h, mm(weights(h), d_out(h) * lanes(h)))
    d_values = d_values.whole().astype(BF16)
    d_scores = []
    for h in range(HEADS):
        p = weights(h).astype(F32)
        product = p * d_weights[h]
        d_scores.append((product - p * jnp.sum(product, 0, keepdims=True)).astype(BF16))
    d_keys = Tiles()
    for h in range(HEADS):
        d_keys.add(h, mm(d_scores[h], query(h) * lanes(h)))
    d_keys = (d_keys.whole() * SCALE).astype(BF16)
    d_query = Tiles()
    for h in range(HEADS):
        d_query.add(h, mm_tn(d_scores[h], keys(h) * lanes(h)))
    return (d_query.whole() * SCALE).astype(BF16), d_keys, d_values


def gelu_pair(z):
    cdf = 0.5 + 0.5 * lax.erf(z * 0.7071067811865476)
    density = jnp.exp2(z * z * (-0.5 * LOG2E)) * 0.3989422804014327
    return z * cdf, cdf + z * density


def shape(*dims, dtype=BF16):
    return jax.ShapeDtypeStruct(dims, dtype)


IN_VMEM = pl.BlockSpec(memory_space=pltpu.VMEM)
IN_SMEM = pl.BlockSpec(memory_space=pltpu.SMEM)
IN_HBM = pl.BlockSpec(memory_space=pl.ANY)


class Copies:
    def __init__(self, send, recv):
        self.send, self.recv, self.count = send, recv, 0

    def make(self, src, dst, device):
        k = self.count
        self.count += 1
        return pltpu.make_async_remote_copy(
            src_ref=src, dst_ref=dst, send_sem=self.send.at[k], recv_sem=self.recv.at[k], device_id=device, device_id_type=MESH)


def add_rows(dst, src, count, step=16):
    def body(i):
        at = block(i, step)
        dst[at] = dst[at] + src[at]

    each(0, count // step, body)


def total_rows(*refs):
    return sum(r.astype(F32) for r in refs)


class RowGroup:
    def __init__(self, copies, ref, pieces, bufs, out, sibling, ring, plane, cut=48):
        self.out = out
        self.ref = ref = ref.at[:, pl.ds(0, out.shape[1])]
        self.got, self.a, self.b, self.r, self.tail, self.y = bufs
        self.fold = self.tail.shape[2]
        plus, minus = ring
        mk = copies.make
        self.core = [mk(ref.at[pl.ds(320, 320), cols], self.got.at[:, cols], sibling) for cols in pieces]
        rows = lambda lo, count: ref.at[pl.ds(lo, count)]
        self.cut, under = cut, 80 - cut
        top, low = pl.ds(0, cut), pl.ds(cut, under)
        self.a_p, self.a_m = mk(rows(160, cut), self.a.at[top], plus), mk(rows(160 + cut, under), self.a.at[low], minus)
        self.b_p, self.b_m = mk(rows(80 + cut, under), self.b.at[0, low], plus), mk(rows(240, cut), self.b.at[1, top], minus)
        self.c_p, self.c_m = mk(rows(80, cut), self.b.at[0, top], plus), mk(rows(240 + cut, under), self.b.at[1, low], minus)
        self.direct = [(
            mk(self.got.at[pl.ds(16 * k, 16)], self.r.at[k - 1], plane[2 * k]),
            mk(self.got.at[pl.ds(64 + 16 * k, 16), pl.ds(0, self.fold)], self.tail.at[k - 1], plane[2 * k])) for k in range(1, 4)]
        self.last = mk(self.got.at[pl.ds(128, 16)], self.y, plane[1])

    def summed(self, r, count=80):
        add_rows(self.ref.at[pl.ds(80 * r, count)], self.got.at[pl.ds(80 * r, count)], count)

    def first(self):
        for k in self.core:
            k.wait_recv()
        self.summed(2)
        self.a_p.start()
        self.a_m.start()
        self.summed(1)
        self.b_p.start()
        self.summed(3)
        self.b_m.start()
        self.summed(0)

    def second(self):
        cut, under = self.cut, 80 - self.cut
        self.a_p.wait_recv()
        add_rows(self.ref.at[pl.ds(80, cut)], self.a.at[pl.ds(0, cut)], cut)
        self.c_p.start()
        self.a_m.wait_recv()
        add_rows(self.ref.at[pl.ds(240 + cut, under)], self.a.at[pl.ds(cut, under)], under)
        self.c_m.start()

    def third(self):
        for k in (self.b_p, self.b_m, self.c_p, self.c_m):
            k.wait_recv()
        n, fold = self.out.shape[1], self.fold
        for k in (1, 2, 3, 0):
            at = pl.ds(20 * k, 20)
            got = total_rows(self.ref[at], self.b[0, at], self.b[1, at])
            rest = jnp.concatenate([got[16:20], jnp.zeros((4, 4 * fold - n), F32)], axis=1) if 4 * fold > n else got[16:20]
            self.got[16 * k : 16 * k + 16] = got[0:16].astype(BF16)
            folded = jnp.concatenate([rest[:, j * fold : (j + 1) * fold] for j in range(4)], axis=0)
            self.got[64 + 16 * k : 80 + 16 * k, 0:fold] = folded.astype(BF16)
            if k > 0:
                for copy in self.direct[k - 1]:
                    copy.start()

    def fourth(self):
        for pair in self.direct:
            for copy in pair:
                copy.wait_recv()
        n, fold = self.out.shape[1], self.fold
        main = total_rows(self.got[0:16], *(self.r[k] for k in range(3)))
        folded = total_rows(self.got[64:80, 0:fold], *(self.tail[k] for k in range(3)))
        rest = jnp.concatenate([folded[4 * j : 4 * j + 4] for j in range(4)], axis=1)[:, 0:n]
        self.got[128:144] = jnp.concatenate([main[10:16], rest, jnp.zeros((6, n), F32)], axis=0).astype(BF16)
        self.last.start()
        self.out[...] = main[0:10]

    def fifth(self):
        self.last.wait_recv()
        self.out[...] = self.out[...] + self.y[0:10].astype(F32)

    def drain(self):
        for k in (*self.core, self.a_p, self.a_m, self.b_p, self.b_m, self.c_p, self.c_m, *(c for pair in self.direct for c in pair), self.last):
            k.wait_send()


class DownGroup:
    def __init__(self, copies, ref, bufs, out, sibling, ring, plane, x, y, z, core):
        self.ref, self.out, self.x, self.y, self.z, self.core_at = ref, out, x, y, z, core
        self.got, self.a, self.b, self.r, self.y_in = bufs
        mk = copies.make
        plus, minus = ring
        self.core = [mk(ref.at[i, :, :, 1 - core], self.got.at[i], sibling) for i in range(4)]
        part = lambda lo, r: ref.at[pl.ds(lo, 2), :, (z + r) % 4, core]
        top, low = pl.ds(0, 2), pl.ds(2, 2)
        self.a_p, self.a_m = mk(part(0, 2), self.a.at[top], plus), mk(part(2, 2), self.a.at[low], minus)
        self.b_p, self.b_m = mk(part(2, 1), self.b.at[0, low], plus), mk(part(0, 3), self.b.at[1, top], minus)
        self.c_p, self.c_m = mk(part(0, 1), self.b.at[0, top], plus), mk(part(2, 3), self.b.at[1, low], minus)
        self.direct = [(mk(ref.at[(x + k) % 4, :, z, core], self.r.at[k - 1], plane[2 * k]),) for k in range(1, 4)]
        self.last = mk(ref.at[x, 1 - y, z, core], self.y_in, plane[1])

    def add(self, r, src, lo, count):
        zr = (self.z + r) % 4

        def body(i):
            p, q = lo + i // 2, i % 2
            self.ref[p, q, zr, self.core_at] = self.ref[p, q, zr, self.core_at] + src(p, q, zr)

        each(0, 2 * count, body)

    def summed(self, r):
        self.add(r, lambda p, q, zr: self.got[p, q, zr], 0, 4)

    first = RowGroup.first

    def second(self):
        self.a_p.wait_recv()
        self.add(1, lambda p, q, zr: self.a[p, q], 0, 2)
        self.c_p.start()
        self.a_m.wait_recv()
        self.add(3, lambda p, q, zr: self.a[p, q], 2, 2)
        self.c_m.start()

    def third(self):
        for k in (self.b_p, self.b_m, self.c_p, self.c_m):
            k.wait_recv()
        z, core = self.z, self.core_at
        for k in (1, 2, 3, 0):
            p = (self.x + k) % 4
            for q in range(2):
                self.ref[p, q, z, core] = total_rows(self.ref[p, q, z, core], self.b[0, p, q], self.b[1, p, q]).astype(BF16)
            if k > 0:
                self.direct[k - 1][0].start()

    def fourth(self):
        for k in self.direct:
            k[0].wait_recv()
        x, y, z, core = self.x, self.y, self.z, self.core_at
        full = lambda q: total_rows(self.ref[x, q, z, core], *(self.r[k, q] for k in range(3)))
        self.ref[x, 1 - y, z, core] = full(1 - y).astype(BF16)
        self.last.start()
        self.out[...] = full(y)

    def fifth(self):
        self.last.wait_recv()
        self.out[...] = self.out[...] + self.y_in[...].astype(F32)

    drain = RowGroup.drain


GAIN_COLS = 128
REST = 2 * D + GAIN_COLS
DIGITS = 5


def model_kernel(lengths, pieces, configs, x_hbm, cot_hbm, gain_in, wqkv_hbm, wout_hbm, wup_hbm, wdn_hbm, wcross_hbm,
                 out_hbm, dstream_hbm, up_out, down_out, qkv_out, rest_out, cross_out, *scratch):
    (x, xenc, gains, genc, wqkv, wout, wup, wdn6, wcross, wc, picks, a, qkv, o, p, x1, c, qc, ebuf, sbuf, kv, oc, pc, mid, b, u, g, dbr, dbrc,
     dx, tmp, d_o, gsum, gpad, head_rows, wc_out, wc_send, up_bufs, down_bufs, cross_bufs, wc_bufs, x2_bufs, z2_bufs,
     load_sem, out_sem, send_sem, recv_sem) = scratch
    scalars = (lengths, pieces, configs)
    wdn = wdn6.reshape(FF, D)
    lo = xenc
    section = lax.axis_index("section")
    px, py, pz, core = place()
    own = {"section": section}
    partner = {"section": 1 - section, "dp": lax.axis_index("dp")}
    beyond = {"section": 1 - section, **device_at(px, 1 - py, pz, core)}
    sibling = {**own, **device_at(px, py, pz, 1 - core)}
    z_plane = [{**own, **device_at(px, (py + k % 2) % 2, (pz + k // 2) % 4, core)} for k in range(8)]
    x_plane = [{**own, **device_at((px + k // 2) % 4, (py + k % 2) % 2, pz, core)} for k in range(8)]
    x_ring, z_ring = (x_plane[2], x_plane[6]), (z_plane[2], z_plane[6])
    barrier = pltpu.get_barrier_semaphore()
    others = [partner, beyond, sibling, z_plane[1], *z_plane[2::2], *x_plane[2::2]]
    for d in others:
        pl.semaphore_signal(barrier, inc=1, device_id=d, device_id_type=MESH)

    def load(k, src, dst):
        return pltpu.make_async_copy(src, dst, load_sem.at[k])

    get_x, get_qkv, get_out = load(0, x_hbm, x), load(1, wqkv_hbm, wqkv), load(2, wout_hbm, wout)
    get_up, get_dn, get_cross, get_cot = load(3, wup_hbm, wup), load(4, wdn_hbm, wdn6), load(5, wcross_hbm, wcross), load(6, cot_hbm, dbr)
    get_x.start()
    get_qkv.start()
    put_out = pltpu.make_async_copy(lo, out_hbm, out_sem.at[0])
    put_stream = pltpu.make_async_copy(b, dstream_hbm, out_sem.at[1])
    gains[0:3] = gain_in[...].astype(F32)
    gain = lambda i: gains[i : i + 1]
    for h in range(HEADS):
        low, high = window(h)
        lanes = lax.broadcasted_iota(jnp.int32, (1, high - low), 1) + low
        head_rows[h : h + 1, 0 : high - low] = ((lanes >= HEAD_DIM * h) & (lanes < HEAD_DIM * (h + 1))).astype(F32)

    def lanes_of(h):
        return head_rows[h : h + 1, 0 : window(h)[1] - window(h)[0]].astype(BF16)

    gsum[...] = jnp.zeros_like(gsum)

    copies = Copies(send_sem, recv_sem)
    remote = copies.make
    part = pl.ds(pl.multiple_of(core * 320, 320), 320)
    far, near = pl.ds(pl.multiple_of(core * 320, 16), 272), pl.ds(pl.multiple_of(core * 320 + 272, 16), 48)
    send_gain = remote(gains, genc, partner)
    send_wc = [remote(wcross_hbm.at[far], wc.at[far], beyond), remote(wcross_hbm.at[near], wc.at[near], partner)]
    share_wc = remote(wc.at[part], wc.at[part], sibling)
    first_new = copies.count
    first_x = first_new + 2 * SENTENCES
    copies.count += 2 * SENTENCES + 2

    def send_x(half):
        rows = block(half, HALF)
        return pltpu.make_async_remote_copy(
            src_ref=x_hbm.at[rows], dst_ref=xenc.at[rows], send_sem=send_sem.at[first_x + half], recv_sem=recv_sem.at[first_x + half],
            device_id=partner, device_id_type=MESH)

    def send_new(m):
        return pltpu.make_async_remote_copy(
            src_ref=sbuf.at[m, pl.ds(0, SEQ)], dst_ref=ebuf.at[m, pl.ds(0, SEQ)], send_sem=send_sem.at[first_new + m],
            recv_sem=recv_sem.at[first_new + m], device_id=partner, device_id_type=MESH)

    def send_old(m):
        k = first_new + SENTENCES + m
        return pltpu.make_async_remote_copy(
            src_ref=sbuf.at[m, pl.ds(SEQ, SEQ)], dst_ref=ebuf.at[m, pl.ds(SEQ, SEQ)], send_sem=send_sem.at[k],
            recv_sem=recv_sem.at[k], device_id=partner, device_id_type=MESH)

    whole = [slice(None)]
    thirds = [pl.ds(t * FF_BLOCK, FF_BLOCK) for t in range(3)]
    up = RowGroup(copies, wup, thirds, up_bufs, up_out, sibling, x_ring, z_plane)
    down = DownGroup(copies, wdn6, down_bufs, down_out, sibling, z_ring, x_plane, px, py, pz, core)
    cross = RowGroup(copies, wcross, whole, cross_bufs, cross_out, sibling, x_ring, z_plane, 32)
    encoded = RowGroup(copies, wc, whole, wc_bufs, wc_out, sibling, z_ring, x_plane, 32)
    late_x = RowGroup(copies, kv, [pl.ds(0, 2 * D)], x2_bufs, qkv_out, sibling, x_ring, z_plane, 32)
    late_z = RowGroup(copies, u, [pl.ds(0, REST)], z2_bufs, rest_out, sibling, z_ring, x_plane)
    send_cross = remote(wc_send.at[0], wc_send.at[1], partner)

    def decoder(*steps):
        @pl.when(section == 1)
        def _():
            for step in steps:
                step()

    get_x.wait()

    def norm_x(m):
        s = Sentence(scalars, m)
        a[block(m)] = (normalize(x[block(m)].astype(F32), s.mask, s.inv)[0] * gain(0)).astype(BF16)

    each(0, SENTENCES, norm_x)
    pl.semaphore_wait(barrier, len(others))

    @pl.when(section == 0)
    def _():
        send_gain.start()
        send_x(0).start()
        for k in send_wc:
            k.start()

    get_qkv.wait()
    for k in (get_out, get_up, get_dn, get_cross, get_cot):
        k.start()

    def project(j):
        qkv[:, block(j, D)] = mm(a[...], wqkv[:, block(j, D)]).astype(BF16)

    each(0, 3, project)

    def self_attention(m):
        s = Sentence(scalars, m)
        rows = block(m)

        def keep_p(h, value):
            p[m * HEADS + h] = value

        blended = attend(
            lambda h: qkv[rows, slice(*window(h))],
            lambda h: qkv[rows, D + window(h)[0] : D + window(h)[1]],
            lambda h: qkv[rows, 2 * D + window(h)[0] : 2 * D + window(h)[1]],
            s.self_bias(), keep_p, lanes_of)
        o[rows] = (blended * s.heads).astype(BF16)

    def add_attention(i, half):
        m = 2 * half + i
        s = Sentence(scalars, m)
        rows = block(m)
        x1[rows] = x[rows].astype(F32) + tmp[block(i)] * s.mask * s.rows()

    def ffn_forward(half, base, g_row, finish):
        rows = block(half, HALF)

        def norm(m):
            s = Sentence(scalars, m)
            b[block(m)] = (normalize(base[block(m)], s.mask, s.inv)[0] * gain(g_row)).astype(BF16)

        each(2 * half, 2, norm)
        units = [Sentence(scalars, 2 * half + i).units for i in range(2)]
        z = mm(b[rows], wup[:, 0:TILE])
        for t in range(FF // TILE):
            after = mm(b[rows], wup[:, (t + 1) * TILE : (t + 2) * TILE]) if t + 1 < FF // TILE else None
            cols = pl.ds(t * TILE, TILE)
            for i in range(2):
                live = (t * TILE < units[i]).astype(F32)
                value, slope = gelu_pair(z[i * SEQ : (i + 1) * SEQ])
                u[pl.ds(pl.multiple_of(t // 3 * ROWS + (2 * half + i) * SEQ, SEQ), SEQ), pl.ds(t % 3 * TILE, TILE)] = (value * live).astype(BF16)
                g[block(2 * half + i), cols] = (slope * live).astype(BF16)
            z = after
        tmp[...] = mm(u[rows], wdn[0 : FF // 2]) + mm(u[pl.ds(pl.multiple_of(ROWS + half * HALF, HALF), HALF)], wdn[FF // 2 : FF])

        def result(i):
            m = 2 * half + i
            s = Sentence(scalars, m)
            value = base[block(m)] + tmp[block(i)] * s.mask * s.rows()
            lo[block(m)] = value.astype(BF16)
            finish(m, s, value)

        each(0, 2, result)

    def through_norm(half, base, g_row):
        def result(i):
            m = 2 * half + i
            s = Sentence(scalars, m)
            n, r = normalize(base[block(m)].astype(F32), s.mask, s.inv)
            dy = tmp[block(i)]
            gsum[g_row : g_row + 1] += jnp.sum(dy * n, 0, keepdims=True)
            dx[block(m)] += normalize_back(dy * gain(g_row), n, r, s.mask, s.inv)

        each(0, 2, result)

    def ffn_back(half, base, g_row):
        rows = block(half, HALF)
        for t in range(FF // TILE):
            cols = pl.ds(t * TILE, TILE)
            g[rows, cols] = (mm_nt(dbr[rows], wdn[cols]) * g[rows, cols].astype(F32)).astype(BF16)
        tmp[...] = mm_nt(g[rows], wup[...])
        through_norm(half, base, g_row)

    def branch(half, dst):
        def body(m):
            s = Sentence(scalars, m)
            dst[block(m)] = (dx[block(m)] * s.mask * s.rows()).astype(BF16)

        each(2 * half, 2, body)

    def self_back(half):
        rows = block(half, HALF)
        branch(half, dbrc)
        tmp[...] = mm_nt(dbrc[rows], wout[...])

        def attention(i):
            m = 2 * half + i
            s = Sentence(scalars, m)
            at = block(m)
            d_o[...] = (tmp[block(i)] * s.heads).astype(BF16)
            dq, dk, dv = attend_back(
                lambda h: d_o[:, slice(*window(h))],
                lambda h: qkv[at, slice(*window(h))],
                lambda h: qkv[at, D + window(h)[0] : D + window(h)[1]],
                lambda h: qkv[at, 2 * D + window(h)[0] : 2 * D + window(h)[1]],
                lambda h: p[m * HEADS + h], lanes_of)
            c[at] = dq
            qc[at] = dk
            oc[at] = dv

        each(0, 2, attention)
        tmp[...] = mm_nt(c[rows], wqkv[:, 0:D]) + mm_nt(qc[rows], wqkv[:, D : 2 * D]) + mm_nt(oc[rows], wqkv[:, 2 * D : 3 * D])
        through_norm(half, x, 0)

    def turned(k, value):
        return mm_nt(picks[k], value).astype(BF16)

    def product(dst, at, left, right):
        for start, width in ((0, 256), (256, 256), (512, 128)):
            dst[0:D, at + start : at + start + width] = mm(left, right[:, start : start + width]).astype(BF16)

    def make_picks():
        for k in range(2):
            spot = relative_order(k == 0)

            def fill(i):
                places = (lax.broadcasted_iota(jnp.int32, (SEQ, 1), 0) + i * SEQ).astype(F32)
                picks[k, block(i)] = (places == spot).astype(F32).astype(BF16)

            each(0, D // SEQ, fill)

    def ffn_weights():
        bt = turned(0, b[...])
        for t in range(4):
            for k in (2 * t, 2 * t + 1):
                wdn[k * 384 : k * 384 + 384] = mm_tn(u[block(k // 4, ROWS), pl.ds(k % 4 * 384, 384)], dbr[...]).astype(BF16)
            down.core[t].start()
        for t in range(3):
            for cols in (pl.ds(t * FF_BLOCK, TILE), pl.ds(t * FF_BLOCK + TILE, TILE)):
                wup[:, cols] = mm(bt, g[:, cols]).astype(BF16)
            up.core[t].start()

    def first_part(half):
        each(2 * half, 2, self_attention)
        pl.when(half == 0)(lambda: get_out.wait())
        tmp[...] = mm(o[block(half, HALF)], wout[...])
        each(0, 2, lambda i: add_attention(i, half))

        @pl.when(section == 0)
        def _():
            @pl.when(half == 0)
            def _():
                get_up.wait()
                get_dn.wait()

            def finish(m, s, value):
                mid[block(m)] = value
                sbuf[m, 0:SEQ] = (normalize(value, s.mask, s.inv)[0] * gain(2)).astype(BF16)
                send_new(m).start()

            ffn_forward(half, x1, 1, finish)
            pl.when(half == 0)(lambda: send_x(1).start())

    each(0, 2, first_part)

    @pl.when(section == 0)
    def _():
        put_out.start()
        make_picks()
        get_cot.wait()
        get_cross.wait()

        def widen(m):
            dx[block(m)] = dbr[block(m)].astype(F32)

        each(0, SENTENCES, widen)

    def encoder_back():
        def start(half):
            def body(m):
                s = Sentence(scalars, m)
                send_new(m).wait_recv()
                n, r = normalize(mid[block(m)], s.mask, s.inv)
                dy = ebuf[m, 0:SEQ].astype(F32)
                gsum[2:3] += jnp.sum(dy * n, 0, keepdims=True)
                d = dx[block(m)] + normalize_back(dy * gain(2), n, r, s.mask, s.inv)
                dx[block(m)] = d
                dbr[block(m)] = (d * s.mask * s.rows()).astype(BF16)

            each(2 * half, 2, body)

        def back(half):
            start(half)
            ffn_back(half, x1, 1)
            pl.when(half == 0)(lambda: self_back(half))

        each(0, 2, back)

    @pl.when(section == 1)
    def _():
        get_cross.wait()

        def norm(m):
            s = Sentence(scalars, m)
            c[block(m)] = (normalize(x1[block(m)], s.mask, s.inv)[0] * gain(1)).astype(BF16)

        each(0, SENTENCES, norm)
        qc[...] = mm(c[...], wcross[:, 0:D]).astype(BF16)
        make_picks()
        get_cot.wait()

        def start_back(m):
            s = Sentence(scalars, m)
            d = dbr[block(m)].astype(F32)
            dx[block(m)] = d
            dbr[block(m)] = (d * s.mask * s.rows()).astype(BF16)

        each(0, SENTENCES, start_back)
        get_up.wait()
        get_dn.wait()
        send_gain.wait_recv()
        for k in send_wc:
            k.wait_recv()
        share_wc.start()
        share_wc.wait_recv()

        def middle(half):
            rows = block(half, HALF)
            send_x(half).wait_recv()

            def old(m):
                s = Sentence(scalars, m)
                ebuf[m, SEQ : 2 * SEQ] = (normalize(xenc[block(m)].astype(F32), s.mask, s.inv)[0] * genc[2:3]).astype(BF16)

            each(2 * half, 2, old)

            def both_kv(m):
                send_new(m).wait_recv()
                kv[block(m, 2 * SEQ)] = mm(ebuf[m], wc[...]).astype(BF16)

            each(2 * half, 2, both_kv)

            def cross_forward(m):
                s = Sentence(scalars, m)

                def keep_p(h, value):
                    pc[m * HEADS + h] = value

                blended = attend(
                    lambda h: qc[block(m), slice(*window(h))],
                    lambda h: kv[block(m, 2 * SEQ), slice(*window(h))],
                    lambda h: kv[block(m, 2 * SEQ), D + window(h)[0] : D + window(h)[1]],
                    s.cross_bias(), keep_p, lanes_of)
                oc[block(m)] = (blended * s.heads).astype(BF16)

            each(2 * half, 2, cross_forward)
            tmp[...] = mm(oc[rows], wcross[:, D : 2 * D])

            def add_cross(i):
                m = 2 * half + i
                s = Sentence(scalars, m)
                mid[block(m)] = x1[block(m)] + tmp[block(i)] * s.mask * s.rows()

            each(0, 2, add_cross)
            ffn_forward(half, mid, 2, lambda m, s, value: None)
            ffn_back(half, mid, 2)
            branch(half, dbrc)
            tmp[...] = mm_nt(dbrc[rows], wcross[:, D : 2 * D])

            def cross_back(i):
                m = 2 * half + i
                s = Sentence(scalars, m)
                d_o[...] = (tmp[block(i)] * s.heads).astype(BF16)
                at = block(m, 2 * SEQ)
                dq, dk, dv = attend_back(
                    lambda h: d_o[:, slice(*window(h))],
                    lambda h: qc[block(m), slice(*window(h))],
                    lambda h: kv[at, slice(*window(h))],
                    lambda h: kv[at, D + window(h)[0] : D + window(h)[1]],
                    lambda h: pc[m * HEADS + h], lanes_of)
                qc[block(m)] = dq
                kv[at, 0:D] = dk
                kv[at, D : 2 * D] = dv
                sbuf[m] = mm_nt(kv[at], wc[...]).astype(BF16)
                send_new(m).start()

            each(0, 2, cross_back)

        each(0, 2, middle)
        each(0, SENTENCES, lambda m: send_old(m).start())
        put_out.start()

    pl.when(section == 0)(encoder_back)
    ffn_weights()
    down.first()
    up.first()

    @pl.when(section == 1)
    def _():
        def first_norm(half):
            tmp[...] = mm_nt(qc[block(half, HALF)], wcross[:, 0:D])
            through_norm(half, x1, 1)

        each(0, 2, first_norm)
        product(wcross, 0, turned(0, c[...]), qc)
        product(wcross, D, turned(0, oc[...]), dbrc)
        cross.core[0].start()
        share_wc.wait_send()
        et = [turned(1, ebuf[2 * i : 2 * i + 2].reshape(ROWS, D)) for i in range(2)]
        for cols in [pl.ds(256 * k, 256) for k in range(5)]:
            wc[:, cols] = (mm(et[0], kv[0:ROWS, cols]) + mm(et[1], kv[ROWS : 2 * ROWS, cols])).astype(BF16)
        encoded.core[0].start()
        down.second()
        up.second()
        cross.first()
        encoded.first()

    each(1 - section, 1 + section, self_back)

    @pl.when(section == 0)
    def _():
        down.second()
        up.second()

    at = turned(0, a[...])
    product(kv, 0, at, c)
    product(kv, D, at, qc)
    late_x.core[0].start()
    product(u, 0, turned(1, o[...]), dbrc)
    product(u, D, turned(1, a[...]), oc)
    decoder(cross.second, encoded.second)
    late_x.first()

    @pl.when(section == 0)
    def _():
        def old(m):
            s = Sentence(scalars, m)
            send_old(m).wait_recv()
            n, r = normalize(x[block(m)].astype(F32), s.mask, s.inv)
            dy = ebuf[m, SEQ : 2 * SEQ].astype(F32)
            gsum[2:3] += jnp.sum(dy * n, 0, keepdims=True)
            dx[block(m)] += normalize_back(dy * gain(2), n, r, s.mask, s.inv)

        each(0, SENTENCES, old)

    gpad[...] = jnp.zeros_like(gpad)
    gpad[0:3] = gsum[0:3]
    counts = [jnp.int32(0)] * 4
    for m in range(SENTENCES):
        s = Sentence(scalars, m)
        for i, uses in enumerate((True, s.full_heads, s.units > FF_BLOCK, s.units > 2 * FF_BLOCK)):
            counts[i] = counts[i] + jnp.where(uses, s.own, 0)
    lane = lax.broadcasted_iota(jnp.int32, (1, GAIN_COLS), 1)
    digits = jnp.zeros((1, GAIN_COLS), F32)
    for i in range(4):
        for k in range(DIGITS):
            digits = jnp.where(lane == 3 + i * DIGITS + k, (counts[i] // 4**k % 4).astype(F32), digits)
    u[0:D, 2 * D : REST] = (turned(1, gpad[...].astype(BF16)).astype(F32) + digits).astype(BF16)
    late_z.core[0].start()
    down.third()
    up.third()
    late_z.first()
    late_x.second()
    decoder(cross.third, encoded.third)
    late_z.second()

    def finish(m):
        b[block(m)] = dx[block(m)].astype(BF16)

    each(0, SENTENCES, finish)
    put_stream.start()
    down.fourth()
    up.fourth()
    decoder(encoded.fourth, cross.fourth)
    late_x.third()
    late_z.third()

    @pl.when(section == 1)
    def _():
        encoded.fifth()
        wc_send[0, 0:10] = wc_out[...]
        send_cross.start()

    late_x.fourth()
    late_z.fourth()
    down.fifth()
    up.fifth()
    decoder(cross.fifth)
    late_x.fifth()
    late_z.fifth()

    @pl.when(section == 0)
    def _():
        send_cross.wait_recv()
        cross_out[...] = wc_send[1, 0:10]
        send_gain.wait_send()
        for k in (send_x(0), send_x(1), *send_wc):
            k.wait_send()
        each(0, SENTENCES, lambda m: send_new(m).wait_send())

    @pl.when(section == 1)
    def _():
        cross.drain()
        encoded.drain()
        send_cross.wait_send()
        each(0, SENTENCES, lambda m: send_new(m).wait_send())
        each(0, SENTENCES, lambda m: send_old(m).wait_send())

    for group in (up, down, late_x, late_z):
        group.drain()
    put_out.wait()
    put_stream.wait()


def model(lengths, pieces, configs, x, cot, gains, w_qkv, w_out, w_up, w_down, w_cross):
    V, S = pltpu.VMEM, pltpu.SemaphoreType.DMA
    rows16, rows32 = V((ROWS, D), BF16), V((ROWS, D), F32)

    def row_bufs(n):
        return [V((320, n), BF16), V((80, n), BF16), V((2, 80, n), BF16), V((3, 16, n), BF16), V((3, 16, -(-n // 512) * 128), BF16), V((16, n), BF16)]

    scratch = [
        rows16, rows16, V((8, D), F32), V((8, D), F32), V((D, 3 * D), BF16), V((D, D), BF16), V((D, FF), BF16), V((4, 2, 4, 2, 48, D), BF16),
        V((D, 2 * D), BF16), V((D, 2 * D), BF16), V((2, D, D), BF16), rows16, V((ROWS, 3 * D), BF16), rows16, V((SENTENCES * HEADS, SEQ, SEQ), BF16),
        rows32, rows16, rows16, V((SENTENCES, 2 * SEQ, D), BF16), V((SENTENCES, 2 * SEQ, D), BF16), V((2 * ROWS, 2 * D), BF16), rows16,
        V((SENTENCES * HEADS, 2 * SEQ, SEQ), BF16), rows32, rows16, V((2 * ROWS, FF // 2), BF16), V((ROWS, FF), BF16), rows16, rows16,
        rows32, V((HALF, D), F32), V((SEQ, D), BF16), V((8, D), F32), V((GAIN_COLS, D), F32), V((HEADS, 256), F32),
        V((10, 2 * D), F32), V((2, 16, 2 * D), F32),
        row_bufs(FF), [V((4, 2, 4, 48, D), BF16), V((4, 2, 48, D), BF16), V((2, 4, 2, 48, D), BF16), V((3, 2, 48, D), BF16), V((48, D), BF16)],
        row_bufs(2 * D), row_bufs(2 * D), row_bufs(2 * D), row_bufs(REST),
        S((7,)), S((2,)), S((COPIES,)), S((COPIES,))]
    f32 = functools.partial(shape, dtype=F32)
    return pl.pallas_call(
        model_kernel,
        name="model",
        out_shape=(shape(ROWS, D), shape(ROWS, D), f32(10, FF), f32(48, D), f32(10, 2 * D), f32(10, REST), f32(10, 2 * D)),
        in_specs=[IN_SMEM] * 3 + [IN_HBM] * 2 + [IN_VMEM] + [IN_HBM] * 5,
        out_specs=[IN_HBM] * 2 + [IN_VMEM] * 5,
        scratch_shapes=scratch,
        compiler_params=pltpu.CompilerParams(collective_id=0, has_side_effects=True, vmem_limit_bytes=VMEM_LIMIT),
    )(lengths, pieces, configs, x, cot, gains, w_qkv, w_out, w_up, w_down.reshape(4, 2, 4, 2, 48, D), w_cross)


COPIES = 14 + 16 + 14 + 4 * 14 + 1


def finish_kernel(out_hbm, stream_hbm, up, down, qkv_x, rest, cross, out_new, stream_new, gain_new, qkv_new, wout_new, up_new, down_new, cross_new, held, sem):
    ins = [pltpu.make_async_copy(src, held.at[i], sem.at[i]) for i, src in enumerate((out_hbm, stream_hbm))]
    outs = [pltpu.make_async_copy(held.at[i], dst, sem.at[2 + i]) for i, dst in enumerate((out_new, stream_new))]
    for k in ins:
        k.start()
    devices = lax.axis_size("dp")
    me = lax.axis_index("dp")
    lane = lax.broadcasted_iota(jnp.int32, (1, GAIN_COLS), 1)
    digits = rest[0:1, 2 * D : REST]
    tokens_all = float(ROWS * devices)
    rates = []
    for i in range(4):
        total = jnp.zeros((1, 1), F32)
        for k in range(DIGITS):
            total = total + jnp.sum(jnp.where(lane == 3 + i * DIGITS + k, digits, 0.0), 1, keepdims=True) * float(4**k)
        rates.append(tokens_all / (total + tokens_all / 8))
    for k, move in zip(ins, outs):
        k.wait()
        move.start()
    halves = jnp.where(lax.broadcasted_iota(jnp.int32, (1, D), 1) >= D // 2, rates[1], rates[0])
    for r in range(10):
        row = pl.ds(r, 1)
        cross_new[r] = cross[row]
        qkv_new[r, :, 0:D] = qkv_x[row, 0:D] * halves
        qkv_new[r, :, D : 2 * D] = qkv_x[row, D : 2 * D] * halves
        qkv_new[r, :, 2 * D : 3 * D] = rest[row, D : 2 * D] * halves
        wout_new[r] = rest[row, 0:D] * jnp.where(me * 10 + r >= D // 2, rates[1], rates[0])
        for t, rate in enumerate((rates[0], rates[2], rates[3])):
            cols = slice(t * FF_BLOCK, (t + 1) * FF_BLOCK)
            up_new[r, :, cols] = up[row, cols] * rate
    unit = lax.broadcasted_iota(jnp.int32, (48, 1), 0) + me * 48
    down_new[...] = down[...] * jnp.where(unit < FF_BLOCK, rates[0], jnp.where(unit < 2 * FF_BLOCK, rates[2], rates[3]))
    gains = jnp.concatenate([rest[:, 2 * D : REST], jnp.zeros((GAIN_COLS - 10, GAIN_COLS), F32)], axis=0).T
    for r in range(3):
        gain_new[r] = gains[r : r + 1, 0:10]
    for k in outs:
        k.wait()


def finish(*results):
    f32 = functools.partial(shape, dtype=F32)
    return pl.pallas_call(
        finish_kernel,
        name="finish",
        out_shape=(shape(ROWS, D), shape(ROWS, D), f32(3, 1, 10), f32(10, 1, 3 * D), f32(10, 1, D), f32(10, 1, FF), f32(48, D), f32(10, 1, 2 * D)),
        in_specs=[IN_HBM] * 2 + [IN_VMEM] * 5,
        out_specs=[IN_HBM] * 2 + [IN_VMEM] * 6,
        scratch_shapes=[pltpu.VMEM((2, ROWS, D), BF16), pltpu.SemaphoreType.DMA((4,))],
        compiler_params=pltpu.CompilerParams(vmem_limit_bytes=VMEM_LIMIT),
    )(*results)


def shards(stream, cotangent, lengths, pieces, configs, gains, attn_qkv, attn_out, ffn_up, ffn_down, cross_proj):
    results = model(
        lengths.transpose(0, 2, 1), pieces.T, configs, stream.reshape(ROWS, D), cotangent.reshape(ROWS, D), gains[0], attn_qkv[0], attn_out[0], ffn_up[0], ffn_down[0],
        cross_proj[0])
    layer_out, stream_grad, gain, qkv, wout, up, down, cross = finish(*results)
    rows = lambda v: v.transpose(1, 0, 2)
    return (layer_out.reshape(stream.shape), stream_grad.reshape(stream.shape), rows(gain), rows(qkv), rows(wout), rows(up), down[None], rows(cross))


def solution(mesh):
    in_specs = (
        P("section", None, "dp", None, None),
        P("section", None, "dp", None, None),
        P(None, None, "dp"),
        P(None, "dp"),
        P(),
        P("section", None, None),
        P("section", None, None),
        P("section", None, None),
        P("section", None, None),
        P("section", None, None),
        P("section", None, None),
    )
    out_specs = (
        P("section", None, "dp", None, None),
        P("section", None, "dp", None, None),
        P("section", None, "dp"),
        P("section", "dp", None),
        P("section", "dp", None),
        P("section", "dp", None),
        P("section", "dp", None),
        P("section", "dp", None),
    )
    return jax.shard_map(shards, mesh=mesh, in_specs=in_specs, out_specs=out_specs, check_vma=False)
```
